128 devices in a mesh: machine: 32 (over x, z, core), local: 4 (over y).
Axes of the slice: x: 4, y: 4, z: 4, core: 2. Of those that a mesh axis runs over, the one named last changes fastest.
Arguments:
- features: bfloat16 [262144, 768], P(('machine', 'local')), may hold values from -6 to 6
- w_self: bfloat16 [768, 256], replicated, may hold values from -0.21875 to 0.21875
- w_neigh: bfloat16 [768, 256], replicated, may hold values from -0.875 to 0.875
- mirror_master_part: int32 [65536, 1], P(('machine', 'local')), may hold values from 0 to 127; in each aligned block of 512 rows (0 to 511, 512 to 1023, ...) at most 8 rows name the same one
- mirror_row: int32 [65536], P(('machine', 'local')), may hold values from 0 to 2047
- tile_count: int32 [2560], P(('machine', 'local')), may hold values from 1 to 16, as said below
- tile_column: int32 [2560, 16], P(('machine', 'local')), may hold values from 0 to 19
- tile_weight: bfloat16 [2560, 16, 128, 128], P(('machine', 'local')), may hold values from 0 to 1, as said below
- cotangent: bfloat16 [262144, 256], P(('machine', 'local')), may hold values from -0.01171875 to 0.01171875
Outputs:
- mixed: bfloat16 [262144, 256], P(('machine', 'local'))
- grad_features: bfloat16 [262144, 768], P(('machine', 'local'))
- grad_self: float32 [768, 256], replicated
- grad_neigh: float32 [768, 256], replicated
The draws below stay inside these ranges and needn't reach their ends.
Inputs may be any that keep to these rules, and one draw needn't show every extreme that they name: `mirror_master_part`: among the 512 mirrors of one partition at most 8 have their master on any one partition, and in every draw some partition reaches 8. `tile_count`: every partition has a row block with 16 tiles. `tile_weight`: edge weights are nonnegative.
All inputs are finite; a program needn't handle non-finite values.
Results may differ from the reference program's by a relative error of at most 0.0053.
Values may be sent and summed in bfloat16 or wider, within the bound.
No kernel may reach another device: no remote copies, remote signals or barrier semaphores. Data moves between devices by JAX's collectives and lax.ppermute only.
A program may use at most 192 MiB of HBM per device.

```python
import math
import jax
import jax.numpy as jnp
import numpy as np
from jax import lax

MASTER_PER_PART = 2048
MIRROR_PER_PART = 512
IN_W = 768
HID = 256
TMAX = 16
ROWB = 20
MIRROR_LIMIT = 8
NODES = 262144
TOTAL_MIRRORS = 65536
BLOCKS = 2560
DEVICES = 128


def draw_tile_count(key, part):
    key = jax.random.fold_in(key, 11)
    first, second, third = jax.random.split(key, 3)
    groups = BLOCKS // ROWB
    level = jax.random.randint(first, (groups, 1), 1 + TMAX // 4, TMAX + 1)
    counts = jax.random.randint(second, (groups, ROWB), 1, level + 1)
    full = jax.random.randint(third, (groups, 1), 0, ROWB)
    spots = jnp.arange(ROWB, dtype=jnp.int32)[None, :]
    counts = jnp.where(spots == full, TMAX, counts)
    return counts.reshape(BLOCKS).astype(jnp.int32)


def draw_tile_weight(key, part):
    key = jax.random.fold_in(key, 23)
    first, second, third = jax.random.split(key, 3)
    shape = (BLOCKS, TMAX, 128, 128)
    base = jax.random.uniform(first, shape, jnp.float32, 0.0, 1.0)
    lowest = math.log(0.1)
    row_scale = jnp.exp(jax.random.uniform(second, (BLOCKS, 1, 128, 1), jnp.float32, lowest, 0.0))
    column_scale = jnp.exp(jax.random.uniform(third, (BLOCKS, TMAX, 1, 128), jnp.float32, math.log(0.2), 0.0))
    return (base * row_scale * column_scale).astype(jnp.bfloat16)


def with_ends(drawn, rng, least, high):
    index_at = [jax.random.randint(jax.random.fold_in(rng, axis), (), 0, length) for axis, length in enumerate(drawn.shape)]
    main_axis = drawn.shape.index(max(drawn.shape))
    beside = index_at[:main_axis] + [(index_at[main_axis] + 1) % drawn.shape[main_axis]] + index_at[main_axis + 1:]
    return drawn.at[tuple(index_at)].set(least).at[tuple(beside)].set(high)


def steps_of(stream_key, dims, cuts, least, top_value):
    level = 1.0
    for axis_at, shards_of in cuts:
        heights = jax.random.uniform(jax.random.fold_in(jax.random.fold_in(stream_key, 6), axis_at), (shards_of,), jnp.float32, least / len(cuts), top_value / len(cuts))
        level = level * jnp.repeat(jnp.exp(heights), dims[axis_at] // shards_of).reshape((-1,) + (1,) * (len(dims) - 1 - axis_at))
    return level


def cumulative_ranks(count, skew):
    portions = [(1 << 20) // math.isqrt(grade ** skew) + 1 for grade in range(1, count + 1)]
    width = 1 + sum(portions) // (1 << 30)
    return np.cumsum(np.array([max(1, weight // width) for weight in portions]))


def skewed_ids(own_key, dims, amount, slope):
    listing = cumulative_ranks(amount, slope)
    ticket = jax.random.randint(jax.random.fold_in(own_key, 1), dims, 0, int(listing[amount - 1]))
    rank = jnp.searchsorted(jnp.asarray(listing, jnp.int32), ticket, side="right")
    return jax.random.permutation(jax.random.fold_in(own_key, 2), amount)[rank].astype(jnp.int32)


def shared_out(key, own, number, rows, number_of, top, bound, slope):
    order = jax.random.permutation(key, number_of)
    crowded, usual = load_shares(number_of, rows * top, bound, slope, True), load_shares(number_of, rows * top, bound, slope, False)
    places = jnp.arange(number_of)

    def named(lengths, turn):
        used = int((lengths > 0).sum())
        fixed = max(1, used // 4)
        moved = fixed + (places - fixed + turn * (used - fixed)) % max(1, number_of - fixed)
        return jnp.zeros((number_of,), jnp.int32).at[order[jnp.where(places < fixed, places, moved)]].set(jnp.asarray(lengths, jnp.int32))

    lengths = jnp.where(number % 4 == 0, named(crowded, number // 4), named(usual, number - number // 4 - 1))
    mixed = jax.random.permutation(jax.random.fold_in(own, 3), number_of)
    donor, taker = mixed[0:number_of // 2 * 2:2], mixed[1:number_of // 2 * 2:2]
    margin = jnp.minimum(lengths[donor] - 1, bound - lengths[taker]) // 2
    margin = jnp.where((donor == order[0]) | (taker == order[0]) | (lengths[taker] == 0), 0, jnp.maximum(margin, 0))
    moved = jax.random.randint(jax.random.fold_in(own, 4), (number_of // 2,), 0, 1 << 20) % (margin + 1)
    lengths = lengths.at[donor].add(-moved).at[taker].add(moved)
    members = jnp.searchsorted(jnp.cumsum(lengths), jnp.arange(rows * top), side="right").astype(jnp.int32)
    table = members.reshape(top, rows).T
    table = table[jax.random.permutation(jax.random.fold_in(own, 1), rows)]
    turn = jax.random.randint(jax.random.fold_in(own, 2), (rows, 1), 0, top)
    return jnp.take_along_axis(table, (jnp.arange(top)[None, :] + turn) % top, axis=1)


def load_shares(count, total, limit, skew, full):
    weights = [(1 << 20) // math.isqrt(standing ** skew) + 1 for standing in range(1, count + 1)]
    largest = limit if full else min(limit, max(-(-total // count), total * weights[0] // sum(weights)))
    least = 1 if total - largest >= count - 1 else 0
    given, surplus = [largest] + [least] * (count - 1), total - largest - least * (count - 1)
    while surplus > 0:
        free = [i for i in range(1, count) if given[i] < largest] or [i for i in range(1, count) if given[i] < limit]
        pool, remaining = sum([weights[i] for i in free]), surplus
        for i in free:
            more = min(limit - given[i], max(1, remaining * weights[i] // pool), surplus)
            given[i] = given[i] + more
            surplus = surplus - more
    return np.array(given)


def gaussian(stream_key, dims, scale, bound, pieces=(), kind=jnp.bfloat16):
    values = jax.random.normal(stream_key, dims, jnp.float32) * scale
    if len(pieces) > 0:
        values = steps_of(stream_key, dims, pieces, -0.22, 0.18) * values
    return jnp.clip(values, min=-bound, max=bound).astype(kind)


def setup_inputs(seed: int = 0) -> dict:
    splits = jax.random.split(jax.random.key(seed), 10)
    features = gaussian(splits[0], (NODES, IN_W), 1.0, 6.0, ((0, 128),))
    w_self = gaussian(splits[1], (IN_W, HID), IN_W ** -0.5, 0.21875)
    w_neigh = gaussian(splits[2], (IN_W, HID), (IN_W // 16) ** -0.5, 0.875)
    mirror_master_part_keys = jax.random.split(jax.random.fold_in(splits[3], 1), TOTAL_MIRRORS // MIRROR_PER_PART)
    mirror_master_part_turns = jax.random.permutation(jax.random.fold_in(splits[3], 3), TOTAL_MIRRORS // MIRROR_PER_PART)
    mirror_master_part = jax.vmap(lambda own, number: shared_out(jax.random.fold_in(splits[3], 2), own, number, MIRROR_PER_PART, DEVICES, 1, MIRROR_LIMIT, 2))(mirror_master_part_keys, mirror_master_part_turns).reshape((TOTAL_MIRRORS, 1))
    mirror_row = with_ends(skewed_ids(splits[4], (TOTAL_MIRRORS,), MASTER_PER_PART, 2), jax.random.fold_in(splits[4], 3), 0, MASTER_PER_PART - 1).astype(jnp.int32)
    tile_count = draw_tile_count(jax.random.fold_in(splits[9], 71), 0)
    tile_column = with_ends(jax.random.randint(splits[6], (BLOCKS, TMAX), 0, ROWB), jax.random.fold_in(splits[6], 1), 0, ROWB - 1).astype(jnp.int32)
    tile_weight = draw_tile_weight(jax.random.fold_in(splits[9], 71), 0)
    cotangent = gaussian(splits[8], (NODES, HID), (NODES ** -0.5), 0.01171875, ((0, 128),))
    return dict(features=features, w_self=w_self, w_neigh=w_neigh, mirror_master_part=mirror_master_part, mirror_row=mirror_row, tile_count=tile_count, tile_column=tile_column, tile_weight=tile_weight, cotangent=cotangent)


def activate(value):
    return jax.nn.gelu(value, approximate=True)

def reference(features, w_self, w_neigh, mirror_master_part, mirror_row, tile_count, tile_column, tile_weight, cotangent):
    partition_list = NODES // MASTER_PER_PART
    mirror_slots = MASTER_PER_PART + MIRROR_PER_PART
    row_blocks = mirror_slots // 128
    master_part = (mirror_master_part[:, 0] * MASTER_PER_PART + mirror_row).astype(jnp.int32)
    used = (jnp.arange(TMAX, dtype=jnp.int32)[None, :] < tile_count[:, None]).astype(jnp.bfloat16)
    adjacency = (tile_weight * used[:, :, None, None]).reshape(partition_list, row_blocks, TMAX, 128, 128)
    columns = tile_column.reshape(partition_list, row_blocks, TMAX)
    master_parts = master_part.reshape(partition_list, MIRROR_PER_PART)
    projected = jnp.dot(features, w_neigh, preferred_element_type=jnp.float32).astype(jnp.bfloat16)

    def forward_one(items):
        tiles, cols, mirror_ids, owning_part = items
        slab = jnp.concatenate([owning_part, projected[mirror_ids]], axis=0).reshape(row_blocks, 128, HID)
        picked = slab[cols].astype(jnp.float32)
        tiles_wide = tiles.astype(jnp.float32)
        part = jnp.einsum('btij,btjf->bif', tiles_wide, picked)
        degree_part = lax.optimization_barrier(jnp.sum(tiles_wide, axis=(1, 3)))
        return (part.reshape(mirror_slots, HID), degree_part.reshape(mirror_slots))
    parts, degree_parts = lax.map(forward_one, (adjacency, columns, master_parts, projected.reshape(partition_list, MASTER_PER_PART, HID)))
    aggregate = parts[:, :MASTER_PER_PART].reshape(NODES, HID).at[master_part].add(parts[:, MASTER_PER_PART:].reshape(-1, HID))
    degree = degree_parts[:, :MASTER_PER_PART].reshape(NODES).at[master_part].add(degree_parts[:, MASTER_PER_PART:].reshape(-1))
    scale = 1.0 / (1.0 + degree)
    pre = jnp.dot(features, w_self, preferred_element_type=jnp.float32) + aggregate * scale[:, None]
    result, pullback = jax.vjp(activate, pre)
    mixed = result.astype(jnp.bfloat16)
    d_pre = pullback(cotangent.astype(jnp.float32))[0]
    d_pre_low = d_pre.astype(jnp.bfloat16)
    d_aggregate = (d_pre * scale[:, None]).astype(jnp.bfloat16)

    def backward_one(items):
        tiles, cols, mirror_ids, owning_part = items
        slab = jnp.concatenate([owning_part, d_aggregate[mirror_ids]], axis=0).reshape(row_blocks, 128, HID)
        contrib = jnp.einsum('btij,bif->btjf', tiles.astype(jnp.float32), slab.astype(jnp.float32))
        grads = jnp.zeros((row_blocks, 128, HID), jnp.float32).at[cols].add(contrib)
        return grads.reshape(mirror_slots, HID)
    d_parts = lax.map(backward_one, (adjacency, columns, master_parts, d_aggregate.reshape(partition_list, MASTER_PER_PART, HID)))
    d_projected = d_parts[:, :MASTER_PER_PART].reshape(NODES, HID).at[master_part].add(d_parts[:, MASTER_PER_PART:].reshape(-1, HID))
    d_projected = d_projected.astype(jnp.bfloat16)
    grad_features = (jnp.dot(d_pre_low, w_self.T, preferred_element_type=jnp.float32) + jnp.dot(d_projected, w_neigh.T, preferred_element_type=jnp.float32)).astype(jnp.bfloat16)
    grad_self = jnp.dot(features.T, d_pre_low, preferred_element_type=jnp.float32)
    grad_neigh = jnp.dot(features.T, d_projected, preferred_element_type=jnp.float32)
    return (mixed, grad_features, grad_self, grad_neigh)
```

```python
import jax
import jax.numpy as jnp
from jax import lax
from jax.sharding import PartitionSpec as P


def activate(value):
    return jax.nn.gelu(value, approximate=True)


def carry_values(buffer, partition_list, capacity):
    width = buffer.shape[1]
    moved = lax.all_to_all(
        buffer.reshape(partition_list, capacity, width),
        ("machine", "local"),
        split_axis=0,
        concat_axis=0,
        tiled=True,
    )
    return moved.reshape(buffer.shape)


def return_sums(rows, degree, partition_list, capacity):
    width = rows.shape[1]
    moved_rows, moved_degree = (
        lax.all_to_all(
            rows.astype(jnp.bfloat16).reshape(partition_list, capacity, width),
            ("machine", "local"),
            split_axis=0,
            concat_axis=0,
            tiled=True,
        ),
        lax.all_to_all(
            degree.reshape(partition_list, capacity),
            ("machine", "local"),
            split_axis=0,
            concat_axis=0,
            tiled=True,
        ),
    )
    return (moved_rows.reshape(rows.shape).astype(jnp.float32), moved_degree.reshape(degree.shape))


def return_grads(rows, partition_list, capacity):
    width = rows.shape[1]
    moved = lax.all_to_all(
        rows.astype(jnp.bfloat16).reshape(partition_list, capacity, width),
        ("machine", "local"),
        split_axis=0,
        concat_axis=0,
        tiled=True,
    )
    return moved.reshape(rows.shape).astype(jnp.float32)


def sum_everywhere(first, second, partition_list):
    rows, width = first.shape
    both = jnp.concatenate([first, second], axis=0).astype(jnp.bfloat16)
    parts = lax.all_to_all(
        both.reshape(partition_list, 2 * rows // partition_list, width),
        ("machine", "local"),
        split_axis=0,
        concat_axis=0,
        tiled=True,
    )
    share = jnp.sum(parts.astype(jnp.float32), axis=0).astype(jnp.bfloat16)
    whole = lax.all_to_all(
        jnp.broadcast_to(share[None], parts.shape),
        ("machine", "local"),
        split_axis=0,
        concat_axis=0,
        tiled=True,
    )
    whole = whole.reshape(2 * rows, width).astype(jnp.float32)
    return whole[:rows], whole[rows:]


def masked_tiles(tile_weight, tile_count):
    tiles_max = tile_weight.shape[1]
    used = (jnp.arange(tiles_max, dtype=jnp.int32)[None, :] < tile_count[:, None]).astype(
        tile_weight.dtype
    )
    return tile_weight * used[:, :, None, None]


def aggregate_tiles(tiles, tile_column, slab):
    row_blocks = tiles.shape[0]
    edge = tiles.shape[2]
    width = slab.shape[1]
    blocks = slab.reshape(row_blocks, edge, width)
    picked = blocks[tile_column]
    partial_value = jnp.einsum("btij,btjf->bif", tiles, picked, preferred_element_type=jnp.float32)
    degree = jnp.sum(tiles, axis=(1, 3), dtype=jnp.float32)
    return (partial_value.reshape(row_blocks * edge, width), degree.reshape(row_blocks * edge))


def spread_tiles(tiles, tile_column, d_slab):
    row_blocks = tiles.shape[0]
    edge = tiles.shape[2]
    width = d_slab.shape[1]
    rows_here = d_slab.reshape(row_blocks, edge, width)
    contrib = jnp.einsum("btij,bif->btjf", tiles, rows_here, preferred_element_type=jnp.float32)
    placing = (
        tile_column[:, :, None] == jnp.arange(row_blocks, dtype=jnp.int32)[None, None, :]
    ).astype(jnp.float32)
    grads = jnp.einsum("btc,btjf->cjf", placing, contrib, precision=lax.Precision.HIGHEST)
    return grads.reshape(row_blocks * edge, width)


def on_device(
    features,
    w_self,
    w_neigh,
    mirror_master_part,
    mirror_row,
    tile_count,
    tile_column,
    tile_weight,
    cotangent,
):
    masters = features.shape[0]
    mirrors = mirror_row.shape[0]
    width = w_neigh.shape[1]
    partition_list = lax.axis_size("machine") * lax.axis_size("local")
    capacity = 2 * mirrors // partition_list
    peer = mirror_master_part[:, 0]
    member = (peer[:, None] == jnp.arange(partition_list, dtype=jnp.int32)[None, :]).astype(
        jnp.int32
    )
    ranking = jnp.sum(member * (jnp.cumsum(member, axis=0) - 1), axis=1)
    places = peer * capacity + ranking
    wanted = jnp.zeros((partition_list * capacity,), jnp.int32).at[places].set(mirror_row)
    present = jnp.zeros((partition_list * capacity,), jnp.int32).at[places].set(1)
    asked, alive = (
        lax.all_to_all(
            wanted.reshape(partition_list, capacity),
            ("machine", "local"),
            split_axis=0,
            concat_axis=0,
            tiled=True,
        ),
        lax.all_to_all(
            present.reshape(partition_list, capacity),
            ("machine", "local"),
            split_axis=0,
            concat_axis=0,
            tiled=True,
        ),
    )
    asked = asked.reshape(-1)
    alive = alive.reshape(-1).astype(jnp.float32)
    tiles = masked_tiles(tile_weight, tile_count)
    projected = jnp.dot(features, w_neigh, preferred_element_type=jnp.float32).astype(jnp.bfloat16)
    arrived = carry_values(projected[asked], partition_list, capacity)
    slab = jnp.concatenate([projected, arrived[places]], axis=0)
    partial_value, degree_part = aggregate_tiles(tiles, tile_column, slab)
    send_rows = (
        jnp.zeros((partition_list * capacity, width), jnp.float32)
        .at[places]
        .set(partial_value[masters:])
    )
    send_degree = (
        jnp.zeros((partition_list * capacity,), jnp.float32).at[places].set(degree_part[masters:])
    )
    back_rows, back_degree = return_sums(send_rows, send_degree, partition_list, capacity)
    aggregate = partial_value[:masters].at[asked].add(back_rows * alive[:, None])
    degree = degree_part[:masters].at[asked].add(back_degree * alive)
    scale = 1.0 / (1.0 + degree)
    pre = jnp.dot(features, w_self, preferred_element_type=jnp.float32) + aggregate * scale[:, None]
    result, pullback = jax.vjp(activate, pre)
    mixed = result.astype(jnp.bfloat16)
    d_pre = pullback(cotangent.astype(jnp.float32))[0]
    d_pre_low = d_pre.astype(jnp.bfloat16)
    d_aggregate = (d_pre * scale[:, None]).astype(jnp.bfloat16)
    d_arrived = carry_values(d_aggregate[asked], partition_list, capacity)
    d_slab = jnp.concatenate([d_aggregate, d_arrived[places]], axis=0)
    d_partial = spread_tiles(tiles, tile_column, d_slab)
    send_grads = (
        jnp.zeros((partition_list * capacity, width), jnp.float32)
        .at[places]
        .set(d_partial[masters:])
    )
    back_grads = return_grads(send_grads, partition_list, capacity)
    d_projected = (
        d_partial[:masters].at[asked].add(back_grads * alive[:, None]).astype(jnp.bfloat16)
    )
    grad_features = (
        jnp.dot(d_pre_low, w_self.T, preferred_element_type=jnp.float32)
        + jnp.dot(d_projected, w_neigh.T, preferred_element_type=jnp.float32)
    ).astype(jnp.bfloat16)
    local_self = lax.dot_general(
        features, d_pre_low, (((0,), (0,)), ((), ())), preferred_element_type=jnp.float32
    )
    local_neigh = lax.dot_general(
        features, d_projected, (((0,), (0,)), ((), ())), preferred_element_type=jnp.float32
    )
    grad_self, grad_neigh = sum_everywhere(local_self, local_neigh, partition_list)
    return (mixed, grad_features, grad_self, grad_neigh)


def solution(mesh):
    placed = (
        P(("machine", "local"), None),
        P(),
        P(),
        P(("machine", "local"), None),
        P(("machine", "local")),
        P(("machine", "local")),
        P(("machine", "local"), None),
        P(("machine", "local"), None, None, None),
        P(("machine", "local"), None),
    )
    return jax.shard_map(
        on_device,
        mesh=mesh,
        in_specs=placed,
        out_specs=(P(("machine", "local"), None), P(("machine", "local"), None), P(), P()),
        check_vma=False,
    )
```

```python
import jax
import jax.numpy as jnp
from jax import lax
from jax.experimental import pallas as pl
from jax.experimental.pallas import tpu as pltpu
from jax.sharding import PartitionSpec as P

F32 = jnp.float32
BF16 = jnp.bfloat16
I32 = jnp.int32
EDGE = 128
SLOTS = 8
VMEM_BYTES = 60 * 1024 * 1024
EXACT = lax.Precision.HIGHEST
ROOT = 0.7978845608028654
CUBIC = 0.044715


def dot(a, b, ca=1, cb=0, precision=None):
    return lax.dot_general(
        a, b, (((ca,), (cb,)), ((), ())), precision=precision, preferred_element_type=F32
    )


def iota(shape, dim):
    return lax.broadcasted_iota(I32, shape, dim)


def pick_rows(rows, base, row):
    return jnp.where(iota((rows, row.shape[1]), 0) + base == row, 1.0, 0.0).astype(BF16)


def pick_columns(column, base, columns):
    lane = iota(column.shape, 1) + base
    parts = [
        jnp.where(column == lane + EDGE * g, 1.0, 0.0).astype(BF16) for g in range(columns // EDGE)
    ]
    return jnp.concatenate(parts, axis=1)


def params():
    return pltpu.CompilerParams(vmem_limit_bytes=VMEM_BYTES)


def whole(*shape):
    return pl.BlockSpec(shape, lambda *_: (0,) * len(shape))


def cost(flops, nbytes):
    return pl.CostEstimate(flops=int(flops), bytes_accessed=int(nbytes), transcendentals=0)


def place_kernel(count, peer, row, tiles, ask, slot_row, slot_column, held, sem):
    first = count.shape[0] - held.shape[0]
    copy = pltpu.make_async_copy(tiles.at[pl.ds(first, held.shape[0])], held, sem)
    copy.start()
    mirrors = peer.shape[1]
    parts = ask.shape[0]
    member = iota((parts, mirrors), 0) == peer[...]
    earlier = jnp.where(
        iota((mirrors, mirrors), 0) < iota((mirrors, mirrors), 1), 1.0, 0.0
    ).astype(BF16)
    before = dot(jnp.where(member, 1.0, 0.0).astype(BF16), earlier)
    rank = jnp.sum(jnp.where(member, before, 0.0), axis=0, keepdims=True).astype(I32)
    slot = peer[...] * SLOTS + rank
    slot_row[...] = slot
    slot_column[...] = jnp.transpose(
        jnp.broadcast_to(slot.astype(F32), (EDGE, mirrors))
    ).astype(I32)
    lanes = iota((EDGE, mirrors), 0)
    rows = jnp.where(member, (row[...] + 1).astype(F32), 0.0)
    asked = dot(rows, jnp.where(lanes == rank, 1.0, 0.0), 1, 1, EXACT)
    copy.wait()
    degrees = []
    for b in range(held.shape[0]):
        used = iota((16, held.shape[1] * EDGE), 1) < count[first + b] * EDGE
        flat = jnp.concatenate([held[b, t] for t in range(held.shape[1])], axis=1)
        degrees.append(dot(jnp.where(used, 1.0, 0.0).astype(BF16), flat, 1, 1)[0:1])
    degree = jnp.where(member, jnp.concatenate(degrees, axis=1), 0.0)
    ask[...] = asked + dot(degree, jnp.where(lanes == rank + SLOTS, 1.0, 0.0), 1, 1, EXACT)


def place(tile_count, peer, row, tiles, parts):
    mirrors = row.shape[0]
    blocks = mirrors // EDGE
    smem = pl.BlockSpec(memory_space=pltpu.SMEM)
    return pl.pallas_call(
        place_kernel,
        grid=(1,),
        in_specs=[
            smem,
            whole(1, mirrors),
            whole(1, mirrors),
            pl.BlockSpec(memory_space=pl.ANY),
        ],
        out_specs=[whole(parts, EDGE), whole(1, mirrors), whole(mirrors, EDGE)],
        out_shape=[
            jax.ShapeDtypeStruct((parts, EDGE), F32),
            jax.ShapeDtypeStruct((1, mirrors), I32),
            jax.ShapeDtypeStruct((mirrors, EDGE), I32),
        ],
        scratch_shapes=[
            pltpu.VMEM((blocks, *tiles.shape[1:]), BF16),
            pltpu.SemaphoreType.DMA,
        ],
        compiler_params=params(),
        cost_estimate=cost(1e9, 2 << 20),
    )(tile_count, peer.reshape(1, mirrors), row.reshape(1, mirrors), tiles)


def fetch_kernel(arrived, values, rows, asked_row, degree_row, asked_column):
    slots = rows.shape[0]
    parts = arrived.shape[0]
    spread = jnp.where(iota((slots, parts), 0) // SLOTS == iota((slots, parts), 1), 1.0, 0.0)
    every = dot(spread, arrived[...], 1, 0, EXACT)
    lane, own = iota((slots, EDGE), 1), iota((slots, EDGE), 0) % SLOTS
    asked = jnp.sum(jnp.where(lane == own, every, 0.0), axis=1, keepdims=True) - 1.0
    asked = jnp.broadcast_to(asked, (slots, EDGE))
    asked_column[...] = asked.astype(I32)
    asked_row[...] = jnp.transpose(asked)[0:8].astype(I32)
    degree = jnp.sum(jnp.where(lane == own + SLOTS, every, 0.0), axis=1, keepdims=True)
    degree_row[...] = jnp.transpose(jnp.broadcast_to(degree, (slots, EDGE)))[0:8]
    step = 256

    def body(g, carry):
        at = pl.ds(pl.multiple_of(g * step, step), step)
        rows[at, :] = dot(pick_columns(asked_column[at, :], 0, values.shape[0]), values[...]).astype(BF16)
        return carry

    lax.fori_loop(0, slots // step, body, 0)


def fetch(arrived, values, slots):
    parts, width = arrived.shape[0], values.shape[1]
    return pl.pallas_call(
        fetch_kernel,
        grid=(1,),
        in_specs=[whole(parts, EDGE), whole(*values.shape)],
        out_specs=[whole(slots, width), whole(8, slots), whole(8, slots), whole(slots, EDGE)],
        out_shape=[
            jax.ShapeDtypeStruct((slots, width), BF16),
            jax.ShapeDtypeStruct((8, slots), I32),
            jax.ShapeDtypeStruct((8, slots), F32),
            jax.ShapeDtypeStruct((slots, EDGE), I32),
        ],
        compiler_params=params(),
        cost_estimate=cost(2e9, 2 << 20),
    )(arrived, values)


def near_kernel(count, column, tiles, values, partial, degree, slab):
    b = pl.program_id(0)
    blocks = values.shape[0] // EDGE
    width = values.shape[1]

    @pl.when(b == 0)
    def _():
        slab[: values.shape[0], :width] = values[...]
        slab[: values.shape[0], width:] = jnp.ones((values.shape[0], EDGE), BF16)
        slab[values.shape[0] :, :] = jnp.zeros((2 * EDGE, width + EDGE), BF16)
        slab[values.shape[0] + EDGE :, width:] = jnp.ones((EDGE, EDGE), BF16)

    n = count[b]

    def body(i, total):
        right = []
        for k in range(4):
            t = 4 * i + k
            c = column[b, t]
            c = jnp.where(t < n, jnp.where(c < blocks, c, blocks + 1), blocks)
            right.append(slab[pl.ds(pl.multiple_of(c * EDGE, EDGE), EDGE), :])
        left = jnp.concatenate([tiles[0, 4 * i + k] for k in range(4)], axis=1)
        return total + dot(left, jnp.concatenate(right, axis=0))

    total = lax.fori_loop(0, (n + 3) // 4, body, jnp.zeros((EDGE, width + EDGE), F32))
    partial[...] = total[:, :width]
    degree[...] = total[:, width:]


def near(tile_count, tile_column, tiles, values):
    row_blocks, most = tiles.shape[:2]
    rows, width = values.shape
    return pl.pallas_call(
        near_kernel,
        grid_spec=pltpu.PrefetchScalarGridSpec(
            num_scalar_prefetch=2,
            grid=(row_blocks,),
            in_specs=[
                pl.BlockSpec((1, most, EDGE, EDGE), lambda b, *_: (b, 0, 0, 0)),
                whole(rows, width),
            ],
            out_specs=[
                pl.BlockSpec((EDGE, width), lambda b, *_: (b, 0)),
                pl.BlockSpec((EDGE, EDGE), lambda b, *_: (b, 0)),
            ],
            scratch_shapes=[pltpu.VMEM((rows + 2 * EDGE, width + EDGE), BF16)],
        ),
        out_shape=[
            jax.ShapeDtypeStruct((row_blocks * EDGE, width), F32),
            jax.ShapeDtypeStruct((row_blocks * EDGE, EDGE), F32),
        ],
        compiler_params=params(),
        cost_estimate=cost(6e9, 16 << 20),
    )(tile_count, tile_column, tiles, values)


def mirror_out_kernel(
    count, column, arrived, slot_column, slot_row, partial, tiles, send, slab, held, total, sem
):
    blocks = held.shape[0]
    first = count.shape[0] - blocks
    copy = pltpu.make_async_copy(tiles.at[pl.ds(first, blocks)], held, sem)
    copy.start()
    slab[...] = dot(pick_columns(slot_column[...], 0, arrived.shape[0]), arrived[...]).astype(BF16)
    total[...] = partial[...]
    copy.wait()
    for b in range(blocks):
        n = count[first + b]

        def body(t, carry):
            c = column[first + b, t]

            @pl.when(c >= first)
            def _():
                at = pl.ds(pl.multiple_of((c - first) * EDGE, EDGE), EDGE)
                total[b * EDGE : (b + 1) * EDGE, :] += dot(held[b, t], slab[at, :])

            return carry

        lax.fori_loop(0, n, body, 0)
    send[...] = dot(pick_rows(send.shape[0], 0, slot_row[...]), total[...].astype(BF16)).astype(BF16)


def mirror_out(tile_count, tile_column, arrived, slot_column, slot_row, partial, tiles):
    slots, width = arrived.shape
    mirrors = slot_row.shape[1]
    last = partial.shape[0] // mirrors - 1
    smem = pl.BlockSpec(memory_space=pltpu.SMEM)
    return pl.pallas_call(
        mirror_out_kernel,
        grid=(1,),
        in_specs=[
            smem,
            smem,
            whole(slots, width),
            whole(mirrors, EDGE),
            whole(1, mirrors),
            pl.BlockSpec((mirrors, width), lambda *_: (last, 0)),
            pl.BlockSpec(memory_space=pl.ANY),
        ],
        out_specs=[whole(slots, width), whole(mirrors, width)],
        out_shape=[
            jax.ShapeDtypeStruct((slots, width), BF16),
            jax.ShapeDtypeStruct((mirrors, width), BF16),
        ],
        scratch_shapes=[
            pltpu.VMEM((mirrors // EDGE, *tiles.shape[1:]), BF16),
            pltpu.VMEM((mirrors, width), F32),
            pltpu.SemaphoreType.DMA,
        ],
        compiler_params=params(),
        cost_estimate=cost(2e9, 4 << 20),
    )(tile_count, tile_column, arrived, slot_column, slot_row, partial, tiles)


def far_kernel(
    count, column, tiles, mirrors, partial, degree, own, asked_row, degree_row, base, scale, slab
):
    b = pl.program_id(0)
    blocks = mirrors.shape[0] // EDGE
    first = count.shape[0] - blocks

    @pl.when(b == 0)
    def _():
        slab[: mirrors.shape[0], :] = mirrors[...]
        slab[mirrors.shape[0] :, :] = jnp.zeros((EDGE, mirrors.shape[1]), BF16)

    n = count[b]

    def body(i, total):
        right = []
        for k in range(4):
            t = 4 * i + k
            c = column[b, t]
            c = jnp.where((t < n) & (c >= first), c - first, blocks)
            right.append(slab[pl.ds(pl.multiple_of(c * EDGE, EDGE), EDGE), :])
        left = jnp.concatenate([tiles[0, 4 * i + k] for k in range(4)], axis=1)
        return total + dot(left, jnp.concatenate(right, axis=0))

    total = lax.fori_loop(0, (n + 3) // 4, body, partial[...])
    hit = iota((EDGE, asked_row.shape[1]), 0) + b * EDGE == asked_row[0:1]
    more = jnp.sum(jnp.where(hit, degree_row[0:1], 0.0), axis=1, keepdims=True)
    factor = 1.0 / (1.0 + (degree[...] + more))
    scale[...] = factor
    base[...] = own[...] + total * jnp.concatenate([factor, factor], axis=1)


def far(tile_count, tile_column, tiles, mirrors, partial, degree, own, asked_row, degree_row):
    most = tiles.shape[1]
    masters, width = own.shape
    return pl.pallas_call(
        far_kernel,
        grid_spec=pltpu.PrefetchScalarGridSpec(
            num_scalar_prefetch=2,
            grid=(masters // EDGE,),
            in_specs=[
                pl.BlockSpec((1, most, EDGE, EDGE), lambda b, *_: (b, 0, 0, 0)),
                whole(*mirrors.shape),
                pl.BlockSpec((EDGE, width), lambda b, *_: (b, 0)),
                pl.BlockSpec((EDGE, EDGE), lambda b, *_: (b, 0)),
                pl.BlockSpec((EDGE, width), lambda b, *_: (b, 0)),
                whole(*asked_row.shape),
                whole(*degree_row.shape),
            ],
            out_specs=[
                pl.BlockSpec((EDGE, width), lambda b, *_: (b, 0)),
                pl.BlockSpec((EDGE, EDGE), lambda b, *_: (b, 0)),
            ],
            scratch_shapes=[pltpu.VMEM((mirrors.shape[0] + EDGE, width), BF16)],
        ),
        out_shape=[
            jax.ShapeDtypeStruct((masters, width), F32),
            jax.ShapeDtypeStruct((masters, EDGE), F32),
        ],
        compiler_params=params(),
        cost_estimate=cost(6e9, 16 << 20),
    )(tile_count, tile_column, tiles, mirrors, partial, degree, own, asked_row, degree_row)


def turn_kernel(base, scale, cotangent, back, asked_row, asked_column, mixed, low, spread, send, total):
    g = pl.program_id(0)
    rows = base.shape[0]
    both = jnp.concatenate([scale[...], scale[...]], axis=1)
    added = dot(pick_rows(rows, g * rows, asked_row[0:1]), back[...])
    u = base[...] + added * both
    square = u * u
    bend = jnp.tanh(ROOT * (u + CUBIC * square * u))
    half = 0.5 * (1.0 + bend)
    mixed[...] = (u * half).astype(BF16)
    slope = half + 0.5 * u * (1.0 - bend * bend) * (ROOT * (1.0 + 3.0 * CUBIC * square))
    d_pre = cotangent[...].astype(F32) * slope
    low[...] = d_pre.astype(BF16)
    d_aggregate = (d_pre * both).astype(BF16)
    spread[...] = d_aggregate
    part = dot(pick_columns(asked_column[...], g * rows, rows), d_aggregate)

    @pl.when(g == 0)
    def _():
        total[...] = part

    @pl.when(g > 0)
    def _():
        total[...] += part

    @pl.when(g == pl.num_programs(0) - 1)
    def _():
        send[...] = total[...].astype(BF16)


def turn(base, scale, cotangent, back, asked_row, asked_column):
    masters, width = base.shape
    slots = back.shape[0]
    rows = 256
    block = pl.BlockSpec((rows, width), lambda g: (g, 0))
    return pl.pallas_call(
        turn_kernel,
        grid=(masters // rows,),
        in_specs=[
            block,
            pl.BlockSpec((rows, EDGE), lambda g: (g, 0)),
            block,
            whole(slots, width),
            whole(*asked_row.shape),
            whole(*asked_column.shape),
        ],
        out_specs=[block, block, block, whole(slots, width)],
        out_shape=[jax.ShapeDtypeStruct((masters, width), BF16)] * 3
        + [jax.ShapeDtypeStruct((slots, width), BF16)],
        scratch_shapes=[pltpu.VMEM((slots, width), F32)],
        compiler_params=params(),
        cost_estimate=cost(3e9, 8 << 20),
    )(base, scale, cotangent, back, asked_row, asked_column)


def add_back(n, count_from, column, b, tiles, values, total, low, high):
    def body(i, carry):
        right = jnp.concatenate([tiles[0, 2 * i], tiles[0, 2 * i + 1]], axis=1)
        product = dot(values, right)
        for k in range(2):
            t = 2 * i + k
            c = column[b, t]
            c = jnp.where((t < n) & (c >= low) & (c < high), c - low, high - low)
            total[c] += product[:, k * EDGE : (k + 1) * EDGE]
        return carry

    lax.fori_loop(count_from, (n + 1) // 2, body, 0)


def back_near_kernel(count, column, tiles, values, total):
    b = pl.program_id(0)

    @pl.when(b == 0)
    def _():
        total[...] = jnp.zeros(total.shape, F32)

    turned = jnp.transpose(values[...].astype(F32)).astype(BF16)
    add_back(count[b], 0, column, b, tiles, turned, total, 0, total.shape[0] - 1)


def back_near(tile_count, tile_column, tiles, values):
    row_blocks, most = tiles.shape[:2]
    masters, width = values.shape
    return pl.pallas_call(
        back_near_kernel,
        grid_spec=pltpu.PrefetchScalarGridSpec(
            num_scalar_prefetch=2,
            grid=(masters // EDGE,),
            in_specs=[
                pl.BlockSpec((1, most, EDGE, EDGE), lambda b, *_: (b, 0, 0, 0)),
                pl.BlockSpec((EDGE, width), lambda b, *_: (b, 0)),
            ],
            out_specs=whole(row_blocks + 1, width, EDGE),
        ),
        out_shape=jax.ShapeDtypeStruct((row_blocks + 1, width, EDGE), F32),
        compiler_params=params(),
        cost_estimate=cost(6e9, 16 << 20),
    )(tile_count, tile_column, tiles, values)


def mirror_back_kernel(
    count, column, arrived, slot_column, slot_row, partial, tiles, send, turned, held, total, rows, sem
):
    blocks = held.shape[0]
    first = count.shape[0] - blocks
    copy = pltpu.make_async_copy(tiles.at[pl.ds(first, blocks)], held, sem)
    copy.start()
    slab = dot(pick_columns(slot_column[...], 0, arrived.shape[0]), arrived[...])
    for b in range(blocks):
        turned[b] = jnp.transpose(slab[b * EDGE : (b + 1) * EDGE]).astype(BF16)
    total[...] = partial[...]
    copy.wait()
    for b in range(blocks):
        n = count[first + b]

        def body(t, carry):
            c = column[first + b, t]

            @pl.when(c >= first)
            def _():
                total[c - first] += dot(turned[b], held[b, t])

            return carry

        lax.fori_loop(0, n, body, 0)
    for c in range(blocks):
        rows[c * EDGE : (c + 1) * EDGE, :] = jnp.transpose(total[c]).astype(BF16)
    send[...] = dot(pick_rows(send.shape[0], 0, slot_row[...]), rows[...]).astype(BF16)


def mirror_back(tile_count, tile_column, arrived, slot_column, slot_row, partial, tiles):
    slots, width = arrived.shape
    mirrors = slot_row.shape[1]
    blocks = mirrors // EDGE
    at = tiles.shape[0] // blocks - 1
    smem = pl.BlockSpec(memory_space=pltpu.SMEM)
    return pl.pallas_call(
        mirror_back_kernel,
        grid=(1,),
        in_specs=[
            smem,
            smem,
            whole(slots, width),
            whole(mirrors, EDGE),
            whole(1, mirrors),
            pl.BlockSpec((blocks, width, EDGE), lambda *_: (at, 0, 0)),
            pl.BlockSpec(memory_space=pl.ANY),
        ],
        out_specs=[whole(slots, width), whole(blocks, width, EDGE)],
        out_shape=[
            jax.ShapeDtypeStruct((slots, width), BF16),
            jax.ShapeDtypeStruct((blocks, width, EDGE), BF16),
        ],
        scratch_shapes=[
            pltpu.VMEM((blocks, *tiles.shape[1:]), BF16),
            pltpu.VMEM((blocks, width, EDGE), F32),
            pltpu.VMEM((mirrors, width), BF16),
            pltpu.SemaphoreType.DMA,
        ],
        compiler_params=params(),
        cost_estimate=cost(2e9, 4 << 20),
    )(tile_count, tile_column, arrived, slot_column, slot_row, partial, tiles)


def back_far_kernel(count, column, tiles, turned, partial, total):
    b = pl.program_id(0)
    masters = total.shape[0] - 1

    @pl.when(b == 0)
    def _():
        total[:masters] = partial[...]
        total[masters] = jnp.zeros(total.shape[1:], F32)

    at = masters + b
    add_back(count[at], 0, column, at, tiles, turned[0], total, 0, masters)


def back_far(tile_count, tile_column, tiles, turned, partial):
    row_blocks, most = tiles.shape[:2]
    blocks, width = turned.shape[:2]
    masters = row_blocks - blocks
    return pl.pallas_call(
        back_far_kernel,
        grid_spec=pltpu.PrefetchScalarGridSpec(
            num_scalar_prefetch=2,
            grid=(blocks,),
            in_specs=[
                pl.BlockSpec((1, most, EDGE, EDGE), lambda b, *_: (masters + b, 0, 0, 0)),
                pl.BlockSpec((1, width, EDGE), lambda b, *_: (b, 0, 0)),
                whole(masters, width, EDGE),
            ],
            out_specs=whole(masters + 1, width, EDGE),
        ),
        out_shape=jax.ShapeDtypeStruct((masters + 1, width, EDGE), F32),
        compiler_params=params(),
        cost_estimate=cost(3e9, 8 << 20),
    )(tile_count, tile_column, tiles, turned, partial)


def finish_kernel(partial, back, asked_column, features, grad_self, turned, grads, flipped, total):
    g = pl.program_id(0)
    columns = turned.shape[1]
    width = turned.shape[0]
    inputs = features.shape[1]

    @pl.when(g == 0)
    def _():
        flipped[...] = jnp.transpose(back[...].astype(F32)).astype(BF16)
        total[...] = jnp.zeros(total.shape, F32)

    own = jnp.concatenate([partial[0], partial[1]], axis=1)
    value = own + dot(flipped[...], pick_columns(asked_column[...], g * columns, columns))
    value = value.astype(BF16)
    turned[...] = value
    total[...] += dot(value, features[...])

    @pl.when(g == pl.num_programs(0) - 1)
    def _():
        for h in range(width // EDGE):
            part = pl.ds(h * EDGE, EDGE)
            grads[pl.ds(h * inputs, inputs), :] = grad_self[:, h * EDGE : (h + 1) * EDGE]
            grads[pl.ds((width // EDGE + h) * inputs, inputs), :] = jnp.transpose(
                total[part, :]
            ).astype(BF16)


def finish(partial, back, asked_column, features, grad_self):
    slots, width = back.shape
    masters, inputs = features.shape
    columns = 2 * EDGE
    lines = 2 * inputs * width // EDGE
    return pl.pallas_call(
        finish_kernel,
        grid=(masters // columns,),
        in_specs=[
            pl.BlockSpec((2, width, EDGE), lambda g: (g, 0, 0)),
            whole(slots, width),
            whole(slots, EDGE),
            pl.BlockSpec((columns, inputs), lambda g: (g, 0)),
            whole(inputs, width),
        ],
        out_specs=[pl.BlockSpec((width, columns), lambda g: (0, g)), whole(lines, EDGE)],
        out_shape=[
            jax.ShapeDtypeStruct((width, masters), BF16),
            jax.ShapeDtypeStruct((lines, EDGE), BF16),
        ],
        scratch_shapes=[pltpu.VMEM((width, slots), BF16), pltpu.VMEM((width, inputs), F32)],
        compiler_params=params(),
        cost_estimate=cost(3e9, 8 << 20),
    )(partial, back, asked_column, features, grad_self)


def share_kernel(parts, out):
    share = jnp.sum(parts[...].astype(F32), axis=0, keepdims=True).astype(BF16)
    out[...] = jnp.broadcast_to(share, out.shape)


def share_out(parts):
    return pl.pallas_call(
        share_kernel,
        out_shape=jax.ShapeDtypeStruct(parts.shape, BF16),
        compiler_params=params(),
        cost_estimate=cost(1e6, 2 << 20),
    )(parts)


def unpack_kernel(lines, first, second):
    inputs = first.shape[0]
    for at, out in enumerate((first, second)):
        halves = [
            lines[(2 * at + h) * inputs : (2 * at + h + 1) * inputs, :].astype(F32) for h in range(2)
        ]
        out[...] = jnp.concatenate(halves, axis=1)


def unpack(lines, inputs, width):
    return pl.pallas_call(
        unpack_kernel,
        out_shape=[jax.ShapeDtypeStruct((inputs, width), F32)] * 2,
        compiler_params=params(),
        cost_estimate=cost(1e6, 2 << 20),
    )(lines)


def exchange(buffer, parts):
    moved = lax.all_to_all(
        buffer.reshape(parts, buffer.shape[0] // parts, buffer.shape[1]),
        ("machine", "local"),
        split_axis=0,
        concat_axis=0,
        tiled=True,
    )
    return moved.reshape(buffer.shape)


def on_device(
    features,
    w_self,
    w_neigh,
    mirror_master_part,
    mirror_row,
    tile_count,
    tile_column,
    tile_weight,
    cotangent,
):
    inputs, width = w_neigh.shape
    parts = lax.axis_size("machine") * lax.axis_size("local")
    slots = SLOTS * parts
    peer = mirror_master_part[:, 0]
    ask, slot_row, slot_column = place(tile_count, peer, mirror_row, tile_weight, parts)
    asked = exchange(ask, parts)
    projected = jnp.dot(features, w_neigh, preferred_element_type=F32).astype(BF16)
    own = jnp.dot(features, w_self, preferred_element_type=F32)
    rows, asked_row, degree_row, asked_column = fetch(asked, projected, slots)
    rows, projected = lax.optimization_barrier((rows, projected))
    arrived = exchange(rows, parts)
    partial, degree = near(tile_count, tile_column, tile_weight, projected)
    send, slab = mirror_out(
        tile_count, tile_column, arrived, slot_column, slot_row, partial, tile_weight
    )
    back = exchange(send, parts)
    base, scale = far(
        tile_count, tile_column, tile_weight, slab, partial, degree, own, asked_row, degree_row
    )
    mixed, low, spread, send = turn(base, scale, cotangent, back, asked_row, asked_column)
    arrived = exchange(send, parts)
    partial = back_near(tile_count, tile_column, tile_weight, spread)
    grad_self = lax.dot_general(
        features, low, (((0,), (0,)), ((), ())), preferred_element_type=F32
    ).astype(BF16)
    send, turned = mirror_back(
        tile_count, tile_column, arrived, slot_column, slot_row, partial, tile_weight
    )
    back = exchange(send, parts)
    partial = back_far(tile_count, tile_column, tile_weight, turned, partial)
    d_projected, grads = finish(partial, back, asked_column, features, grad_self)
    shares = exchange(grads, parts).reshape(parts, -1, EDGE)
    grad_features = (
        lax.dot_general(low, w_self, (((1,), (1,)), ((), ())), preferred_element_type=F32)
        + lax.dot_general(d_projected, w_neigh, (((0,), (1,)), ((), ())), preferred_element_type=F32)
    ).astype(BF16)
    sums = exchange(share_out(shares).reshape(grads.shape), parts)
    grad_self, grad_neigh = unpack(sums, inputs, width)
    return (mixed, grad_features, grad_self, grad_neigh)


def solution(mesh):
    placed = (
        P(("machine", "local"), None),
        P(),
        P(),
        P(("machine", "local"), None),
        P(("machine", "local")),
        P(("machine", "local")),
        P(("machine", "local"), None),
        P(("machine", "local"), None, None, None),
        P(("machine", "local"), None),
    )
    return jax.shard_map(
        on_device,
        mesh=mesh,
        in_specs=placed,
        out_specs=(P(("machine", "local"), None), P(("machine", "local"), None), P(), P()),
        check_vma=False,
    )
```

```python
import jax
import jax.numpy as jnp
from jax import lax
from jax.experimental import pallas as pl
from jax.experimental.pallas import tpu as pltpu
from jax.sharding import PartitionSpec as P

F32 = jnp.float32
BF16 = jnp.bfloat16
I32 = jnp.int32
EDGE = 128
SLOTS = 8
MIB = 1024 * 1024
VMEM_BYTES = 60 * MIB
GROUP = 4
ROOT = 0.7978845608028654
CUBIC = 0.044715
EVERY = ("chip", "core", "local")


def dot(a, b, ca=1, cb=0):
    return lax.dot_general(a, b, (((ca,), (cb,)), ((), ())), preferred_element_type=F32)


def iota(shape, dim):
    return lax.broadcasted_iota(I32, shape, dim)


def pick_rows(rows, base, row):
    return jnp.where(iota((rows, row.shape[1]), 0) + base == row, 1.0, 0.0).astype(BF16)


def pick_columns(column, base, columns):
    lane = iota(column.shape, 1) + base
    parts = [
        jnp.where(column == lane + EDGE * g, 1.0, 0.0).astype(BF16) for g in range(columns // EDGE)
    ]
    return jnp.concatenate(parts, axis=1)


def block(b, size=EDGE):
    return pl.ds(pl.multiple_of(b * size, size), size)


def struct(*shape, dtype=BF16):
    return jax.ShapeDtypeStruct(shape, dtype)


class Moved:
    def __init__(self, far, held, sems, pieces, inward):
        self.far, self.held, self.sems, self.pieces, self.inward = far, held, sems, pieces, inward
        self.size = far.shape[0] // pieces
        self.started, self.waited = False, False

    def rows(self, p):
        return slice(p * self.size, (p + 1) * self.size)

    def copy(self, p):
        at = pl.ds(p * self.size, self.size)
        ends = self.far.at[at], self.held.at[at]
        return pltpu.make_async_copy(*(ends if self.inward else ends[::-1]), self.sems.at[p])

    def start(self, p=0):
        self.started = True
        self.copy(p).start()

    def wait(self, p=0):
        self.copy(p).wait()

    def all(self):
        if not self.waited:
            for p in range(self.pieces):
                self.wait(p)
        self.waited = True
        return self.held


def run(kernel, scalars, ins, outs, scratch=(), flops=1e9):
    ins, outs = list(ins), list(outs)
    n, m = len(ins), len(outs)
    own = [k for k in range(n + m) if k >= n or ins[k][1]]

    def body(*refs):
        scalar_refs, refs = refs[: len(scalars)], refs[len(scalars) :]
        far, refs = list(refs[: n + m]), refs[n + m :]
        held, sems, rest = refs[: len(own)], refs[len(own) : 2 * len(own)], refs[2 * len(own) :]
        for at, k in enumerate(own):
            far[k] = Moved(far[k], held[at], sems[at], (ins + outs)[k][1], k < n)
            if k < n and ins[k][1] == 1:
                far[k].start()
        kernel(scalar_refs, far[:n], far[n:], *rest)
        for out in far[n:]:
            if not out.started:
                for p in range(out.pieces):
                    out.start(p)
        for out in far[n:]:
            out.all()

    def place_of(k):
        shape = ins[k][0] if k < n else outs[k - n][0]
        spare = 0 if k < n else outs[k - n][2]
        return pltpu.VMEM((shape.shape[0] + spare, *shape.shape[1:]), shape.dtype)

    smem, any_space = pl.BlockSpec(memory_space=pltpu.SMEM), pl.BlockSpec(memory_space=pl.ANY)
    return pl.pallas_call(
        body,
        in_specs=[smem] * len(scalars) + [any_space] * n,
        out_specs=[any_space] * m,
        out_shape=[out[0] for out in outs],
        scratch_shapes=[place_of(k) for k in own]
        + [pltpu.SemaphoreType.DMA(((ins + outs)[k][1],)) for k in own]
        + list(scratch),
        compiler_params=params(),
        cost_estimate=cost(flops),
    )(*scalars, *[x for x, _ in ins])


def params():
    return pltpu.CompilerParams(vmem_limit_bytes=VMEM_BYTES)


def cost(flops):
    return pl.CostEstimate(flops=int(flops), bytes_accessed=4 * MIB, transcendentals=0)


def groups(tiles):
    return tiles.shape[0] // GROUP


def thirds(value):
    first = value.astype(BF16).astype(F32)
    second = (value - first).astype(BF16).astype(F32)
    return first, second, value - first - second


def used_ones(n, most):
    return jnp.concatenate(
        [jnp.full((EDGE, EDGE), jnp.where(t < n, 1.0, 0.0), F32).astype(BF16) for t in range(most)],
        axis=0,
    )


def place_kernel(scalars, ins, outs):
    (count,) = scalars
    peer, row, tiles = ins
    ask, slot_row, slot_column = outs
    mirrors = peer.held.shape[1]
    parts = ask.held.shape[0]
    blocks, most = mirrors // EDGE, tiles.held.shape[1]
    first = count.shape[0] - blocks
    last = tiles.pieces - 1
    tiles.start(last)
    peer = peer.all()[...]
    member = iota((parts, mirrors), 0) == peer
    chosen = jnp.where(member, 1.0, 0.0).astype(BF16)
    earlier = jnp.where(
        iota((mirrors, mirrors), 0) < iota((mirrors, mirrors), 1), 1.0, 0.0
    ).astype(BF16)
    before = dot(chosen, earlier)
    rank = jnp.sum(jnp.where(member, before, 0.0), axis=0, keepdims=True).astype(I32)
    slot = peer * SLOTS + rank
    slot_row.held[...] = slot
    slot_column.held[...] = jnp.transpose(
        jnp.broadcast_to(slot.astype(F32), (EDGE, mirrors))
    ).astype(I32)
    slot_row.start()
    slot_column.start()
    lane = iota((EDGE, mirrors), 0) - rank
    named = row.all()[...] + 1
    degrees = []
    tiles.wait(last)
    for b in range(first, first + blocks):
        flat = jnp.concatenate([tiles.held[b, t] for t in range(most)], axis=1)
        degrees.append(jnp.transpose(dot(flat, used_ones(count[b], most)))[0:1])
    fields = (named // EDGE).astype(F32), (named % EDGE).astype(F32)
    fields += thirds(jnp.concatenate(degrees, axis=1))
    lines = jnp.zeros((EDGE, mirrors), F32)
    for k, field in enumerate(fields):
        lines = jnp.where(lane == SLOTS * k, field, lines)
    ask.held[...] = dot(chosen, lines.astype(BF16), 1, 1)


def place(tile_count, peer, row, tiles, parts):
    mirrors = row.shape[0]
    return run(
        place_kernel,
        (tile_count,),
        ((peer.reshape(1, mirrors), 1), (row.reshape(1, mirrors), 1), (tiles, groups(tiles))),
        (
            (struct(parts, EDGE, dtype=F32), 1, 0),
            (struct(1, mirrors, dtype=I32), 1, 0),
            (struct(mirrors, EDGE, dtype=I32), 1, 0),
        ),
    )


def slot_lines(arrived, slots):
    parts = arrived.shape[0]
    spread = jnp.where(iota((slots, parts), 0) // SLOTS == iota((slots, parts), 1), 1.0, 0.0)
    return dot(spread.astype(BF16), arrived[...].astype(BF16))


def gather(values, asked_column, rows):
    step = 512
    for g in range(rows.shape[0] // step):
        at = slice(g * step, (g + 1) * step)
        rows[at, :] = dot(pick_columns(asked_column[at, :], 0, values.shape[0]), values[...]).astype(BF16)


def fetch_kernel(scalars, ins, outs):
    arrived, values = ins
    rows, asked_column = outs
    slots = rows.held.shape[0]
    every = slot_lines(arrived.all(), slots)
    lane = iota((slots, EDGE), 1) - iota((slots, EDGE), 0) % SLOTS
    asked = jnp.where(lane == 0, every * EDGE, jnp.where(lane == SLOTS, every, 0.0))
    asked = jnp.sum(asked, axis=1, keepdims=True) - 1.0
    asked_column.held[...] = jnp.broadcast_to(asked, (slots, EDGE)).astype(I32)
    asked_column.start()
    gather(values.all(), asked_column.held, rows.held)


def fetch(arrived, values, slots):
    return run(
        fetch_kernel,
        (),
        ((arrived, 1), (values, 1)),
        ((struct(slots, values.shape[1]), 1, 0), (struct(slots, EDGE, dtype=I32), 1, 0)),
        flops=2e9,
    )


def near_kernel(scalars, ins, outs, slab):
    count, column = scalars
    values, arrived, asked_column, tiles = ins
    partial, asked_row, degree_row = outs
    most = tiles.held.shape[1]
    for g in range(tiles.pieces):
        tiles.start(g)
    rows, width = values.held.shape
    blocks = rows // EDGE
    slab[rows:, :] = jnp.zeros((EDGE, width), BF16)
    slab[:rows, :] = values.all()[...]
    for g in range(tiles.pieces):
        tiles.wait(g)
        for b in range(g * GROUP, (g + 1) * GROUP):
            right = []
            for t in range(most):
                c = column[b, t]
                c = jnp.where((t < count[b]) & (c < blocks), c, blocks)
                right.append(slab[block(c), :])
            left = jnp.concatenate([tiles.held[b, t] for t in range(most)], axis=1)
            partial.held[b * EDGE : (b + 1) * EDGE, :] = dot(left, jnp.concatenate(right, axis=0))
        partial.start(g)
    slots = asked_column.held.shape[0]
    asked_row.held[...] = jnp.transpose(asked_column.all()[...].astype(F32))[0:8].astype(I32)
    lane = iota((slots, EDGE), 1) - iota((slots, EDGE), 0) % SLOTS
    mine = (lane == 2 * SLOTS) | (lane == 3 * SLOTS) | (lane == 4 * SLOTS)
    sums = jnp.sum(jnp.where(mine, slot_lines(arrived.all(), slots), 0.0), axis=1, keepdims=True)
    degree_row.held[...] = jnp.transpose(jnp.broadcast_to(sums, (slots, EDGE)))[0:8]


def near(tile_count, tile_column, arrived, asked_column, values, tiles):
    rows, width = values.shape
    slots, row_blocks = asked_column.shape[0], tiles.shape[0]
    return run(
        near_kernel,
        (tile_count, tile_column),
        ((values, 1), (arrived, 1), (asked_column, 1), (tiles, groups(tiles))),
        (
            (struct(row_blocks * EDGE, width, dtype=F32), groups(tiles), 0),
            (struct(8, slots, dtype=I32), 1, 0),
            (struct(8, slots, dtype=F32), 1, 0),
        ),
        (pltpu.VMEM((rows + EDGE, width), BF16),),
        flops=5e9,
    )


def far_product(n, column, b, tiles, padded, first):
    blocks = padded.shape[0] // EDGE - 1
    right = []
    for t in range(tiles.shape[1]):
        c = column[b, t]
        c = jnp.where((t < n) & (c >= first), c - first, blocks)
        right.append(padded[block(c), :])
    left = jnp.concatenate([tiles[b, t] for t in range(tiles.shape[1])], axis=1)
    return dot(left, jnp.concatenate(right, axis=0))


def mirror_out_kernel(scalars, ins, outs, total):
    count, column = scalars
    arrived, slot_column, partial, tiles, slot_row = ins
    send, padded = outs
    mirrors = total.shape[0]
    blocks = mirrors // EDGE
    first = tiles.held.shape[0] - blocks
    last = tiles.pieces - 1
    tiles.start(last)
    partial.start(last)
    pick = pick_columns(slot_column.all()[...], 0, arrived.held.shape[0])
    padded.held[:mirrors, :] = dot(pick, arrived.all()[...]).astype(BF16)
    padded.held[mirrors:, :] = jnp.zeros((EDGE, padded.held.shape[1]), BF16)
    padded.start()
    partial.wait(last)
    tiles.wait(last)
    for b in range(first, first + blocks):
        more = far_product(count[b], column, b, tiles.held, padded.held, first)
        total[(b - first) * EDGE : (b - first + 1) * EDGE, :] = (
            partial.held[b * EDGE : (b + 1) * EDGE, :] + more
        ).astype(BF16)
    slots = send.held.shape[0]
    send.held[...] = dot(pick_rows(slots, 0, slot_row.all()[...]), total[...]).astype(BF16)


def mirror_out(tile_count, tile_column, arrived, slot_column, slot_row, partial, tiles):
    slots, width = arrived.shape
    mirrors = slot_row.shape[1]
    return run(
        mirror_out_kernel,
        (tile_count, tile_column),
        (
            (arrived, 1),
            (slot_column, 1),
            (partial, groups(tiles)),
            (tiles, groups(tiles)),
            (slot_row, 1),
        ),
        ((struct(slots, width), 1, 0), (struct(mirrors + EDGE, width), 1, 0)),
        (pltpu.VMEM((mirrors, width), BF16),),
        flops=2e9,
    )


def far_kernel(scalars, ins, outs):
    count, column = scalars
    padded, asked_row, degree_row, tiles, partial, own = ins
    base, scale = outs
    for g in range(own.pieces):
        for source in (tiles, partial, own):
            source.start(g)
    row_blocks, most = base.held.shape[0] // EDGE, tiles.held.shape[1]
    padded, asked, degrees = padded.all(), asked_row.all()[0:1], degree_row.all()[0:1]
    for g in range(own.pieces):
        for source in (tiles, partial, own):
            source.wait(g)
        for b in range(g * GROUP, (g + 1) * GROUP):
            at = slice(b * EDGE, (b + 1) * EDGE)
            total = partial.held[at, :] + far_product(
                count[b], column, b, tiles.held, padded, row_blocks
            )
            weights = jnp.zeros((EDGE, EDGE), F32)
            for t in range(most):
                used = jnp.where(t < count[b], 1.0, 0.0)
                weights += tiles.held[b, t].astype(F32) * used
            hit = iota((EDGE, asked.shape[1]), 0) + b * EDGE == asked
            given = jnp.where(hit, degrees, 0.0)
            for k in range(asked.shape[1] // EDGE):
                weights += given[:, k * EDGE : (k + 1) * EDGE]
            degree = jnp.sum(weights, axis=1, keepdims=True)
            factor = jnp.broadcast_to(1.0 / (1.0 + degree), (EDGE, EDGE))
            scale.held[at, :] = factor
            base.held[at, :] = own.held[at, :] + total * jnp.concatenate([factor, factor], axis=1)
        base.start(g)
    scale.start()


def far(tile_count, tile_column, tiles, padded, partial, own, asked_row, degree_row):
    masters, width = own.shape
    n = masters // EDGE // GROUP
    return run(
        far_kernel,
        (tile_count, tile_column),
        (
            (padded, 1),
            (asked_row, 1),
            (degree_row, 1),
            (tiles, groups(tiles)),
            (partial, groups(tiles)),
            (own, n),
        ),
        ((struct(masters, width, dtype=F32), n, 0), (struct(masters, EDGE, dtype=F32), 1, 0)),
        flops=5e9,
    )


def turn_kernel(scalars, ins, outs):
    asked_row, back, base, scale, cotangent, asked_column = ins
    mixed, low, spread, send = outs
    for p in range(base.pieces):
        for source in (base, scale, cotangent):
            source.start(p)
    asked, back = asked_row.all()[0:1], back.all()
    step = 512
    for g in range(base.held.shape[0] // step):
        if g * step % base.size == 0:
            for source in (base, scale, cotangent):
                source.wait(g * step // base.size)
        at = slice(g * step, (g + 1) * step)
        both = jnp.concatenate([scale.held[at, :], scale.held[at, :]], axis=1)
        added = dot(pick_rows(step, g * step, asked), back[...])
        u = base.held[at, :] + added * both
        square = u * u
        bend = jnp.tanh(u * (ROOT + (ROOT * CUBIC) * square))
        half = 0.5 + 0.5 * bend
        mixed.held[at, :] = (u * half).astype(BF16)
        slope = half * (1.0 + u * (1.0 - bend) * (ROOT + (3.0 * ROOT * CUBIC) * square))
        d_pre = cotangent.held[at, :].astype(F32) * slope
        low.held[at, :] = d_pre.astype(BF16)
        spread.held[at, :] = (d_pre * both).astype(BF16)
    for out in (spread, low, mixed):
        out.start()
    gather(spread.held, asked_column.all(), send.held)


def turn(base, scale, cotangent, back, asked_row, asked_column):
    masters, width = base.shape
    return run(
        turn_kernel,
        (),
        (
            (asked_row, 1),
            (back, 1),
            (base, 2),
            (scale, 2),
            (cotangent, 2),
            (asked_column, 1),
        ),
        ((struct(masters, width), 1, 0),) * 3 + ((struct(*back.shape), 1, 0),),
        flops=3e9,
    )


def add_back(n, column, b, tiles, values, total, low):
    blocks = total.shape[0] - 1
    for i in range(0, tiles.shape[1], 4):
        right = jnp.concatenate([tiles[b, i + k] for k in range(4)], axis=1)
        product = dot(values, right)
        for k in range(4):
            c = column[b, i + k] - low
            c = jnp.where((i + k < n) & (c >= 0) & (c < blocks), c, blocks)
            total[c] += product[:, k * EDGE : (k + 1) * EDGE]


def back_near_kernel(scalars, ins, outs):
    count, column = scalars
    values, tiles = ins
    (total,) = outs
    blocks = values.held.shape[0] // EDGE
    for g in range(blocks // GROUP):
        tiles.start(g)
    total.held[...] = jnp.zeros(total.held.shape, F32)
    values = values.all()
    for g in range(blocks // GROUP):
        tiles.wait(g)

        def body(b, carry):
            turned = jnp.transpose(values[block(b), :].astype(F32)).astype(BF16)
            add_back(count[b], column, b, tiles.held, turned, total.held, 0)
            return carry

        lax.fori_loop(g * GROUP, (g + 1) * GROUP, body, 0)


def back_near(tile_count, tile_column, values, tiles):
    row_blocks, width = tiles.shape[0], values.shape[1]
    (total,) = run(
        back_near_kernel,
        (tile_count, tile_column),
        ((values, 1), (tiles, groups(tiles))),
        ((struct(row_blocks, width, EDGE, dtype=F32), 1, 1),),
        flops=5e9,
    )
    return total


def mirror_back_kernel(scalars, ins, outs, total, rows, sem):
    count, column = scalars
    arrived, slot_column, tiles, partial, slot_row = ins
    send, turned = outs
    blocks = turned.held.shape[0]
    first = tiles.held.shape[0] - blocks
    last = tiles.pieces - 1
    tiles.start(last)
    copy = pltpu.make_async_copy(partial.at[pl.ds(first, blocks)], total.at[pl.ds(0, blocks)], sem)
    copy.start()
    pick = pick_columns(slot_column.all()[...], 0, arrived.held.shape[0])
    slab = dot(pick, arrived.all()[...])
    for b in range(blocks):
        turned.held[b] = jnp.transpose(slab[b * EDGE : (b + 1) * EDGE]).astype(BF16)
    turned.start()
    total[blocks] = jnp.zeros(total.shape[1:], F32)
    copy.wait()
    tiles.wait(last)
    for b in range(blocks):
        add_back(count[first + b], column, first + b, tiles.held, turned.held[b], total, first)
    for c in range(blocks):
        rows[c * EDGE : (c + 1) * EDGE, :] = jnp.transpose(total[c]).astype(BF16)
    slots = send.held.shape[0]
    send.held[...] = dot(pick_rows(slots, 0, slot_row.all()[...]), rows[...]).astype(BF16)


def mirror_back(tile_count, tile_column, arrived, slot_column, slot_row, partial, tiles):
    slots, width = arrived.shape
    mirrors = slot_row.shape[1]
    blocks = mirrors // EDGE
    return run(
        mirror_back_kernel,
        (tile_count, tile_column),
        ((arrived, 1), (slot_column, 1), (tiles, groups(tiles)), (partial, 0), (slot_row, 1)),
        ((struct(slots, width), 1, 0), (struct(blocks, width, EDGE), 1, 0)),
        (
            pltpu.VMEM((blocks + 1, width, EDGE), F32),
            pltpu.VMEM((mirrors, width), BF16),
            pltpu.SemaphoreType.DMA,
        ),
        flops=2e9,
    )


def back_far_kernel(scalars, ins, outs, sem):
    count, column = scalars
    turned, partial, tiles = ins
    (total,) = outs
    blocks = turned.held.shape[0]
    masters = total.held.shape[0] - 1
    copy = pltpu.make_async_copy(partial.at[pl.ds(0, masters)], total.held.at[pl.ds(0, masters)], sem)
    copy.start()
    tiles.start(tiles.pieces - 1)
    total.held[masters] = jnp.zeros(total.held.shape[1:], F32)
    turned.all()
    copy.wait()
    tiles.wait(tiles.pieces - 1)

    def body(b, carry):
        add_back(count[masters + b], column, masters + b, tiles.held, turned.held[b], total.held, 0)
        return carry

    lax.fori_loop(0, blocks, body, 0)


def back_far(tile_count, tile_column, tiles, turned, partial):
    blocks, width = turned.shape[:2]
    (total,) = run(
        back_far_kernel,
        (tile_count, tile_column),
        ((turned, 1), (partial, 0), (tiles, groups(tiles))),
        ((struct(tiles.shape[0] - blocks, width, EDGE, dtype=F32), 1, 1),),
        (pltpu.SemaphoreType.DMA,),
        flops=3e9,
    )
    return total


def finish_kernel(scalars, ins, outs):
    (core,) = scalars
    back, asked_column, partial, features, grad_self = ins
    turned, keep, give = outs
    width, masters = turned.held.shape
    inputs = features.held.shape[1]
    step = 512
    flipped = jnp.transpose(back.all()[...].astype(F32)).astype(BF16)
    asked, partial = asked_column.all(), partial.all()
    for g in range(masters // step):
        own = []
        for b in range(g * step // EDGE, (g + 1) * step // EDGE):
            own.append(partial[b])
        added = dot(flipped, pick_columns(asked[...], g * step, step))
        turned.held[:, g * step : (g + 1) * step] = (
            jnp.concatenate(own, axis=1) + added
        ).astype(BF16)
    turned.start()
    total = dot(turned.held[...], features.all()[...])
    grad_self = grad_self.all()
    for h in range(width // EDGE):
        lines = pl.ds(h * inputs, inputs)
        first = grad_self[:, h * EDGE : (h + 1) * EDGE].astype(F32)
        second = jnp.transpose(total[h * EDGE : (h + 1) * EDGE, :])
        keep.held[lines, :] = jnp.where(core[0] == 0, first, second)
        give.held[lines, :] = jnp.where(core[0] == 0, second, first).astype(BF16)


def finish(core, partial, back, asked_column, features, grad_self):
    width = back.shape[1]
    masters, inputs = features.shape
    lines = inputs * width // EDGE
    return run(
        finish_kernel,
        (core,),
        (
            (back, 1),
            (asked_column, 1),
            (partial, 1),
            (features, 1),
            (grad_self, 1),
        ),
        (
            (struct(width, masters), 1, 0),
            (struct(lines, EDGE, dtype=F32), 1, 0),
            (struct(lines, EDGE), 1, 0),
        ),
        flops=3e9,
    )


def input_grads_kernel(scalars, ins, outs):
    low, turned, w_self, w_neigh = ins
    (out,) = outs
    step = out.size
    own, other, low, turned = w_self.all(), w_neigh.all(), low.all(), turned.all()
    for g in range(out.pieces):
        at = slice(g * step, (g + 1) * step)
        d_projected = jnp.transpose(turned[:, at].astype(F32)).astype(BF16)
        value = dot(low[at, :], own[...], 1, 1) + dot(d_projected, other[...], 1, 1)
        out.held[at, :] = value.astype(BF16)
        out.start(g)


def input_grads(low, turned, w_self, w_neigh):
    masters, inputs = low.shape[0], w_self.shape[0]
    (out,) = run(
        input_grads_kernel,
        (),
        ((low, 1), (turned, 1), (w_self, 1), (w_neigh, 1)),
        ((struct(masters, inputs), 2, 0),),
        flops=3e9,
    )
    return out


def share_kernel(parts, out):
    share = jnp.sum(parts[...].astype(F32), axis=0, keepdims=True).astype(BF16)
    out[...] = jnp.broadcast_to(share, out.shape)


def share_out(parts):
    return pl.pallas_call(
        share_kernel,
        out_shape=struct(*parts.shape),
        compiler_params=params(),
        cost_estimate=cost(1e8),
    )(parts)


def unpack_kernel(core, mine, other, first, second):
    inputs = first.shape[0]
    for h in range(2):
        lines, lanes = pl.ds(h * inputs, inputs), pl.ds(h * EDGE, EDGE)
        a, b = mine[lines, :].astype(F32), other[lines, :].astype(F32)
        first[:, lanes] = jnp.where(core[0] == 0, a, b)
        second[:, lanes] = jnp.where(core[0] == 0, b, a)


def unpack(core, mine, other, inputs, width):
    smem, vmem = pl.BlockSpec(memory_space=pltpu.SMEM), pl.BlockSpec(memory_space=pltpu.VMEM)
    return pl.pallas_call(
        unpack_kernel,
        in_specs=[smem, vmem, vmem],
        out_specs=[vmem, vmem],
        out_shape=[struct(inputs, width, dtype=F32)] * 2,
        compiler_params=params(),
        cost_estimate=cost(1e8),
    )(core, mine, other)


def exchange(buffer, axes=EVERY):
    parts = lax.axis_size(axes)
    moved = lax.all_to_all(
        buffer.reshape(parts, buffer.shape[0] // parts, buffer.shape[1]),
        axes,
        split_axis=0,
        concat_axis=0,
        tiled=True,
    )
    return moved.reshape(buffer.shape)


def to_other_core(value):
    return lax.ppermute(value, "core", [(0, 1), (1, 0)])


def on_device(
    features,
    w_self,
    w_neigh,
    mirror_master_part,
    mirror_row,
    tile_count,
    tile_column,
    tile_weight,
    cotangent,
):
    inputs, width = w_neigh.shape
    parts = lax.axis_size(EVERY)
    core = lax.axis_index("core").astype(I32).reshape(1)
    slots = SLOTS * parts
    peer = mirror_master_part[:, 0]
    ask, slot_row, slot_column = place(tile_count, peer, mirror_row, tile_weight, parts)
    asked = exchange(ask)
    tiles = tile_weight
    projected = jnp.dot(features, w_neigh, preferred_element_type=F32).astype(BF16)
    own = jnp.dot(features, w_self, preferred_element_type=F32)
    rows, asked_column = fetch(asked, projected, slots)
    arrived = exchange(rows)
    partial, asked_row, degree_row = near(
        tile_count, tile_column, asked, asked_column, projected, tiles
    )
    send, padded = mirror_out(
        tile_count, tile_column, arrived, slot_column, slot_row, partial, tiles
    )
    back = exchange(send)
    base, scale = far(
        tile_count, tile_column, tiles, padded, partial, own, asked_row, degree_row
    )
    mixed, low, spread, send = turn(base, scale, cotangent, back, asked_row, asked_column)
    arrived = exchange(send)
    partial = back_near(tile_count, tile_column, spread, tiles)
    grad_self = lax.dot_general(
        features, low, (((0,), (0,)), ((), ())), preferred_element_type=F32
    ).astype(BF16)
    send, turned = mirror_back(
        tile_count, tile_column, arrived, slot_column, slot_row, partial, tiles
    )
    back = exchange(send)
    partial = back_far(tile_count, tile_column, tiles, turned, partial)
    d_projected, keep, give = finish(core, partial, back, asked_column, features, grad_self)
    pair = (keep + to_other_core(give).astype(F32)).astype(BF16)
    same = ("chip", "local")
    shares = exchange(pair, same).reshape(lax.axis_size(same), -1, EDGE)
    grad_features = input_grads(low, d_projected, w_self, w_neigh)
    shares, grad_features = lax.optimization_barrier((shares, grad_features))
    mine = exchange(share_out(shares).reshape(pair.shape), same)
    grad_self, grad_neigh = unpack(core, mine, to_other_core(mine), inputs, width)
    return (mixed, grad_features, grad_self, grad_neigh)


def solution(mesh):
    machine, local = mesh.devices.shape
    devices = mesh.devices.reshape(machine // 2, 2, local)
    split, rows = P(EVERY), P(EVERY, None)
    return jax.shard_map(
        on_device,
        mesh=jax.sharding.Mesh(devices, EVERY),
        in_specs=(rows, P(), P(), rows, split, split, rows, P(EVERY, None, None, None), rows),
        out_specs=(rows, rows, P(), P()),
        check_vma=False,
    )
```

```python
import jax
import jax.numpy as jnp
from jax import lax
from jax.experimental import pallas as pl
from jax.experimental.pallas import tpu as pltpu
from jax.sharding import PartitionSpec as P

F32 = jnp.float32
BF16 = jnp.bfloat16
I32 = jnp.int32
EDGE = 128
SLOTS = 8
MIB = 1024 * 1024
VMEM_BYTES = 60 * MIB
GROUP = 4
ROOT = 0.7978845608028654
CUBIC = 0.044715
EVERY = ("chip", "core", "local")


def dot(a, b, ca=1, cb=0):
    return lax.dot_general(a, b, (((ca,), (cb,)), ((), ())), preferred_element_type=F32)


def iota(shape, dim):
    return lax.broadcasted_iota(I32, shape, dim)


def pick_rows(rows, base, row):
    return jnp.where(iota((rows, row.shape[1]), 0) + base == row, 1.0, 0.0).astype(BF16)


def pick_columns(column, base, columns):
    lane = iota(column.shape, 1) + base
    parts = [
        jnp.where(column == lane + EDGE * g, 1.0, 0.0).astype(BF16) for g in range(columns // EDGE)
    ]
    return jnp.concatenate(parts, axis=1)


def struct(*shape, dtype=BF16):
    return jax.ShapeDtypeStruct(shape, dtype)


class Moved:
    def __init__(self, far, held, sems, pieces, inward):
        self.far, self.held, self.sems, self.pieces, self.inward = far, held, sems, pieces, inward
        self.size = far.shape[0] // pieces
        self.started, self.waited = False, False

    def rows(self, p):
        return slice(p * self.size, (p + 1) * self.size)

    def copy(self, p):
        at = pl.ds(p * self.size, self.size)
        ends = self.far.at[at], self.held.at[at]
        return pltpu.make_async_copy(*(ends if self.inward else ends[::-1]), self.sems.at[p])

    def start(self, p=0):
        self.started = True
        self.copy(p).start()

    def wait(self, p=0):
        self.copy(p).wait()

    def all(self):
        if not self.waited:
            for p in range(self.pieces):
                self.wait(p)
        self.waited = True
        return self.held


def run(kernel, scalars, ins, outs, scratch=(), flops=1e9):
    ins, outs = list(ins), list(outs)
    n, m = len(ins), len(outs)
    own = [k for k in range(n + m) if (ins + outs)[k][1]]

    def body(*refs):
        scalar_refs, refs = refs[: len(scalars)], refs[len(scalars) :]
        far, refs = list(refs[: n + m]), refs[n + m :]
        held, sems, rest = refs[: len(own)], refs[len(own) : 2 * len(own)], refs[2 * len(own) :]
        for at, k in enumerate(own):
            far[k] = Moved(far[k], held[at], sems[at], (ins + outs)[k][1], k < n)
            if k < n and ins[k][1] == 1:
                far[k].start()
        kernel(scalar_refs, far[:n], far[n:], *rest)
        results = [far[k] for k in own if k >= n]
        for out in results:
            if not out.started:
                for p in range(out.pieces):
                    out.start(p)
        for out in results:
            out.all()

    def place_of(k):
        shape = ins[k][0] if k < n else outs[k - n][0]
        spare = 0 if k < n else outs[k - n][2]
        return pltpu.VMEM((shape.shape[0] + spare, *shape.shape[1:]), shape.dtype)

    smem, any_space = pl.BlockSpec(memory_space=pltpu.SMEM), pl.BlockSpec(memory_space=pl.ANY)
    return pl.pallas_call(
        body,
        in_specs=[smem] * len(scalars) + [any_space] * n,
        out_specs=[any_space] * m,
        out_shape=[out[0] for out in outs],
        scratch_shapes=[place_of(k) for k in own]
        + [pltpu.SemaphoreType.DMA(((ins + outs)[k][1],)) for k in own]
        + list(scratch),
        compiler_params=params(),
        cost_estimate=cost(flops),
    )(*scalars, *[x for x, _ in ins])


def params():
    return pltpu.CompilerParams(vmem_limit_bytes=VMEM_BYTES)


def cost(flops):
    return pl.CostEstimate(flops=int(flops), bytes_accessed=4 * MIB, transcendentals=0)


def groups(tiles):
    return tiles.shape[0] // GROUP


def thirds(value):
    first = value.astype(BF16).astype(F32)
    second = (value - first).astype(BF16).astype(F32)
    return first, second, value - first - second


def used_ones(n, most):
    return jnp.concatenate(
        [jnp.full((EDGE, EDGE), jnp.where(t < n, 1.0, 0.0), F32).astype(BF16) for t in range(most)],
        axis=0,
    )


def place_kernel(scalars, ins, outs):
    (count,) = scalars
    peer, row, tiles = ins
    ask, slot_row, slot_column = outs
    mirrors = peer.held.shape[1]
    parts = ask.held.shape[0]
    blocks, most = mirrors // EDGE, tiles.held.shape[1]
    first = count.shape[0] - blocks
    last = tiles.pieces - 1
    tiles.start(last)
    peer = peer.all()[...]
    member = iota((parts, mirrors), 0) == peer
    chosen = jnp.where(member, 1.0, 0.0).astype(BF16)
    earlier = jnp.where(
        iota((mirrors, mirrors), 0) < iota((mirrors, mirrors), 1), 1.0, 0.0
    ).astype(BF16)
    before = dot(chosen, earlier)
    rank = jnp.sum(jnp.where(member, before, 0.0), axis=0, keepdims=True).astype(I32)
    slot = peer * SLOTS + rank
    slot_row.held[...] = slot
    slot_column.held[...] = jnp.transpose(
        jnp.broadcast_to(slot.astype(F32), (EDGE, mirrors))
    ).astype(I32)
    slot_row.start()
    slot_column.start()
    lane = iota((EDGE, mirrors), 0) - rank
    named = row.all()[...] + 1
    degrees = []
    tiles.wait(last)
    for b in range(first, first + blocks):
        flat = jnp.concatenate([tiles.held[b, t] for t in range(most)], axis=1)
        degrees.append(jnp.transpose(dot(flat, used_ones(count[b], most)))[0:1])
    fields = (named // EDGE).astype(F32), (named % EDGE).astype(F32)
    fields += thirds(jnp.concatenate(degrees, axis=1))
    lines = jnp.zeros((EDGE, mirrors), F32)
    for k, field in enumerate(fields):
        lines = jnp.where(lane == SLOTS * k, field, lines)
    ask.held[...] = dot(chosen, lines.astype(BF16), 1, 1)


def place(tile_count, peer, row, tiles, parts):
    mirrors = row.shape[0]
    return run(
        place_kernel,
        (tile_count,),
        ((peer.reshape(1, mirrors), 1), (row.reshape(1, mirrors), 1), (tiles, groups(tiles))),
        (
            (struct(parts, EDGE, dtype=F32), 1, 0),
            (struct(1, mirrors, dtype=I32), 1, 0),
            (struct(mirrors, EDGE, dtype=I32), 1, 0),
        ),
    )


def slot_lines(arrived, slots):
    parts = arrived.shape[0]
    spread = jnp.where(iota((slots, parts), 0) // SLOTS == iota((slots, parts), 1), 1.0, 0.0)
    return dot(spread.astype(BF16), arrived[...].astype(BF16))


def gather(values, asked_column, rows):
    step = 512
    for g in range(rows.shape[0] // step):
        at = slice(g * step, (g + 1) * step)
        rows[at, :] = dot(pick_columns(asked_column[at, :], 0, values.shape[0]), values[...]).astype(BF16)


def fetch_kernel(scalars, ins, outs):
    arrived, values = ins
    rows, asked_column = outs
    slots = rows.held.shape[0]
    every = slot_lines(arrived.all(), slots)
    lane = iota((slots, EDGE), 1) - iota((slots, EDGE), 0) % SLOTS
    asked = jnp.where(lane == 0, every * EDGE, jnp.where(lane == SLOTS, every, 0.0))
    asked = jnp.sum(asked, axis=1, keepdims=True) - 1.0
    asked_column.held[...] = jnp.broadcast_to(asked, (slots, EDGE)).astype(I32)
    asked_column.start()
    gather(values.all(), asked_column.held, rows.held)


def fetch(arrived, values, slots):
    return run(
        fetch_kernel,
        (),
        ((arrived, 1), (values, 1)),
        ((struct(slots, values.shape[1]), 1, 0), (struct(slots, EDGE, dtype=I32), 1, 0)),
        flops=2e9,
    )


def flat(tiles, rows, columns):
    lines = [jnp.concatenate([tiles[b, c] for c in columns], axis=1) for b in rows]
    return jnp.concatenate(lines, axis=0)


def densify(count, column, tiles, dense, g):
    members = range(g * GROUP, (g + 1) * GROUP)
    last = dense.shape[1] - 1
    longest = count[g * GROUP]
    for b in members:
        longest = jnp.maximum(longest, count[b])

    def body(t, carry):
        for b in members:
            c = jnp.where(t < count[b], column[b, t], last)
            dense[b, c] = dense[b, c] + tiles[b, t]
        return carry

    lax.fori_loop(0, longest, body, 0)


def near_kernel(scalars, ins, outs, dense, far_sems, near_sem):
    count, column = scalars
    values, tiles, arrived, asked_column = ins
    partial, degree, asked_row, degree_row, near, far = outs
    row_blocks = tiles.held.shape[0]
    cut, last = near.shape[1], dense.shape[1] - 1

    def far_copy(g):
        at = pl.ds(g * GROUP, GROUP)
        return pltpu.make_async_copy(dense.at[at, pl.ds(cut, last - cut)], far.at[at], far_sems.at[g])

    near_copy = pltpu.make_async_copy(
        dense.at[pl.ds(row_blocks - GROUP, GROUP), pl.ds(0, cut)], near, near_sem
    )
    for g in range(tiles.pieces):
        tiles.start(g)
    for b in range(row_blocks):
        dense[b] = jnp.zeros(dense.shape[1:], BF16)
    slots = asked_column.held.shape[0]
    asked_row.held[...] = jnp.transpose(asked_column.all()[...].astype(F32))[0:8].astype(I32)
    lane = iota((slots, EDGE), 1) - iota((slots, EDGE), 0) % SLOTS
    mine = (lane == 2 * SLOTS) | (lane == 3 * SLOTS) | (lane == 4 * SLOTS)
    sums = jnp.sum(jnp.where(mine, slot_lines(arrived.all(), slots), 0.0), axis=1, keepdims=True)
    degree_row.held[...] = jnp.transpose(jnp.broadcast_to(sums, (slots, EDGE)))[0:8]
    values = values.all()
    for g in range(tiles.pieces):
        tiles.wait(g)
        densify(count, column, tiles.held, dense, g)
        far_copy(g).start()
        if g == tiles.pieces - 1:
            near_copy.start()
        for b in range(g * GROUP, (g + 1) * GROUP):
            at = slice(b * EDGE, (b + 1) * EDGE)
            partial.held[at, :] = dot(flat(dense, (b,), range(cut)), values[...])
            if g < degree.pieces:
                weights = dense[b, 0].astype(F32)
                for c in range(1, last):
                    weights += dense[b, c].astype(F32)
                total = jnp.sum(weights, axis=1, keepdims=True)
                degree.held[at, :] = jnp.broadcast_to(total, (EDGE, EDGE))
        partial.start(g)
        if g < degree.pieces:
            degree.start(g)
    for g in range(tiles.pieces):
        far_copy(g).wait()
    near_copy.wait()


def near(tile_count, tile_column, tiles, values, arrived, asked_column):
    rows, width = values.shape
    slots, row_blocks = asked_column.shape[0], tiles.shape[0]
    masters = rows // EDGE
    sems = pltpu.SemaphoreType.DMA((groups(tiles),))
    return run(
        near_kernel,
        (tile_count, tile_column),
        ((values, 1), (tiles, groups(tiles)), (arrived, 1), (asked_column, 1)),
        (
            (struct(row_blocks * EDGE, width, dtype=F32), groups(tiles), 0),
            (struct(rows, EDGE, dtype=F32), masters // GROUP, 0),
            (struct(8, slots, dtype=I32), 1, 0),
            (struct(8, slots, dtype=F32), 1, 0),
            (struct(GROUP, masters, EDGE, EDGE), 0, 0),
            (struct(row_blocks, row_blocks - masters, EDGE, EDGE), 0, 0),
        ),
        (
            pltpu.VMEM((row_blocks, row_blocks + 1, EDGE, EDGE), BF16),
            sems,
            pltpu.SemaphoreType.DMA,
        ),
        flops=5e9,
    )


def mirror_out_kernel(scalars, ins, outs):
    arrived, slot_column, partial, tiles, slot_row = ins
    send, slab = outs
    last = tiles.pieces - 1
    tiles.start(last)
    partial.start(last)
    pick = pick_columns(slot_column.all()[...], 0, arrived.held.shape[0])
    slab.held[...] = dot(pick, arrived.all()[...]).astype(BF16)
    slab.start()
    tiles.wait(last)
    blocks = range(tiles.held.shape[1])
    left = flat(tiles.held, [last * GROUP + b for b in blocks], blocks)
    more = dot(left, slab.held[...])
    partial.wait(last)
    total = (partial.held[partial.rows(last), :] + more).astype(BF16)
    slots = send.held.shape[0]
    send.held[...] = dot(pick_rows(slots, 0, slot_row.all()[...]), total).astype(BF16)


def mirror_out(arrived, slot_column, slot_row, partial, tiles):
    slots, width = arrived.shape
    mirrors = slot_row.shape[1]
    return run(
        mirror_out_kernel,
        (),
        (
            (arrived, 1),
            (slot_column, 1),
            (partial, groups(tiles)),
            (tiles, groups(tiles)),
            (slot_row, 1),
        ),
        ((struct(slots, width), 1, 0), (struct(mirrors, width), 1, 0)),
        flops=2e9,
    )


def far_kernel(scalars, ins, outs):
    slab, asked_row, degree_row, tiles, partial, own, degree = ins
    base, scale = outs
    for g in range(own.pieces):
        for source in (tiles, partial, own, degree):
            source.start(g)
    slab, asked, degrees = slab.all(), asked_row.all()[0:1], degree_row.all()[0:1]
    rows = own.size
    for g in range(own.pieces):
        for source in (tiles, partial, own, degree):
            source.wait(g)
        at = own.rows(g)
        left = flat(tiles.held, range(g * GROUP, (g + 1) * GROUP), range(tiles.held.shape[1]))
        total = partial.held[at, :] + dot(left, slab[...])
        hit = iota((rows, asked.shape[1]), 0) + g * rows == asked
        more = jnp.sum(jnp.where(hit, degrees, 0.0), axis=1, keepdims=True)
        factor = 1.0 / (1.0 + (degree.held[at, :] + more))
        scale.held[at, :] = factor
        base.held[at, :] = own.held[at, :] + total * jnp.concatenate([factor, factor], axis=1)
        base.start(g)
    scale.start()


def far(tiles, slab, partial, degree, own, asked_row, degree_row):
    masters, width = own.shape
    n = masters // EDGE // GROUP
    return run(
        far_kernel,
        (),
        (
            (slab, 1),
            (asked_row, 1),
            (degree_row, 1),
            (tiles, groups(tiles)),
            (partial, groups(tiles)),
            (own, n),
            (degree, n),
        ),
        ((struct(masters, width, dtype=F32), n, 0), (struct(masters, EDGE, dtype=F32), 1, 0)),
        flops=5e9,
    )


def turn_kernel(scalars, ins, outs):
    asked_row, back, base, scale, cotangent, asked_column = ins
    mixed, low, spread, send = outs
    for p in range(base.pieces):
        for source in (base, scale, cotangent):
            source.start(p)
    asked, back = asked_row.all()[0:1], back.all()
    step = 512
    for g in range(base.held.shape[0] // step):
        if g * step % base.size == 0:
            for source in (base, scale, cotangent):
                source.wait(g * step // base.size)
        at = slice(g * step, (g + 1) * step)
        both = jnp.concatenate([scale.held[at, :], scale.held[at, :]], axis=1)
        added = dot(pick_rows(step, g * step, asked), back[...])
        u = base.held[at, :] + added * both
        square = u * u
        bend = jnp.tanh(u * (ROOT + (ROOT * CUBIC) * square))
        half = 0.5 + 0.5 * bend
        mixed.held[at, :] = (u * half).astype(BF16)
        slope = half * (1.0 + u * (1.0 - bend) * (ROOT + (3.0 * ROOT * CUBIC) * square))
        d_pre = cotangent.held[at, :].astype(F32) * slope
        low.held[at, :] = d_pre.astype(BF16)
        spread.held[at, :] = (d_pre * both).astype(BF16)
    for out in (spread, low, mixed):
        out.start()
    gather(spread.held, asked_column.all(), send.held)


def turn(base, scale, cotangent, back, asked_row, asked_column):
    masters, width = base.shape
    return run(
        turn_kernel,
        (),
        (
            (asked_row, 1),
            (back, 1),
            (base, 2),
            (scale, 2),
            (cotangent, 2),
            (asked_column, 1),
        ),
        ((struct(masters, width), 1, 0),) * 3 + ((struct(*back.shape), 1, 0),),
        flops=3e9,
    )


def put_blocks(total, first, value):
    for k in range(value.shape[1] // EDGE):
        total[first + k] = value[:, k * EDGE : (k + 1) * EDGE]


def back_near_kernel(scalars, ins, outs, dense):
    count, column = scalars
    tiles, values = ins
    (total,) = outs
    rows = dense.shape[0]
    for g in range(rows // GROUP):
        tiles.start(g)
    for b in range(rows):
        dense[b] = jnp.zeros(dense.shape[1:], BF16)
    turned = jnp.transpose(values.all()[...].astype(F32)).astype(BF16)
    for g in range(rows // GROUP):
        tiles.wait(g)
        densify(count, column, tiles.held, dense, g)
    for g in range(total.pieces):
        right = flat(dense, range(rows), range(g * GROUP, (g + 1) * GROUP))
        put_blocks(total.held, g * GROUP, dot(turned, right))
        total.start(g)


def back_near(tile_count, tile_column, tiles, values):
    row_blocks, width = tiles.shape[0], values.shape[1]
    n = groups(tiles)
    (total,) = run(
        back_near_kernel,
        (tile_count, tile_column),
        ((tiles, n), (values, 1)),
        ((struct(row_blocks, width, EDGE, dtype=F32), n, 0),),
        (pltpu.VMEM((values.shape[0] // EDGE, row_blocks + 1, EDGE, EDGE), BF16),),
        flops=5e9,
    )
    return total


def mirror_back_kernel(scalars, ins, outs):
    arrived, slot_column, tiles, partial, slot_row = ins
    send, turned = outs
    last = tiles.pieces - 1
    tiles.start(last)
    partial.start(last)
    pick = pick_columns(slot_column.all()[...], 0, arrived.held.shape[0])
    turned.held[...] = jnp.transpose(dot(pick, arrived.all()[...])).astype(BF16)
    turned.start()
    tiles.wait(last)
    blocks = range(tiles.held.shape[1])
    right = flat(tiles.held, [last * GROUP + b for b in blocks], blocks)
    more = dot(turned.held[...], right)
    partial.wait(last)
    own = jnp.concatenate([partial.held[last * GROUP + c] for c in blocks], axis=1)
    rows = jnp.transpose(own + more).astype(BF16)
    slots = send.held.shape[0]
    send.held[...] = dot(pick_rows(slots, 0, slot_row.all()[...]), rows).astype(BF16)


def mirror_back(arrived, slot_column, slot_row, partial, tiles):
    slots, width = arrived.shape
    mirrors = slot_row.shape[1]
    return run(
        mirror_back_kernel,
        (),
        (
            (arrived, 1),
            (slot_column, 1),
            (tiles, groups(tiles)),
            (partial, groups(tiles)),
            (slot_row, 1),
        ),
        ((struct(slots, width), 1, 0), (struct(width, mirrors), 1, 0)),
        flops=2e9,
    )


def back_far_kernel(scalars, ins, outs):
    tiles, turned, partial = ins
    (total,) = outs
    for g in range(total.pieces):
        partial.start(g)
    tiles, turned = tiles.all(), turned.all()
    for g in range(total.pieces):
        columns = range(g * GROUP, (g + 1) * GROUP)
        right = flat(tiles, range(tiles.shape[0]), columns)
        partial.wait(g)
        own = jnp.concatenate([partial.held[c] for c in columns], axis=1)
        put_blocks(total.held, g * GROUP, own + dot(turned[...], right))
        total.start(g)


def back_far(tiles, turned, partial):
    width, masters = turned.shape[0], tiles.shape[1]
    (total,) = run(
        back_far_kernel,
        (),
        ((tiles, 1), (turned, 1), (partial, groups(partial))),
        ((struct(masters, width, EDGE, dtype=F32), masters // GROUP, 0),),
        flops=3e9,
    )
    return total


def finish_kernel(scalars, ins, outs):
    (core,) = scalars
    back, asked_column, partial, features, grad_self = ins
    turned, keep, give = outs
    width, masters = turned.held.shape
    inputs = features.held.shape[1]
    step = 512
    flipped = jnp.transpose(back.all()[...].astype(F32)).astype(BF16)
    asked, partial = asked_column.all(), partial.all()
    for g in range(masters // step):
        own = []
        for b in range(g * step // EDGE, (g + 1) * step // EDGE):
            own.append(partial[b])
        added = dot(flipped, pick_columns(asked[...], g * step, step))
        turned.held[:, g * step : (g + 1) * step] = (
            jnp.concatenate(own, axis=1) + added
        ).astype(BF16)
    turned.start()
    total = dot(turned.held[...], features.all()[...])
    grad_self = grad_self.all()
    for h in range(width // EDGE):
        lines = pl.ds(h * inputs, inputs)
        first = grad_self[:, h * EDGE : (h + 1) * EDGE].astype(F32)
        second = jnp.transpose(total[h * EDGE : (h + 1) * EDGE, :])
        keep.held[lines, :] = jnp.where(core[0] == 0, first, second)
        give.held[lines, :] = jnp.where(core[0] == 0, second, first).astype(BF16)


def finish(core, partial, back, asked_column, features, grad_self):
    width = back.shape[1]
    masters, inputs = features.shape
    lines = inputs * width // EDGE
    return run(
        finish_kernel,
        (core,),
        (
            (back, 1),
            (asked_column, 1),
            (partial, 1),
            (features, 1),
            (grad_self, 1),
        ),
        (
            (struct(width, masters), 1, 0),
            (struct(lines, EDGE, dtype=F32), 1, 0),
            (struct(lines, EDGE), 1, 0),
        ),
        flops=3e9,
    )


def input_grads_kernel(scalars, ins, outs):
    low, turned, w_self, w_neigh = ins
    (out,) = outs
    step = out.size
    own, other, low, turned = w_self.all(), w_neigh.all(), low.all(), turned.all()
    for g in range(out.pieces):
        at = slice(g * step, (g + 1) * step)
        d_projected = jnp.transpose(turned[:, at].astype(F32)).astype(BF16)
        value = dot(low[at, :], own[...], 1, 1) + dot(d_projected, other[...], 1, 1)
        out.held[at, :] = value.astype(BF16)
        out.start(g)


def input_grads(low, turned, w_self, w_neigh):
    masters, inputs = low.shape[0], w_self.shape[0]
    (out,) = run(
        input_grads_kernel,
        (),
        ((low, 1), (turned, 1), (w_self, 1), (w_neigh, 1)),
        ((struct(masters, inputs), 2, 0),),
        flops=3e9,
    )
    return out


def share_kernel(parts, out):
    share = jnp.sum(parts[...].astype(F32), axis=0, keepdims=True).astype(BF16)
    out[...] = jnp.broadcast_to(share, out.shape)


def share_out(parts):
    return pl.pallas_call(
        share_kernel,
        out_shape=struct(*parts.shape),
        compiler_params=params(),
        cost_estimate=cost(1e8),
    )(parts)


def unpack_kernel(core, mine, other, first, second):
    inputs = first.shape[0]
    for h in range(2):
        lines, lanes = pl.ds(h * inputs, inputs), pl.ds(h * EDGE, EDGE)
        a, b = mine[lines, :].astype(F32), other[lines, :].astype(F32)
        first[:, lanes] = jnp.where(core[0] == 0, a, b)
        second[:, lanes] = jnp.where(core[0] == 0, b, a)


def unpack(core, mine, other, inputs, width):
    smem, vmem = pl.BlockSpec(memory_space=pltpu.SMEM), pl.BlockSpec(memory_space=pltpu.VMEM)
    return pl.pallas_call(
        unpack_kernel,
        in_specs=[smem, vmem, vmem],
        out_specs=[vmem, vmem],
        out_shape=[struct(inputs, width, dtype=F32)] * 2,
        compiler_params=params(),
        cost_estimate=cost(1e8),
    )(core, mine, other)


def exchange(buffer, axes=EVERY):
    parts = lax.axis_size(axes)
    moved = lax.all_to_all(
        buffer.reshape(parts, buffer.shape[0] // parts, buffer.shape[1]),
        axes,
        split_axis=0,
        concat_axis=0,
        tiled=True,
    )
    return moved.reshape(buffer.shape)


def to_other_core(value):
    return lax.ppermute(value, "core", [(0, 1), (1, 0)])


def on_device(
    features,
    w_self,
    w_neigh,
    mirror_master_part,
    mirror_row,
    tile_count,
    tile_column,
    tile_weight,
    cotangent,
):
    inputs, width = w_neigh.shape
    parts = lax.axis_size(EVERY)
    core = lax.axis_index("core").astype(I32).reshape(1)
    slots = SLOTS * parts
    peer = mirror_master_part[:, 0]
    ask, slot_row, slot_column = place(tile_count, peer, mirror_row, tile_weight, parts)
    asked = exchange(ask)
    projected = jnp.dot(features, w_neigh, preferred_element_type=F32).astype(BF16)
    own = jnp.dot(features, w_self, preferred_element_type=F32)
    rows, asked_column = fetch(asked, projected, slots)
    arrived = exchange(rows)
    partial, degree, asked_row, degree_row, near_tiles, far_tiles = near(
        tile_count, tile_column, tile_weight, projected, asked, asked_column
    )
    send, slab = mirror_out(arrived, slot_column, slot_row, partial, far_tiles)
    back = exchange(send)
    base, scale = far(far_tiles, slab, partial, degree, own, asked_row, degree_row)
    mixed, low, spread, send = turn(base, scale, cotangent, back, asked_row, asked_column)
    arrived = exchange(send)
    partial = back_near(tile_count, tile_column, tile_weight, spread)
    grad_self = lax.dot_general(
        features, low, (((0,), (0,)), ((), ())), preferred_element_type=F32
    ).astype(BF16)
    send, turned = mirror_back(arrived, slot_column, slot_row, partial, far_tiles)
    back = exchange(send)
    partial = back_far(near_tiles, turned, partial)
    d_projected, keep, give = finish(core, partial, back, asked_column, features, grad_self)
    pair = (keep + to_other_core(give).astype(F32)).astype(BF16)
    same = ("chip", "local")
    shares = exchange(pair, same).reshape(lax.axis_size(same), -1, EDGE)
    grad_features = input_grads(low, d_projected, w_self, w_neigh)
    shares, grad_features = lax.optimization_barrier((shares, grad_features))
    mine = exchange(share_out(shares).reshape(pair.shape), same)
    grad_self, grad_neigh = unpack(core, mine, to_other_core(mine), inputs, width)
    return (mixed, grad_features, grad_self, grad_neigh)


def solution(mesh):
    machine, local = mesh.devices.shape
    devices = mesh.devices.reshape(machine // 2, 2, local)
    split, rows = P(EVERY), P(EVERY, None)
    return jax.shard_map(
        on_device,
        mesh=jax.sharding.Mesh(devices, EVERY),
        in_specs=(rows, P(), P(), rows, split, split, rows, P(EVERY, None, None, None), rows),
        out_specs=(rows, rows, P(), P()),
        check_vma=False,
    )
```

```python
import jax
import jax.numpy as jnp
from jax import lax
from jax.experimental import pallas as pl
from jax.experimental.pallas import tpu as pltpu
from jax.sharding import PartitionSpec as P

F32 = jnp.float32
BF16 = jnp.bfloat16
I32 = jnp.int32
EDGE = 128
SLOTS = 8
MIB = 1024 * 1024
VMEM_BYTES = 60 * MIB
GROUP = 4
AHEAD = 2
ROOT = 0.7978845608028654
CUBIC = 0.044715
EVERY = ("chip", "core", "local")


def dot(a, b, ca=1, cb=0):
    return lax.dot_general(a, b, (((ca,), (cb,)), ((), ())), preferred_element_type=F32)


def iota(shape, dim):
    return lax.broadcasted_iota(I32, shape, dim)


def pick_rows(rows, base, row):
    return jnp.where(iota((rows, row.shape[1]), 0) + base == row, 1.0, 0.0).astype(BF16)


def pick_columns(column, base, columns):
    lane = iota(column.shape, 1) + base
    parts = [
        jnp.where(column == lane + EDGE * g, 1.0, 0.0).astype(BF16) for g in range(columns // EDGE)
    ]
    return jnp.concatenate(parts, axis=1)


def struct(*shape, dtype=BF16):
    return jax.ShapeDtypeStruct(shape, dtype)


class Moved:
    def __init__(self, far, held, sems, pieces, inward):
        self.far, self.held, self.sems, self.pieces, self.inward = far, held, sems, pieces, inward
        self.size = far.shape[0] // pieces
        self.started, self.waited = False, False

    def rows(self, p):
        return slice(p * self.size, (p + 1) * self.size)

    def copy(self, p):
        at = pl.ds(p * self.size, self.size)
        ends = self.far.at[at], self.held.at[at]
        return pltpu.make_async_copy(*(ends if self.inward else ends[::-1]), self.sems.at[p])

    def start(self, p=0):
        self.started = True
        self.copy(p).start()

    def wait(self, p=0):
        self.copy(p).wait()

    def all(self):
        if not self.waited:
            for p in range(self.pieces):
                self.wait(p)
        self.waited = True
        return self.held


def begin(sources, pieces):
    for g in range(min(AHEAD, pieces)):
        for source in sources:
            source.start(g)


def take(sources, pieces, g):
    for source in sources:
        source.wait(g)
    if g + AHEAD < pieces:
        for source in sources:
            source.start(g + AHEAD)


def run(kernel, scalars, ins, outs, scratch=(), flops=1e9):
    ins, outs = list(ins), list(outs)
    n, m = len(ins), len(outs)
    own = [k for k in range(n + m) if (ins + outs)[k][1]]

    def body(*refs):
        scalar_refs, refs = refs[: len(scalars)], refs[len(scalars) :]
        far, refs = list(refs[: n + m]), refs[n + m :]
        held, sems, rest = refs[: len(own)], refs[len(own) : 2 * len(own)], refs[2 * len(own) :]
        for at, k in enumerate(own):
            far[k] = Moved(far[k], held[at], sems[at], (ins + outs)[k][1], k < n)
            if k < n and ins[k][1] == 1:
                far[k].start()
        kernel(scalar_refs, far[:n], far[n:], *rest)
        results = [far[k] for k in own if k >= n]
        for out in results:
            if not out.started:
                for p in range(out.pieces):
                    out.start(p)
        for out in results:
            out.all()

    def place_of(k):
        shape = ins[k][0] if k < n else outs[k - n][0]
        spare = 0 if k < n else outs[k - n][2]
        return pltpu.VMEM((shape.shape[0] + spare, *shape.shape[1:]), shape.dtype)

    smem, any_space = pl.BlockSpec(memory_space=pltpu.SMEM), pl.BlockSpec(memory_space=pl.ANY)
    return pl.pallas_call(
        body,
        in_specs=[smem] * len(scalars) + [any_space] * n,
        out_specs=[any_space] * m,
        out_shape=[out[0] for out in outs],
        scratch_shapes=[place_of(k) for k in own]
        + [pltpu.SemaphoreType.DMA(((ins + outs)[k][1],)) for k in own]
        + list(scratch),
        compiler_params=params(),
        cost_estimate=cost(flops),
    )(*scalars, *[x for x, _ in ins])


def params(limit=VMEM_BYTES):
    return pltpu.CompilerParams(vmem_limit_bytes=limit)


def cost(flops):
    return pl.CostEstimate(flops=int(flops), bytes_accessed=4 * MIB, transcendentals=0)


def groups(tiles):
    return tiles.shape[0] // GROUP


def thirds(value):
    first = value.astype(BF16).astype(F32)
    second = (value - first).astype(BF16).astype(F32)
    return first, second, value - first - second


def used_ones(n, most):
    return jnp.concatenate(
        [jnp.full((EDGE, EDGE), jnp.where(t < n, 1.0, 0.0), F32).astype(BF16) for t in range(most)],
        axis=0,
    )


def place_kernel(scalars, ins, outs):
    (count,) = scalars
    peer, row, tiles = ins
    ask, slot_row, slot_column = outs
    mirrors = peer.held.shape[1]
    parts = ask.held.shape[0]
    blocks, most = mirrors // EDGE, tiles.held.shape[1]
    first = count.shape[0] - blocks
    last = tiles.pieces - 1
    tiles.start(last)
    peer = peer.all()[...]
    member = iota((parts, mirrors), 0) == peer
    chosen = jnp.where(member, 1.0, 0.0).astype(BF16)
    earlier = jnp.where(
        iota((mirrors, mirrors), 0) < iota((mirrors, mirrors), 1), 1.0, 0.0
    ).astype(BF16)
    before = dot(chosen, earlier)
    rank = jnp.sum(jnp.where(member, before, 0.0), axis=0, keepdims=True).astype(I32)
    slot = peer * SLOTS + rank
    slot_row.held[...] = slot
    slot_column.held[...] = jnp.transpose(
        jnp.broadcast_to(slot.astype(F32), (EDGE, mirrors))
    ).astype(I32)
    slot_row.start()
    slot_column.start()
    lane = iota((EDGE, mirrors), 0) - rank
    named = row.all()[...] + 1
    degrees = []
    tiles.wait(last)
    for b in range(first, first + blocks):
        flat = jnp.concatenate([tiles.held[b, t] for t in range(most)], axis=1)
        degrees.append(jnp.transpose(dot(flat, used_ones(count[b], most)))[0:1])
    fields = (named // EDGE).astype(F32), (named % EDGE).astype(F32)
    fields += thirds(jnp.concatenate(degrees, axis=1))
    lines = jnp.zeros((EDGE, mirrors), F32)
    for k, field in enumerate(fields):
        lines = jnp.where(lane == SLOTS * k, field, lines)
    ask.held[...] = dot(chosen, lines.astype(BF16), 1, 1)


def place(tile_count, peer, row, tiles, parts):
    mirrors = row.shape[0]
    return run(
        place_kernel,
        (tile_count,),
        ((peer.reshape(1, mirrors), 1), (row.reshape(1, mirrors), 1), (tiles, groups(tiles))),
        (
            (struct(parts, EDGE, dtype=F32), 1, 0),
            (struct(1, mirrors, dtype=I32), 1, 0),
            (struct(mirrors, EDGE, dtype=I32), 1, 0),
        ),
    )


def slot_lines(arrived, slots):
    parts = arrived.shape[0]
    spread = jnp.where(iota((slots, parts), 0) // SLOTS == iota((slots, parts), 1), 1.0, 0.0)
    return dot(spread.astype(BF16), arrived[...].astype(BF16))


def gather(values, asked_column, rows):
    step = 512
    for g in range(rows.shape[0] // step):
        at = slice(g * step, (g + 1) * step)
        rows[at, :] = dot(pick_columns(asked_column[at, :], 0, values.shape[0]), values[...]).astype(BF16)


def fetch_kernel(scalars, ins, outs):
    arrived, values = ins
    rows, asked_column = outs
    slots = rows.held.shape[0]
    every = slot_lines(arrived.all(), slots)
    lane = iota((slots, EDGE), 1) - iota((slots, EDGE), 0) % SLOTS
    asked = jnp.where(lane == 0, every * EDGE, jnp.where(lane == SLOTS, every, 0.0))
    asked = jnp.sum(asked, axis=1, keepdims=True) - 1.0
    asked_column.held[...] = jnp.broadcast_to(asked, (slots, EDGE)).astype(I32)
    asked_column.start()
    gather(values.all(), asked_column.held, rows.held)


def fetch(arrived, values, slots):
    return run(
        fetch_kernel,
        (),
        ((arrived, 1), (values, 1)),
        ((struct(slots, values.shape[1]), 1, 0), (struct(slots, EDGE, dtype=I32), 1, 0)),
        flops=2e9,
    )


def flat(tiles, rows, columns):
    lines = [jnp.concatenate([tiles[b, c] for c in columns], axis=1) for b in rows]
    return jnp.concatenate(lines, axis=0)


def densify(count, column, tiles, dense, g, first=0):
    members = range(g * GROUP, (g + 1) * GROUP)
    last = dense.shape[1] - 1
    longest = count[g * GROUP]
    for b in members:
        longest = jnp.maximum(longest, count[b])

    def body(t, carry):
        for b in members:
            c = jnp.where(t < count[b], column[t, b], last)
            dense[b - first, c] = dense[b - first, c] + tiles[b, t]
        return carry

    lax.fori_loop(0, longest, body, 0)


def near_kernel(scalars, ins, outs, dense, far_sems):
    count, column = scalars
    tiles, values = ins
    partial, degree, far = outs
    row_blocks = tiles.held.shape[0]
    last = dense.shape[1] - 1
    cut = last - far.shape[1]

    def far_copy(g):
        at = pl.ds(g * GROUP, GROUP)
        return pltpu.make_async_copy(dense.at[at, pl.ds(cut, last - cut)], far.at[at], far_sems.at[g])

    begin((tiles,), tiles.pieces)
    for b in range(row_blocks):
        dense[b] = jnp.zeros(dense.shape[1:], BF16)
    values = values.all()
    for g in range(tiles.pieces):
        take((tiles,), tiles.pieces, g)
        densify(count, column, tiles.held, dense, g)
        far_copy(g).start()
        for b in range(g * GROUP, (g + 1) * GROUP):
            at = slice(b * EDGE, (b + 1) * EDGE)
            partial.held[at, :] = dot(flat(dense, (b,), range(cut)), values[...])
            if g < degree.pieces:
                weights = dense[b, 0].astype(F32)
                for c in range(1, last):
                    weights += dense[b, c].astype(F32)
                total = jnp.sum(weights, axis=1, keepdims=True)
                degree.held[at, :] = jnp.broadcast_to(total, (EDGE, EDGE))
        partial.start(g)
        if g < degree.pieces:
            degree.start(g)
    for g in range(tiles.pieces):
        far_copy(g).wait()


def near(tile_count, tile_column, tiles, values):
    rows, width = values.shape
    row_blocks = tiles.shape[0]
    masters = rows // EDGE
    return run(
        near_kernel,
        (tile_count, tile_column),
        ((tiles, groups(tiles)), (values, 1)),
        (
            (struct(row_blocks * EDGE, width, dtype=F32), groups(tiles), 0),
            (struct(rows, EDGE, dtype=F32), masters // GROUP, 0),
            (struct(row_blocks, row_blocks - masters, EDGE, EDGE), 0, 0),
        ),
        (
            pltpu.VMEM((row_blocks, row_blocks + 1, EDGE, EDGE), BF16),
            pltpu.SemaphoreType.DMA((groups(tiles),)),
        ),
        flops=5e9,
    )


def mirror_out_kernel(scalars, ins, outs):
    arrived, slot_column, partial, tiles, slot_row = ins
    send, slab = outs
    last = tiles.pieces - 1
    tiles.start(last)
    partial.start(last)
    pick = pick_columns(slot_column.all()[...], 0, arrived.held.shape[0])
    slab.held[...] = dot(pick, arrived.all()[...]).astype(BF16)
    slab.start()
    tiles.wait(last)
    blocks = range(tiles.held.shape[1])
    left = flat(tiles.held, [last * GROUP + b for b in blocks], blocks)
    more = dot(left, slab.held[...])
    partial.wait(last)
    total = (partial.held[partial.rows(last), :] + more).astype(BF16)
    slots = send.held.shape[0]
    send.held[...] = dot(pick_rows(slots, 0, slot_row.all()[...]), total).astype(BF16)


def mirror_out(arrived, slot_column, slot_row, partial, tiles):
    slots, width = arrived.shape
    mirrors = slot_row.shape[1]
    return run(
        mirror_out_kernel,
        (),
        (
            (arrived, 1),
            (slot_column, 1),
            (partial, groups(tiles)),
            (tiles, groups(tiles)),
            (slot_row, 1),
        ),
        ((struct(slots, width), 1, 0), (struct(mirrors, width), 1, 0)),
        flops=2e9,
    )


def far_kernel(scalars, ins, outs):
    slab, arrived, asked_column, tiles, partial, own, degree = ins
    base, scale, asked_row = outs
    sources = (tiles, partial, own, degree)
    begin(sources, own.pieces)
    slots = asked_column.held.shape[0]
    asked = jnp.transpose(asked_column.all()[...].astype(F32))[0:8].astype(I32)
    asked_row.held[...] = asked
    asked_row.start()
    lane = iota((slots, EDGE), 1) - iota((slots, EDGE), 0) % SLOTS
    mine = (lane == 2 * SLOTS) | (lane == 3 * SLOTS) | (lane == 4 * SLOTS)
    sums = jnp.sum(jnp.where(mine, slot_lines(arrived.all(), slots), 0.0), axis=1, keepdims=True)
    degrees = jnp.transpose(jnp.broadcast_to(sums, (slots, EDGE)))[0:1]
    slab = slab.all()
    rows = own.size
    for g in range(own.pieces):
        take(sources, own.pieces, g)
        at = own.rows(g)
        left = flat(tiles.held, range(g * GROUP, (g + 1) * GROUP), range(tiles.held.shape[1]))
        total = partial.held[at, :] + dot(left, slab[...])
        hit = iota((rows, slots), 0) + g * rows == asked[0:1]
        more = jnp.sum(jnp.where(hit, degrees, 0.0), axis=1, keepdims=True)
        factor = 1.0 / (1.0 + (degree.held[at, :] + more))
        scale.held[at, :] = factor
        base.held[at, :] = own.held[at, :] + total * jnp.concatenate([factor, factor], axis=1)
        base.start(g)
    scale.start()


def far(tiles, slab, partial, degree, own, arrived, asked_column):
    masters, width = own.shape
    n = masters // EDGE // GROUP
    return run(
        far_kernel,
        (),
        (
            (slab, 1),
            (arrived, 1),
            (asked_column, 1),
            (tiles, groups(tiles)),
            (partial, groups(tiles)),
            (own, n),
            (degree, n),
        ),
        (
            (struct(masters, width, dtype=F32), n, 0),
            (struct(masters, EDGE, dtype=F32), 1, 0),
            (struct(8, asked_column.shape[0], dtype=I32), 1, 0),
        ),
        flops=5e9,
    )


def turn_kernel(scalars, ins, outs):
    asked_row, back, base, scale, cotangent, asked_column = ins
    mixed, low, spread, send = outs
    for source in (base, scale, cotangent):
        source.start(0)
    asked, back = asked_row.all()[0:1], back.all()
    step = 512
    for g in range(base.held.shape[0] // step):
        if g * step % base.size == 0:
            p = g * step // base.size
            for source in (base, scale, cotangent):
                source.wait(p)
            for source in (base, scale, cotangent, asked_column):
                if p + 1 < source.pieces:
                    source.start(p + 1)
        at = slice(g * step, (g + 1) * step)
        both = jnp.concatenate([scale.held[at, :], scale.held[at, :]], axis=1)
        added = dot(pick_rows(step, g * step, asked), back[...])
        u = base.held[at, :] + added * both
        square = u * u
        bend = jnp.tanh(u * (ROOT + (ROOT * CUBIC) * square))
        half = 0.5 + 0.5 * bend
        mixed.held[at, :] = (u * half).astype(BF16)
        slope = half * (1.0 + u * (1.0 - bend) * (ROOT + (3.0 * ROOT * CUBIC) * square))
        d_pre = cotangent.held[at, :].astype(F32) * slope
        low.held[at, :] = d_pre.astype(BF16)
        spread.held[at, :] = (d_pre * both).astype(BF16)
    asked_column.start(0)
    for out in (spread, low, mixed):
        out.start()
    gather(spread.held, asked_column.all(), send.held)


def turn(base, scale, cotangent, back, asked_row, asked_column):
    masters, width = base.shape
    return run(
        turn_kernel,
        (),
        (
            (asked_row, 1),
            (back, 1),
            (base, 2),
            (scale, 2),
            (cotangent, 2),
            (asked_column, 2),
        ),
        ((struct(masters, width), 1, 0),) * 3 + ((struct(*back.shape), 1, 0),),
        flops=3e9,
    )


def put_blocks(total, first, value):
    for k in range(value.shape[1] // EDGE):
        total[first + k] = value[:, k * EDGE : (k + 1) * EDGE]


def back_near_kernel(scalars, ins, outs, dense):
    count, column = scalars
    tiles, values = ins
    (total,) = outs
    rows = dense.shape[0]
    begin((tiles,), rows // GROUP)
    for b in range(rows):
        dense[b] = jnp.zeros(dense.shape[1:], BF16)
    turned = jnp.transpose(values.all()[...].astype(F32)).astype(BF16)
    for g in range(rows // GROUP):
        take((tiles,), rows // GROUP, g)
        densify(count, column, tiles.held, dense, g)
    for g in range(total.pieces):
        right = flat(dense, range(rows), range(g * GROUP, (g + 1) * GROUP))
        put_blocks(total.held, g * GROUP, dot(turned, right))
        total.start(g)


def back_near(tile_count, tile_column, tiles, values):
    row_blocks, width = tiles.shape[0], values.shape[1]
    n = groups(tiles)
    (total,) = run(
        back_near_kernel,
        (tile_count, tile_column),
        ((tiles, n), (values, 1)),
        ((struct(row_blocks, width, EDGE, dtype=F32), n, 0),),
        (pltpu.VMEM((values.shape[0] // EDGE, row_blocks + 1, EDGE, EDGE), BF16),),
        flops=5e9,
    )
    return total


def mirror_back_kernel(scalars, ins, outs):
    arrived, slot_column, tiles, partial, slot_row = ins
    send, turned = outs
    last = tiles.pieces - 1
    tiles.start(last)
    partial.start(last)
    pick = pick_columns(slot_column.all()[...], 0, arrived.held.shape[0])
    turned.held[...] = jnp.transpose(dot(pick, arrived.all()[...])).astype(BF16)
    turned.start()
    tiles.wait(last)
    blocks = range(tiles.held.shape[1])
    right = flat(tiles.held, [last * GROUP + b for b in blocks], blocks)
    more = dot(turned.held[...], right)
    partial.wait(last)
    own = jnp.concatenate([partial.held[last * GROUP + c] for c in blocks], axis=1)
    rows = jnp.transpose(own + more).astype(BF16)
    slots = send.held.shape[0]
    send.held[...] = dot(pick_rows(slots, 0, slot_row.all()[...]), rows).astype(BF16)


def mirror_back(arrived, slot_column, slot_row, partial, tiles):
    slots, width = arrived.shape
    mirrors = slot_row.shape[1]
    return run(
        mirror_back_kernel,
        (),
        (
            (arrived, 1),
            (slot_column, 1),
            (tiles, groups(tiles)),
            (partial, groups(tiles)),
            (slot_row, 1),
        ),
        ((struct(slots, width), 1, 0), (struct(width, mirrors), 1, 0)),
        flops=2e9,
    )


def back_far_kernel(scalars, ins, outs, dense):
    count, column = scalars
    tiles, turned, partial = ins
    (total,) = outs
    last = tiles.pieces - 1
    tiles.start(last)
    for g in range(total.pieces):
        partial.start(g)
    dense[...] = jnp.zeros(dense.shape, BF16)
    turned = turned.all()
    tiles.wait(last)
    densify(count, column, tiles.held, dense, last, last * GROUP)
    for g in range(total.pieces):
        columns = range(g * GROUP, (g + 1) * GROUP)
        right = flat(dense, range(GROUP), columns)
        partial.wait(g)
        own = jnp.concatenate([partial.held[c] for c in columns], axis=1)
        put_blocks(total.held, g * GROUP, own + dot(turned[...], right))
        total.start(g)


def back_far(tile_count, tile_column, tiles, turned, partial):
    width, mirrors = turned.shape
    row_blocks = tiles.shape[0]
    masters = row_blocks - mirrors // EDGE
    (total,) = run(
        back_far_kernel,
        (tile_count, tile_column),
        ((tiles, groups(tiles)), (turned, 1), (partial, groups(partial))),
        ((struct(masters, width, EDGE, dtype=F32), masters // GROUP, 0),),
        (pltpu.VMEM((mirrors // EDGE, row_blocks + 1, EDGE, EDGE), BF16),),
        flops=3e9,
    )
    return total


def finish_kernel(scalars, ins, outs):
    (core,) = scalars
    back, asked_column, partial, features, grad_self = ins
    turned, keep, give = outs
    width, masters = turned.held.shape
    inputs = features.held.shape[1]
    step = 512
    flipped = jnp.transpose(back.all()[...].astype(F32)).astype(BF16)
    asked, partial = asked_column.all(), partial.all()
    for g in range(masters // step):
        own = []
        for b in range(g * step // EDGE, (g + 1) * step // EDGE):
            own.append(partial[b])
        added = dot(flipped, pick_columns(asked[...], g * step, step))
        turned.held[:, g * step : (g + 1) * step] = (
            jnp.concatenate(own, axis=1) + added
        ).astype(BF16)
    turned.start()
    total = dot(turned.held[...], features.all()[...])
    grad_self = grad_self.all()
    for h in range(width // EDGE):
        lines = pl.ds(h * inputs, inputs)
        first = grad_self[:, h * EDGE : (h + 1) * EDGE].astype(F32)
        second = jnp.transpose(total[h * EDGE : (h + 1) * EDGE, :])
        keep.held[lines, :] = jnp.where(core[0] == 0, first, second)
        give.held[lines, :] = jnp.where(core[0] == 0, second, first).astype(BF16)


def finish(core, partial, back, asked_column, features, grad_self):
    width = back.shape[1]
    masters, inputs = features.shape
    lines = inputs * width // EDGE
    return run(
        finish_kernel,
        (core,),
        (
            (back, 1),
            (asked_column, 1),
            (partial, 1),
            (features, 1),
            (grad_self, 1),
        ),
        (
            (struct(width, masters), 1, 0),
            (struct(lines, EDGE, dtype=F32), 1, 0),
            (struct(lines, EDGE), 1, 0),
        ),
        flops=3e9,
    )


def input_grads_kernel(scalars, ins, outs):
    low, turned, w_self, w_neigh = ins
    (out,) = outs
    step = out.size
    own, other, low, turned = w_self.all(), w_neigh.all(), low.all(), turned.all()
    for g in range(out.pieces):
        at = slice(g * step, (g + 1) * step)
        d_projected = jnp.transpose(turned[:, at].astype(F32)).astype(BF16)
        value = dot(low[at, :], own[...], 1, 1) + dot(d_projected, other[...], 1, 1)
        out.held[at, :] = value.astype(BF16)
        out.start(g)


def input_grads(low, turned, w_self, w_neigh):
    masters, inputs = low.shape[0], w_self.shape[0]
    (out,) = run(
        input_grads_kernel,
        (),
        ((low, 1), (turned, 1), (w_self, 1), (w_neigh, 1)),
        ((struct(masters, inputs), 2, 0),),
        flops=3e9,
    )
    return out


def share_kernel(parts, out):
    share = jnp.sum(parts[...].astype(F32), axis=0, keepdims=True).astype(BF16)
    out[...] = jnp.broadcast_to(share, out.shape)


def share_out(parts):
    return pl.pallas_call(
        share_kernel,
        out_shape=struct(*parts.shape),
        compiler_params=params(8 * MIB),
        cost_estimate=cost(1e8),
    )(parts)


def unpack_kernel(core, mine, other, first, second):
    inputs = first.shape[0]
    for h in range(2):
        lines, lanes = pl.ds(h * inputs, inputs), pl.ds(h * EDGE, EDGE)
        a, b = mine[lines, :].astype(F32), other[lines, :].astype(F32)
        first[:, lanes] = jnp.where(core[0] == 0, a, b)
        second[:, lanes] = jnp.where(core[0] == 0, b, a)


def unpack(core, mine, other, inputs, width):
    smem, vmem = pl.BlockSpec(memory_space=pltpu.SMEM), pl.BlockSpec(memory_space=pltpu.VMEM)
    return pl.pallas_call(
        unpack_kernel,
        in_specs=[smem, vmem, vmem],
        out_specs=[vmem, vmem],
        out_shape=[struct(inputs, width, dtype=F32)] * 2,
        compiler_params=params(8 * MIB),
        cost_estimate=cost(1e8),
    )(core, mine, other)


def exchange(buffer, axes=EVERY):
    parts = lax.axis_size(axes)
    moved = lax.all_to_all(
        buffer.reshape(parts, buffer.shape[0] // parts, buffer.shape[1]),
        axes,
        split_axis=0,
        concat_axis=0,
        tiled=True,
    )
    return moved.reshape(buffer.shape)


def to_other_core(value):
    return lax.ppermute(value, "core", [(0, 1), (1, 0)])


def on_device(
    features,
    w_self,
    w_neigh,
    mirror_master_part,
    mirror_row,
    tile_count,
    tile_column,
    tile_weight,
    cotangent,
):
    inputs, width = w_neigh.shape
    parts = lax.axis_size(EVERY)
    core = lax.axis_index("core").astype(I32).reshape(1)
    slots = SLOTS * parts
    peer = mirror_master_part[:, 0]
    tile_column = tile_column.T
    ask, slot_row, slot_column = place(tile_count, peer, mirror_row, tile_weight, parts)
    asked = exchange(ask)
    projected = jnp.dot(features, w_neigh, preferred_element_type=F32).astype(BF16)
    own = jnp.dot(features, w_self, preferred_element_type=F32)
    asked, own = lax.optimization_barrier((asked, own))
    asked = pltpu.with_memory_space_constraint(asked, pltpu.HBM)
    rows, asked_column = fetch(asked, projected, slots)
    rows, projected = lax.optimization_barrier((rows, projected))
    arrived = exchange(rows)
    partial, degree, far_tiles = near(tile_count, tile_column, tile_weight, projected)
    send, slab = mirror_out(arrived, slot_column, slot_row, partial, far_tiles)
    back = exchange(send)
    base, scale, asked_row = far(far_tiles, slab, partial, degree, own, asked, asked_column)
    mixed, low, spread, send = turn(base, scale, cotangent, back, asked_row, asked_column)
    arrived = exchange(send)
    partial = back_near(tile_count, tile_column, tile_weight, spread)
    grad_self = lax.dot_general(
        features, low, (((0,), (0,)), ((), ())), preferred_element_type=F32
    ).astype(BF16)
    send, turned = mirror_back(arrived, slot_column, slot_row, partial, far_tiles)
    back = exchange(send)
    partial = back_far(tile_count, tile_column, tile_weight, turned, partial)
    d_projected, keep, give = finish(core, partial, back, asked_column, features, grad_self)
    pair = (keep + to_other_core(give).astype(F32)).astype(BF16)
    same = ("chip", "local")
    shares = exchange(pair, same).reshape(lax.axis_size(same), -1, EDGE)
    grad_features = input_grads(low, d_projected, w_self, w_neigh)
    shares, grad_features = lax.optimization_barrier((shares, grad_features))
    mine = exchange(share_out(shares).reshape(pair.shape), same)
    grad_self, grad_neigh = unpack(core, mine, to_other_core(mine), inputs, width)
    return (mixed, grad_features, grad_self, grad_neigh)


def solution(mesh):
    machine, local = mesh.devices.shape
    devices = mesh.devices.reshape(machine // 2, 2, local)
    split, rows = P(EVERY), P(EVERY, None)
    return jax.shard_map(
        on_device,
        mesh=jax.sharding.Mesh(devices, EVERY),
        in_specs=(rows, P(), P(), rows, split, split, rows, P(EVERY, None, None, None), rows),
        out_specs=(rows, rows, P(), P()),
        check_vma=False,
    )
```

```python
import jax
import jax.numpy as jnp
from jax import lax
from jax.experimental import pallas as pl
from jax.experimental.pallas import tpu as pltpu
from jax.sharding import PartitionSpec as P

F32 = jnp.float32
BF16 = jnp.bfloat16
I32 = jnp.int32
EDGE = 128
SLOTS = 8
MIB = 1024 * 1024
VMEM_BYTES = 60 * MIB
GROUP = 4
AHEAD = 2
ROOT = 0.7978845608028654
CUBIC = 0.044715
EVERY = ("chip", "core", "local")


def dot(a, b, ca=1, cb=0):
    return lax.dot_general(a, b, (((ca,), (cb,)), ((), ())), preferred_element_type=F32)


def iota(shape, dim):
    return lax.broadcasted_iota(I32, shape, dim)


def pick_rows(rows, base, row):
    return jnp.where(iota((rows, row.shape[1]), 0) + base == row, 1.0, 0.0).astype(BF16)


def pick_columns(column, base, columns):
    lane = iota(column.shape, 1) + base
    parts = [
        jnp.where(column == lane + EDGE * g, 1.0, 0.0).astype(BF16) for g in range(columns // EDGE)
    ]
    return jnp.concatenate(parts, axis=1)


def struct(*shape, dtype=BF16):
    return jax.ShapeDtypeStruct(shape, dtype)


class Moved:
    def __init__(self, far, held, sems, pieces, inward):
        self.far, self.held, self.sems, self.pieces, self.inward = far, held, sems, pieces, inward
        self.size = far.shape[0] // pieces
        self.started, self.waited = False, False

    def rows(self, p):
        return slice(p * self.size, (p + 1) * self.size)

    def copy(self, p):
        at = pl.ds(p * self.size, self.size)
        ends = self.far.at[at], self.held.at[at]
        return pltpu.make_async_copy(*(ends if self.inward else ends[::-1]), self.sems.at[p])

    def start(self, p=0):
        self.started = True
        self.copy(p).start()

    def wait(self, p=0):
        self.copy(p).wait()

    def all(self):
        if not self.waited:
            for p in range(self.pieces):
                self.wait(p)
        self.waited = True
        return self.held


class Here(Moved):
    def __init__(self, held, pieces):
        self.held, self.pieces = held, pieces
        self.size = held.shape[0] // pieces
        self.waited = True

    def start(self, p=0):
        pass

    def wait(self, p=0):
        pass


def inner(array):
    return ("inner", array)


def begin(sources, pieces):
    for g in range(min(AHEAD, pieces)):
        for source in sources:
            source.start(g)


def take(sources, pieces, g):
    for source in sources:
        source.wait(g)
    if g + AHEAD < pieces:
        for source in sources:
            source.start(g + AHEAD)


def run(kernel, scalars, ins, outs, scratch=(), flops=1e9):
    entries = [(x, pieces, 0) for x, pieces in ins] + list(outs)
    n = len(ins)
    kept = [isinstance(entry[0], tuple) for entry in entries]
    arrays = [entry[0][1] if k else entry[0] for entry, k in zip(entries, kept)]
    own = [k for k, entry in enumerate(entries) if entry[1] and not kept[k]]

    def body(*refs):
        scalar_refs, refs = refs[: len(scalars)], refs[len(scalars) :]
        far, refs = list(refs[: len(entries)]), refs[len(entries) :]
        held, sems, rest = refs[: len(own)], refs[len(own) : 2 * len(own)], refs[2 * len(own) :]
        for k, entry in enumerate(entries):
            if kept[k]:
                far[k] = Here(far[k], entry[1])
        for at, k in enumerate(own):
            far[k] = Moved(far[k], held[at], sems[at], entries[k][1], k < n)
            if k < n and entries[k][1] == 1:
                far[k].start()
        kernel(scalar_refs, far[:n], far[n:], *rest)
        results = [far[k] for k in own if k >= n]
        for out in results:
            if not out.started:
                for p in range(out.pieces):
                    out.start(p)
        for out in results:
            out.all()

    def place_of(k):
        shape = arrays[k].shape
        return pltpu.VMEM((shape[0] + entries[k][2], *shape[1:]), arrays[k].dtype)

    smem, vmem = pl.BlockSpec(memory_space=pltpu.SMEM), pl.BlockSpec(memory_space=pltpu.VMEM)
    specs = [vmem if k else pl.BlockSpec(memory_space=pl.ANY) for k in kept]
    given = [
        pltpu.with_memory_space_constraint(x, pltpu.VMEM) if k else x
        for x, k in zip(arrays[:n], kept)
    ]
    return pl.pallas_call(
        body,
        in_specs=[smem] * len(scalars) + specs[:n],
        out_specs=specs[n:],
        out_shape=[
            pltpu.VMEM(x.shape, x.dtype) if k else x for x, k in zip(arrays[n:], kept[n:])
        ],
        scratch_shapes=[place_of(k) for k in own]
        + [pltpu.SemaphoreType.DMA((entries[k][1],)) for k in own]
        + list(scratch),
        compiler_params=params(),
        cost_estimate=cost(flops),
    )(*scalars, *given)


def params(limit=VMEM_BYTES):
    return pltpu.CompilerParams(vmem_limit_bytes=limit)


def cost(flops):
    return pl.CostEstimate(flops=int(flops), bytes_accessed=4 * MIB, transcendentals=0)


def groups(tiles):
    return tiles.shape[0] // GROUP


def thirds(value):
    first = value.astype(BF16).astype(F32)
    second = (value - first).astype(BF16).astype(F32)
    return first, second, value - first - second


def used_ones(n, most):
    return jnp.concatenate(
        [jnp.full((EDGE, EDGE), jnp.where(t < n, 1.0, 0.0), F32).astype(BF16) for t in range(most)],
        axis=0,
    )


def place_kernel(scalars, ins, outs):
    (count,) = scalars
    peer, row, tiles = ins
    ask, slot_row, slot_column = outs
    mirrors = peer.held.shape[1]
    parts = ask.held.shape[0]
    blocks, most = mirrors // EDGE, tiles.held.shape[1]
    first = count.shape[0] - blocks
    last = tiles.pieces - 1
    tiles.start(last)
    peer = peer.all()[...]
    member = iota((parts, mirrors), 0) == peer
    chosen = jnp.where(member, 1.0, 0.0).astype(BF16)
    earlier = jnp.where(
        iota((mirrors, mirrors), 0) < iota((mirrors, mirrors), 1), 1.0, 0.0
    ).astype(BF16)
    before = dot(chosen, earlier)
    rank = jnp.sum(jnp.where(member, before, 0.0), axis=0, keepdims=True).astype(I32)
    slot = peer * SLOTS + rank
    slot_row.held[...] = slot
    slot_column.held[...] = jnp.transpose(
        jnp.broadcast_to(slot.astype(F32), (EDGE, mirrors))
    ).astype(I32)
    slot_row.start()
    slot_column.start()
    lane = iota((EDGE, mirrors), 0) - rank
    named = row.all()[...] + 1
    degrees = []
    tiles.wait(last)
    for b in range(first, first + blocks):
        flat = jnp.concatenate([tiles.held[b, t] for t in range(most)], axis=1)
        degrees.append(jnp.transpose(dot(flat, used_ones(count[b], most)))[0:1])
    fields = (named // EDGE).astype(F32), (named % EDGE).astype(F32)
    fields += thirds(jnp.concatenate(degrees, axis=1))
    lines = jnp.zeros((EDGE, mirrors), F32)
    for k, field in enumerate(fields):
        lines = jnp.where(lane == SLOTS * k, field, lines)
    ask.held[...] = dot(chosen, lines.astype(BF16), 1, 1)


def place(tile_count, peer, row, tiles, parts):
    mirrors = row.shape[0]
    return run(
        place_kernel,
        (tile_count,),
        ((peer.reshape(1, mirrors), 1), (row.reshape(1, mirrors), 1), (tiles, groups(tiles))),
        (
            (struct(parts, EDGE, dtype=F32), 1, 0),
            (struct(1, mirrors, dtype=I32), 1, 0),
            (struct(mirrors, EDGE, dtype=I32), 1, 0),
        ),
    )


def slot_lines(arrived, slots):
    parts = arrived.shape[0]
    spread = jnp.where(iota((slots, parts), 0) // SLOTS == iota((slots, parts), 1), 1.0, 0.0)
    return dot(spread.astype(BF16), arrived[...].astype(BF16))


def gather(values, asked_column, rows):
    for g in range(rows.pieces):
        at = rows.rows(g)
        pick = pick_columns(asked_column[at, :], 0, values.shape[0])
        rows.held[at, :] = dot(pick, values[...]).astype(BF16)
        rows.start(g)


def to_slots(slot_row, values, send):
    for g in range(send.pieces):
        pick = pick_rows(send.size, g * send.size, slot_row)
        send.held[send.rows(g), :] = dot(pick, values).astype(BF16)
        send.start(g)


def fetch_kernel(scalars, ins, outs):
    arrived, values = ins
    rows, asked_column = outs
    slots = rows.held.shape[0]
    every = slot_lines(arrived.all(), slots)
    lane = iota((slots, EDGE), 1) - iota((slots, EDGE), 0) % SLOTS
    asked = jnp.where(lane == 0, every * EDGE, jnp.where(lane == SLOTS, every, 0.0))
    asked = jnp.sum(asked, axis=1, keepdims=True) - 1.0
    asked_column.held[...] = jnp.broadcast_to(asked, (slots, EDGE)).astype(I32)
    asked_column.start()
    gather(values.all(), asked_column.held, rows)


def fetch(arrived, values, slots):
    return run(
        fetch_kernel,
        (),
        ((arrived, 1), (values, 1)),
        ((struct(slots, values.shape[1]), 2, 0), (struct(slots, EDGE, dtype=I32), 1, 0)),
        flops=2e9,
    )


def flat(tiles, rows, columns):
    lines = [jnp.concatenate([tiles[b, c] for c in columns], axis=1) for b in rows]
    return jnp.concatenate(lines, axis=0)


def densify(count, column, tiles, dense, g, first=0):
    members = range(g * GROUP, (g + 1) * GROUP)
    last = dense.shape[1] - 1
    longest = count[g * GROUP]
    for b in members:
        longest = jnp.maximum(longest, count[b])

    def body(t, carry):
        for b in members:
            c = jnp.where(t < count[b], column[t, b], last)
            dense[b - first, c] = dense[b - first, c] + tiles[b, t]
        return carry

    lax.fori_loop(0, longest, body, 0)


def near_kernel(scalars, ins, outs, dense, far_sems):
    count, column = scalars
    tiles, values = ins
    partial, degree, far = outs
    row_blocks = tiles.held.shape[0]
    last = dense.shape[1] - 1
    cut = last - far.shape[1]

    def far_copy(g):
        at = pl.ds(g * GROUP, GROUP)
        return pltpu.make_async_copy(dense.at[at, pl.ds(cut, last - cut)], far.at[at], far_sems.at[g])

    begin((tiles,), tiles.pieces)
    for b in range(row_blocks):
        dense[b] = jnp.zeros(dense.shape[1:], BF16)
    values = values.all()
    for g in range(tiles.pieces):
        take((tiles,), tiles.pieces, g)
        densify(count, column, tiles.held, dense, g)
        far_copy(g).start()
        for b in range(g * GROUP, (g + 1) * GROUP):
            at = slice(b * EDGE, (b + 1) * EDGE)
            partial.held[at, :] = dot(flat(dense, (b,), range(cut)), values[...])
            if g < degree.pieces:
                weights = dense[b, 0].astype(F32)
                for c in range(1, last):
                    weights += dense[b, c].astype(F32)
                total = jnp.sum(weights, axis=1, keepdims=True)
                degree.held[at, :] = jnp.broadcast_to(total, (EDGE, EDGE))
        partial.start(g)
        if g < degree.pieces:
            degree.start(g)
    for g in range(tiles.pieces):
        far_copy(g).wait()


def near(tile_count, tile_column, tiles, values):
    rows, width = values.shape
    row_blocks = tiles.shape[0]
    masters = rows // EDGE
    return run(
        near_kernel,
        (tile_count, tile_column),
        ((tiles, groups(tiles)), (values, 1)),
        (
            (struct(row_blocks * EDGE, width, dtype=F32), groups(tiles), 0),
            (struct(rows, EDGE, dtype=F32), masters // GROUP, 0),
            (struct(row_blocks, row_blocks - masters, EDGE, EDGE), 0, 0),
        ),
        (
            pltpu.VMEM((row_blocks, row_blocks + 1, EDGE, EDGE), BF16),
            pltpu.SemaphoreType.DMA((groups(tiles),)),
        ),
        flops=5e9,
    )


def mirror_out_kernel(scalars, ins, outs):
    arrived, slot_column, partial, tiles, slot_row = ins
    send, slab = outs
    last = tiles.pieces - 1
    tiles.start(last)
    partial.start(last)
    pick = pick_columns(slot_column.all()[...], 0, arrived.held.shape[0])
    slab.held[...] = dot(pick, arrived.all()[...]).astype(BF16)
    slab.start()
    tiles.wait(last)
    blocks = range(tiles.held.shape[1])
    left = flat(tiles.held, [last * GROUP + b for b in blocks], blocks)
    more = dot(left, slab.held[...])
    partial.wait(last)
    total = (partial.held[partial.rows(last), :] + more).astype(BF16)
    to_slots(slot_row.all()[...], total, send)


def mirror_out(arrived, slot_column, slot_row, partial, tiles):
    slots, width = arrived.shape
    mirrors = slot_row.shape[1]
    return run(
        mirror_out_kernel,
        (),
        (
            (inner(arrived), 1),
            (slot_column, 1),
            (partial, groups(tiles)),
            (tiles, groups(tiles)),
            (slot_row, 1),
        ),
        ((struct(slots, width), 2, 0), (struct(mirrors, width), 1, 0)),
        flops=2e9,
    )


def far_kernel(scalars, ins, outs):
    slab, arrived, asked_column, tiles, partial, own, degree = ins
    base, scale, asked_row = outs
    sources = (tiles, partial, own, degree)
    begin(sources, own.pieces)
    slots = asked_column.held.shape[0]
    asked = jnp.transpose(asked_column.all()[...].astype(F32))[0:8].astype(I32)
    asked_row.held[...] = asked
    asked_row.start()
    lane = iota((slots, EDGE), 1) - iota((slots, EDGE), 0) % SLOTS
    mine = (lane == 2 * SLOTS) | (lane == 3 * SLOTS) | (lane == 4 * SLOTS)
    sums = jnp.sum(jnp.where(mine, slot_lines(arrived.all(), slots), 0.0), axis=1, keepdims=True)
    degrees = jnp.transpose(jnp.broadcast_to(sums, (slots, EDGE)))[0:1]
    slab = slab.all()
    rows = own.size
    for g in range(own.pieces):
        take(sources, own.pieces, g)
        at = own.rows(g)
        left = flat(tiles.held, range(g * GROUP, (g + 1) * GROUP), range(tiles.held.shape[1]))
        total = partial.held[at, :] + dot(left, slab[...])
        hit = iota((rows, slots), 0) + g * rows == asked[0:1]
        more = jnp.sum(jnp.where(hit, degrees, 0.0), axis=1, keepdims=True)
        factor = 1.0 / (1.0 + (degree.held[at, :] + more))
        scale.held[at, :] = factor
        base.held[at, :] = own.held[at, :] + total * jnp.concatenate([factor, factor], axis=1)
        base.start(g)
    scale.start()


def far(tiles, slab, partial, degree, own, arrived, asked_column):
    masters, width = own.shape
    n = masters // EDGE // GROUP
    return run(
        far_kernel,
        (),
        (
            (slab, 1),
            (arrived, 1),
            (asked_column, 1),
            (tiles, groups(tiles)),
            (partial, groups(tiles)),
            (own, n),
            (degree, n),
        ),
        (
            (inner(struct(masters, width, dtype=F32)), n, 0),
            (struct(masters, EDGE, dtype=F32), 1, 0),
            (struct(8, asked_column.shape[0], dtype=I32), 1, 0),
        ),
        flops=5e9,
    )


def turn_kernel(scalars, ins, outs):
    asked_row, back, base, scale, cotangent, asked_column = ins
    mixed, low, spread, send = outs
    for source in (base, scale, cotangent):
        source.start(0)
    asked, back = asked_row.all()[0:1], back.all()
    step = 512
    for g in range(base.held.shape[0] // step):
        if g * step % base.size == 0:
            p = g * step // base.size
            for source in (base, scale, cotangent):
                source.wait(p)
            for source in (base, scale, cotangent, asked_column):
                if p + 1 < source.pieces:
                    source.start(p + 1)
        at = slice(g * step, (g + 1) * step)
        both = jnp.concatenate([scale.held[at, :], scale.held[at, :]], axis=1)
        added = dot(pick_rows(step, g * step, asked), back[...])
        u = base.held[at, :] + added * both
        square = u * u
        bend = jnp.tanh(u * (ROOT + (ROOT * CUBIC) * square))
        half = 0.5 + 0.5 * bend
        mixed.held[at, :] = (u * half).astype(BF16)
        slope = half * (1.0 + u * (1.0 - bend) * (ROOT + (3.0 * ROOT * CUBIC) * square))
        d_pre = cotangent.held[at, :].astype(F32) * slope
        low.held[at, :] = d_pre.astype(BF16)
        spread.held[at, :] = (d_pre * both).astype(BF16)
    asked_column.start(0)
    for out in (spread, low, mixed):
        out.start()
    gather(spread.held, asked_column.all(), send)


def turn(base, scale, cotangent, back, asked_row, asked_column):
    masters, width = base.shape
    return run(
        turn_kernel,
        (),
        (
            (asked_row, 1),
            (inner(back), 1),
            (inner(base), 2),
            (scale, 2),
            (cotangent, 2),
            (asked_column, 2),
        ),
        ((struct(masters, width), 1, 0),) * 3 + ((struct(*back.shape), 2, 0),),
        flops=3e9,
    )


def put_blocks(total, first, value):
    for k in range(value.shape[1] // EDGE):
        total[first + k] = value[:, k * EDGE : (k + 1) * EDGE]


def back_near_kernel(scalars, ins, outs, dense):
    count, column = scalars
    tiles, values = ins
    (total,) = outs
    rows = dense.shape[0]
    begin((tiles,), rows // GROUP)
    for b in range(rows):
        dense[b] = jnp.zeros(dense.shape[1:], BF16)
    turned = jnp.transpose(values.all()[...].astype(F32)).astype(BF16)
    for g in range(rows // GROUP):
        take((tiles,), rows // GROUP, g)
        densify(count, column, tiles.held, dense, g)
    for g in range(total.pieces):
        right = flat(dense, range(rows), range(g * GROUP, (g + 1) * GROUP))
        put_blocks(total.held, g * GROUP, dot(turned, right))
        total.start(g)


def back_near(tile_count, tile_column, tiles, values):
    row_blocks, width = tiles.shape[0], values.shape[1]
    n = groups(tiles)
    (total,) = run(
        back_near_kernel,
        (tile_count, tile_column),
        ((tiles, n), (values, 1)),
        ((struct(row_blocks, width, EDGE, dtype=F32), n, 0),),
        (pltpu.VMEM((values.shape[0] // EDGE, row_blocks + 1, EDGE, EDGE), BF16),),
        flops=5e9,
    )
    return total


def mirror_back_kernel(scalars, ins, outs):
    arrived, slot_column, tiles, partial, slot_row = ins
    send, turned = outs
    last = tiles.pieces - 1
    tiles.start(last)
    partial.start(last)
    pick = pick_columns(slot_column.all()[...], 0, arrived.held.shape[0])
    turned.held[...] = jnp.transpose(dot(pick, arrived.all()[...])).astype(BF16)
    turned.start()
    tiles.wait(last)
    blocks = range(tiles.held.shape[1])
    right = flat(tiles.held, [last * GROUP + b for b in blocks], blocks)
    more = dot(turned.held[...], right)
    partial.wait(last)
    own = jnp.concatenate([partial.held[last * GROUP + c] for c in blocks], axis=1)
    rows = jnp.transpose(own + more).astype(BF16)
    to_slots(slot_row.all()[...], rows, send)


def mirror_back(arrived, slot_column, slot_row, partial, tiles):
    slots, width = arrived.shape
    mirrors = slot_row.shape[1]
    return run(
        mirror_back_kernel,
        (),
        (
            (inner(arrived), 1),
            (slot_column, 1),
            (tiles, groups(tiles)),
            (partial, groups(tiles)),
            (slot_row, 1),
        ),
        ((struct(slots, width), 2, 0), (struct(width, mirrors), 1, 0)),
        flops=2e9,
    )


def back_far_kernel(scalars, ins, outs, dense):
    count, column = scalars
    tiles, turned, partial = ins
    (total,) = outs
    last = tiles.pieces - 1
    tiles.start(last)
    for g in range(total.pieces):
        partial.start(g)
    dense[...] = jnp.zeros(dense.shape, BF16)
    turned = turned.all()
    tiles.wait(last)
    densify(count, column, tiles.held, dense, last, last * GROUP)
    for g in range(total.pieces):
        columns = range(g * GROUP, (g + 1) * GROUP)
        right = flat(dense, range(GROUP), columns)
        partial.wait(g)
        own = jnp.concatenate([partial.held[c] for c in columns], axis=1)
        put_blocks(total.held, g * GROUP, own + dot(turned[...], right))
        total.start(g)


def back_far(tile_count, tile_column, tiles, turned, partial):
    width, mirrors = turned.shape
    row_blocks = tiles.shape[0]
    masters = row_blocks - mirrors // EDGE
    (total,) = run(
        back_far_kernel,
        (tile_count, tile_column),
        ((tiles, groups(tiles)), (turned, 1), (partial, groups(partial))),
        ((inner(struct(masters, width, EDGE, dtype=F32)), masters // GROUP, 0),),
        (pltpu.VMEM((mirrors // EDGE, row_blocks + 1, EDGE, EDGE), BF16),),
        flops=3e9,
    )
    return total


def finish_kernel(scalars, ins, outs):
    (core,) = scalars
    back, asked_column, partial, features, grad_self = ins
    turned, keep, give = outs
    width, masters = turned.held.shape
    inputs = features.held.shape[1]
    step = 512
    flipped = jnp.transpose(back.all()[...].astype(F32)).astype(BF16)
    asked, partial = asked_column.all(), partial.all()
    for g in range(masters // step):
        own = []
        for b in range(g * step // EDGE, (g + 1) * step // EDGE):
            own.append(partial[b])
        added = dot(flipped, pick_columns(asked[...], g * step, step))
        turned.held[:, g * step : (g + 1) * step] = (
            jnp.concatenate(own, axis=1) + added
        ).astype(BF16)
    turned.start()
    total = dot(turned.held[...], features.all()[...])
    grad_self = grad_self.all()
    for h in range(width // EDGE):
        lines = pl.ds(h * inputs, inputs)
        first = grad_self[:, h * EDGE : (h + 1) * EDGE].astype(F32)
        second = jnp.transpose(total[h * EDGE : (h + 1) * EDGE, :])
        keep.held[lines, :] = jnp.where(core[0] == 0, first, second)
        give.held[lines, :] = jnp.where(core[0] == 0, second, first).astype(BF16)


def finish(core, partial, back, asked_column, features, grad_self):
    width = back.shape[1]
    masters, inputs = features.shape
    lines = inputs * width // EDGE
    return run(
        finish_kernel,
        (core,),
        (
            (inner(back), 1),
            (asked_column, 1),
            (inner(partial), 1),
            (features, 1),
            (grad_self, 1),
        ),
        (
            (struct(width, masters), 1, 0),
            (struct(lines, EDGE, dtype=F32), 1, 0),
            (struct(lines, EDGE), 1, 0),
        ),
        flops=3e9,
    )


def input_grads_kernel(scalars, ins, outs):
    low, turned, w_self, w_neigh = ins
    (out,) = outs
    step = out.size
    own, other, low, turned = w_self.all(), w_neigh.all(), low.all(), turned.all()
    for g in range(out.pieces):
        at = slice(g * step, (g + 1) * step)
        d_projected = jnp.transpose(turned[:, at].astype(F32)).astype(BF16)
        value = dot(low[at, :], own[...], 1, 1) + dot(d_projected, other[...], 1, 1)
        out.held[at, :] = value.astype(BF16)
        out.start(g)


def input_grads(low, turned, w_self, w_neigh):
    masters, inputs = low.shape[0], w_self.shape[0]
    (out,) = run(
        input_grads_kernel,
        (),
        ((low, 1), (turned, 1), (w_self, 1), (w_neigh, 1)),
        ((struct(masters, inputs), 2, 0),),
        flops=3e9,
    )
    return out


def share_kernel(parts, out):
    share = jnp.sum(parts[...].astype(F32), axis=0, keepdims=True).astype(BF16)
    out[...] = jnp.broadcast_to(share, out.shape)


def share_out(parts):
    return pl.pallas_call(
        share_kernel,
        out_shape=struct(*parts.shape),
        compiler_params=params(8 * MIB),
        cost_estimate=cost(1e8),
    )(parts)


def unpack_kernel(core, mine, other, first, second):
    inputs = first.shape[0]
    for h in range(2):
        lines, lanes = pl.ds(h * inputs, inputs), pl.ds(h * EDGE, EDGE)
        a, b = mine[lines, :].astype(F32), other[lines, :].astype(F32)
        first[:, lanes] = jnp.where(core[0] == 0, a, b)
        second[:, lanes] = jnp.where(core[0] == 0, b, a)


def unpack(core, mine, other, inputs, width):
    smem, vmem = pl.BlockSpec(memory_space=pltpu.SMEM), pl.BlockSpec(memory_space=pltpu.VMEM)
    return pl.pallas_call(
        unpack_kernel,
        in_specs=[smem, vmem, vmem],
        out_specs=[vmem, vmem],
        out_shape=[struct(inputs, width, dtype=F32)] * 2,
        compiler_params=params(8 * MIB),
        cost_estimate=cost(1e8),
    )(core, mine, other)


def exchange(buffer, axes=EVERY):
    parts = lax.axis_size(axes)
    moved = lax.all_to_all(
        buffer.reshape(parts, buffer.shape[0] // parts, buffer.shape[1]),
        axes,
        split_axis=0,
        concat_axis=0,
        tiled=True,
    )
    return moved.reshape(buffer.shape)


def to_other_core(value):
    return lax.ppermute(value, "core", [(0, 1), (1, 0)])


def on_device(
    features,
    w_self,
    w_neigh,
    mirror_master_part,
    mirror_row,
    tile_count,
    tile_column,
    tile_weight,
    cotangent,
):
    inputs, width = w_neigh.shape
    parts = lax.axis_size(EVERY)
    core = lax.axis_index("core").astype(I32).reshape(1)
    slots = SLOTS * parts
    peer = mirror_master_part[:, 0]
    tile_column = tile_column.T
    ask, slot_row, slot_column = place(tile_count, peer, mirror_row, tile_weight, parts)
    asked = exchange(ask)
    projected = jnp.dot(features, w_neigh, preferred_element_type=F32).astype(BF16)
    own = jnp.dot(features, w_self, preferred_element_type=F32)
    asked, own = lax.optimization_barrier((asked, own))
    asked = pltpu.with_memory_space_constraint(asked, pltpu.HBM)
    rows, asked_column = fetch(asked, projected, slots)
    rows, projected = lax.optimization_barrier((rows, projected))
    arrived = exchange(rows)
    partial, degree, far_tiles = near(tile_count, tile_column, tile_weight, projected)
    send, slab = mirror_out(arrived, slot_column, slot_row, partial, far_tiles)
    back = exchange(send)
    base, scale, asked_row = far(far_tiles, slab, partial, degree, own, asked, asked_column)
    mixed, low, spread, send = turn(base, scale, cotangent, back, asked_row, asked_column)
    arrived = exchange(send)
    partial = back_near(tile_count, tile_column, tile_weight, spread)
    grad_self = lax.dot_general(
        features, low, (((0,), (0,)), ((), ())), preferred_element_type=F32
    ).astype(BF16)
    send, turned = mirror_back(arrived, slot_column, slot_row, partial, far_tiles)
    back = exchange(send)
    partial = back_far(tile_count, tile_column, tile_weight, turned, partial)
    d_projected, keep, give = finish(core, partial, back, asked_column, features, grad_self)
    pair = (keep + to_other_core(give).astype(F32)).astype(BF16)
    same = ("chip", "local")
    shares = exchange(pair, same).reshape(lax.axis_size(same), -1, EDGE)
    grad_features = input_grads(low, d_projected, w_self, w_neigh)
    shares, grad_features = lax.optimization_barrier((shares, grad_features))
    mine = exchange(share_out(shares).reshape(pair.shape), same)
    grad_self, grad_neigh = unpack(core, mine, to_other_core(mine), inputs, width)
    return (mixed, grad_features, grad_self, grad_neigh)


def solution(mesh):
    machine, local = mesh.devices.shape
    devices = mesh.devices.reshape(machine // 2, 2, local)
    split, rows = P(EVERY), P(EVERY, None)
    return jax.shard_map(
        on_device,
        mesh=jax.sharding.Mesh(devices, EVERY),
        in_specs=(rows, P(), P(), rows, split, split, rows, P(EVERY, None, None, None), rows),
        out_specs=(rows, rows, P(), P()),
        check_vma=False,
    )
```

```python
import jax
import jax.numpy as jnp
from jax import lax
from jax.experimental import pallas as pl
from jax.experimental.pallas import tpu as pltpu
from jax.sharding import PartitionSpec as P

F32 = jnp.float32
BF16 = jnp.bfloat16
I32 = jnp.int32
EDGE = 128
SLOTS = 8
MIB = 1024 * 1024
VMEM_BYTES = 60 * MIB
GROUP = 4
AHEAD = 2
ROOT = 0.7978845608028654
CUBIC = 0.044715
EVERY = ("chip", "core", "local")


def dot(a, b, ca=1, cb=0):
    return lax.dot_general(a, b, (((ca,), (cb,)), ((), ())), preferred_element_type=F32)


def iota(shape, dim):
    return lax.broadcasted_iota(I32, shape, dim)


def pick_rows(rows, base, row):
    return jnp.where(iota((rows, row.shape[1]), 0) + base == row, 1.0, 0.0).astype(BF16)


def pick_columns(column, base, columns):
    lane = iota(column.shape, 1) + base
    parts = [
        jnp.where(column == lane + EDGE * g, 1.0, 0.0).astype(BF16) for g in range(columns // EDGE)
    ]
    return jnp.concatenate(parts, axis=1)


def struct(*shape, dtype=BF16):
    return jax.ShapeDtypeStruct(shape, dtype)


class Moved:
    def __init__(self, far, held, sems, pieces, inward):
        self.far, self.held, self.sems, self.pieces, self.inward = far, held, sems, pieces, inward
        self.size = far.shape[0] // pieces
        self.started, self.waited = False, False

    def rows(self, p):
        return slice(p * self.size, (p + 1) * self.size)

    def copy(self, p):
        at = pl.ds(p * self.size, self.size)
        ends = self.far.at[at], self.held.at[at]
        return pltpu.make_async_copy(*(ends if self.inward else ends[::-1]), self.sems.at[p])

    def start(self, p=0):
        self.started = True
        self.copy(p).start()

    def wait(self, p=0):
        self.copy(p).wait()

    def all(self):
        if not self.waited:
            for p in range(self.pieces):
                self.wait(p)
        self.waited = True
        return self.held


class Here(Moved):
    def __init__(self, held, pieces):
        self.held, self.pieces = held, pieces
        self.size = held.shape[0] // pieces
        self.waited = True

    def start(self, p=0):
        pass

    def wait(self, p=0):
        pass


def inner(array):
    return ("inner", array)


def begin(sources, pieces):
    for g in range(min(AHEAD, pieces)):
        for source in sources:
            source.start(g)


def take(sources, pieces, g):
    for source in sources:
        source.wait(g)
    if g + AHEAD < pieces:
        for source in sources:
            source.start(g + AHEAD)


def run(kernel, scalars, ins, outs, scratch=(), flops=1e9):
    entries = [(x, pieces, 0) for x, pieces in ins] + list(outs)
    n = len(ins)
    kept = [isinstance(entry[0], tuple) for entry in entries]
    arrays = [entry[0][1] if k else entry[0] for entry, k in zip(entries, kept)]
    own = [k for k, entry in enumerate(entries) if entry[1] and not kept[k]]

    def body(*refs):
        scalar_refs, refs = refs[: len(scalars)], refs[len(scalars) :]
        far, refs = list(refs[: len(entries)]), refs[len(entries) :]
        held, sems, rest = refs[: len(own)], refs[len(own) : 2 * len(own)], refs[2 * len(own) :]
        for k, entry in enumerate(entries):
            if kept[k]:
                far[k] = Here(far[k], entry[1])
        for at, k in enumerate(own):
            far[k] = Moved(far[k], held[at], sems[at], entries[k][1], k < n)
            if k < n and entries[k][1] == 1:
                far[k].start()
        kernel(scalar_refs, far[:n], far[n:], *rest)
        results = [far[k] for k in own if k >= n]
        for out in results:
            if not out.started:
                for p in range(out.pieces):
                    out.start(p)
        for out in results:
            out.all()

    def place_of(k):
        shape = arrays[k].shape
        return pltpu.VMEM((shape[0] + entries[k][2], *shape[1:]), arrays[k].dtype)

    smem, vmem = pl.BlockSpec(memory_space=pltpu.SMEM), pl.BlockSpec(memory_space=pltpu.VMEM)
    specs = [vmem if k else pl.BlockSpec(memory_space=pl.ANY) for k in kept]
    given = [
        pltpu.with_memory_space_constraint(x, pltpu.VMEM) if k else x
        for x, k in zip(arrays[:n], kept)
    ]
    return pl.pallas_call(
        body,
        in_specs=[smem] * len(scalars) + specs[:n],
        out_specs=specs[n:],
        out_shape=[
            pltpu.VMEM(x.shape, x.dtype) if k else x for x, k in zip(arrays[n:], kept[n:])
        ],
        scratch_shapes=[place_of(k) for k in own]
        + [pltpu.SemaphoreType.DMA((entries[k][1],)) for k in own]
        + list(scratch),
        compiler_params=params(),
        cost_estimate=cost(flops),
    )(*scalars, *given)


def params(limit=VMEM_BYTES):
    return pltpu.CompilerParams(vmem_limit_bytes=limit)


def cost(flops):
    return pl.CostEstimate(flops=int(flops), bytes_accessed=4 * MIB, transcendentals=0)


def groups(tiles):
    return tiles.shape[0] // GROUP


def thirds(value):
    first = value.astype(BF16).astype(F32)
    second = (value - first).astype(BF16).astype(F32)
    return first, second, value - first - second


def used_ones(n, most):
    return jnp.concatenate(
        [jnp.full((EDGE, EDGE), jnp.where(t < n, 1.0, 0.0), F32).astype(BF16) for t in range(most)],
        axis=0,
    )


def place_kernel(scalars, ins, outs):
    (count,) = scalars
    peer, row, tiles = ins
    ask, slot_row, slot_column = outs
    mirrors = peer.held.shape[1]
    parts = ask.held.shape[0]
    blocks, most = mirrors // EDGE, tiles.held.shape[1]
    first = count.shape[0] - blocks
    last = tiles.pieces - 1
    tiles.start(last)
    peer = peer.all()[...]
    member = iota((parts, mirrors), 0) == peer
    chosen = jnp.where(member, 1.0, 0.0).astype(BF16)
    earlier = jnp.where(
        iota((mirrors, mirrors), 0) < iota((mirrors, mirrors), 1), 1.0, 0.0
    ).astype(BF16)
    before = dot(chosen, earlier)
    rank = jnp.sum(jnp.where(member, before, 0.0), axis=0, keepdims=True).astype(I32)
    slot = peer * SLOTS + rank
    slot_row.held[...] = slot
    slot_column.held[...] = jnp.transpose(
        jnp.broadcast_to(slot.astype(F32), (EDGE, mirrors))
    ).astype(I32)
    slot_row.start()
    slot_column.start()
    lane = iota((EDGE, mirrors), 0) - rank
    named = row.all()[...] + 1
    degrees = []
    tiles.wait(last)
    for b in range(first, first + blocks):
        flat = jnp.concatenate([tiles.held[b, t] for t in range(most)], axis=1)
        degrees.append(jnp.transpose(dot(flat, used_ones(count[b], most)))[0:1])
    fields = (named // EDGE).astype(F32), (named % EDGE).astype(F32)
    fields += thirds(jnp.concatenate(degrees, axis=1))
    lines = jnp.zeros((EDGE, mirrors), F32)
    for k, field in enumerate(fields):
        lines = jnp.where(lane == SLOTS * k, field, lines)
    ask.held[...] = dot(chosen, lines.astype(BF16), 1, 1)


def place(tile_count, peer, row, tiles, parts):
    mirrors = row.shape[0]
    return run(
        place_kernel,
        (tile_count,),
        ((peer.reshape(1, mirrors), 1), (row.reshape(1, mirrors), 1), (tiles, groups(tiles))),
        (
            (struct(parts, EDGE, dtype=F32), 1, 0),
            (struct(1, mirrors, dtype=I32), 1, 0),
            (struct(mirrors, EDGE, dtype=I32), 1, 0),
        ),
    )


def slot_lines(arrived, slots):
    parts = arrived.shape[0]
    spread = jnp.where(iota((slots, parts), 0) // SLOTS == iota((slots, parts), 1), 1.0, 0.0)
    return dot(spread.astype(BF16), arrived[...].astype(BF16))


def gather(values, asked_column, rows):
    for g in range(rows.pieces):
        at = rows.rows(g)
        pick = pick_columns(asked_column[at, :], 0, values.shape[0])
        rows.held[at, :] = dot(pick, values[...]).astype(BF16)
        rows.start(g)


def to_slots(slot_row, values, send):
    for g in range(send.pieces):
        pick = pick_rows(send.size, g * send.size, slot_row)
        send.held[send.rows(g), :] = dot(pick, values).astype(BF16)
        send.start(g)


def fetch_kernel(scalars, ins, outs):
    arrived, values = ins
    rows, asked_column = outs
    slots = rows.held.shape[0]
    every = slot_lines(arrived.all(), slots)
    lane = iota((slots, EDGE), 1) - iota((slots, EDGE), 0) % SLOTS
    asked = jnp.where(lane == 0, every * EDGE, jnp.where(lane == SLOTS, every, 0.0))
    asked = jnp.sum(asked, axis=1, keepdims=True) - 1.0
    asked_column.held[...] = jnp.broadcast_to(asked, (slots, EDGE)).astype(I32)
    asked_column.start()
    gather(values.all(), asked_column.held, rows)


def fetch(arrived, values, slots):
    return run(
        fetch_kernel,
        (),
        ((arrived, 1), (values, 1)),
        ((struct(slots, values.shape[1]), 2, 0), (struct(slots, EDGE, dtype=I32), 1, 0)),
        flops=2e9,
    )


def flat(tiles, rows, columns):
    lines = [jnp.concatenate([tiles[b, c] for c in columns], axis=1) for b in rows]
    return jnp.concatenate(lines, axis=0)


def densify(count, column, tiles, dense, g, first=0):
    members = range(g * GROUP, (g + 1) * GROUP)
    last = dense.shape[1] - 1
    longest = count[g * GROUP]
    for b in members:
        longest = jnp.maximum(longest, count[b])

    def body(t, carry):
        for b in members:
            c = jnp.where(t < count[b], column[t, b], last)
            dense[b - first, c] = dense[b - first, c] + tiles[b, t]
        return carry

    lax.fori_loop(0, longest, body, 0)


def near_kernel(scalars, ins, outs, dense, far_sems):
    count, column = scalars
    tiles, values = ins
    partial, degree, far = outs
    row_blocks = tiles.held.shape[0]
    last = dense.shape[1] - 1
    cut = last - far.shape[1]

    def far_copy(g):
        at = pl.ds(g * GROUP, GROUP)
        return pltpu.make_async_copy(dense.at[at, pl.ds(cut, last - cut)], far.at[at], far_sems.at[g])

    begin((tiles,), tiles.pieces)
    for b in range(row_blocks):
        dense[b] = jnp.zeros(dense.shape[1:], BF16)
    values = values.all()
    for g in range(tiles.pieces):
        take((tiles,), tiles.pieces, g)
        densify(count, column, tiles.held, dense, g)
        far_copy(g).start()
        for b in range(g * GROUP, (g + 1) * GROUP):
            at = slice(b * EDGE, (b + 1) * EDGE)
            partial.held[at, :] = dot(flat(dense, (b,), range(cut)), values[...])
            if g < degree.pieces:
                weights = dense[b, 0].astype(F32)
                for c in range(1, last):
                    weights += dense[b, c].astype(F32)
                total = jnp.sum(weights, axis=1, keepdims=True)
                degree.held[at, :] = jnp.broadcast_to(total, (EDGE, EDGE))
        partial.start(g)
        if g < degree.pieces:
            degree.start(g)
    for g in range(tiles.pieces):
        far_copy(g).wait()


def near(tile_count, tile_column, tiles, values):
    rows, width = values.shape
    row_blocks = tiles.shape[0]
    masters = rows // EDGE
    return run(
        near_kernel,
        (tile_count, tile_column),
        ((tiles, groups(tiles)), (values, 1)),
        (
            (struct(row_blocks * EDGE, width, dtype=F32), groups(tiles), 0),
            (struct(rows, EDGE, dtype=F32), masters // GROUP, 0),
            (struct(row_blocks, row_blocks - masters, EDGE, EDGE), 0, 0),
        ),
        (
            pltpu.VMEM((row_blocks, row_blocks + 1, EDGE, EDGE), BF16),
            pltpu.SemaphoreType.DMA((groups(tiles),)),
        ),
        flops=5e9,
    )


def mirror_out_kernel(scalars, ins, outs):
    arrived, slot_column, partial, tiles, slot_row = ins
    send, slab = outs
    last = tiles.pieces - 1
    tiles.start(last)
    partial.start(last)
    pick = pick_columns(slot_column.all()[...], 0, arrived.held.shape[0])
    slab.held[...] = dot(pick, arrived.all()[...]).astype(BF16)
    slab.start()
    tiles.wait(last)
    blocks = range(tiles.held.shape[1])
    left = flat(tiles.held, [last * GROUP + b for b in blocks], blocks)
    more = dot(left, slab.held[...])
    partial.wait(last)
    total = (partial.held[partial.rows(last), :] + more).astype(BF16)
    to_slots(slot_row.all()[...], total, send)


def mirror_out(arrived, slot_column, slot_row, partial, tiles):
    slots, width = arrived.shape
    mirrors = slot_row.shape[1]
    return run(
        mirror_out_kernel,
        (),
        (
            (inner(arrived), 1),
            (slot_column, 1),
            (partial, groups(tiles)),
            (tiles, groups(tiles)),
            (slot_row, 1),
        ),
        ((struct(slots, width), 2, 0), (struct(mirrors, width), 1, 0)),
        flops=2e9,
    )


def far_kernel(scalars, ins, outs):
    slab, arrived, asked_column, tiles, partial, own, degree = ins
    base, scale, asked_row = outs
    sources = (tiles, partial, own, degree)
    begin(sources, own.pieces)
    slots = asked_column.held.shape[0]
    asked = jnp.transpose(asked_column.all()[...].astype(F32))[0:8].astype(I32)
    asked_row.held[...] = asked
    asked_row.start()
    lane = iota((slots, EDGE), 1) - iota((slots, EDGE), 0) % SLOTS
    mine = (lane == 2 * SLOTS) | (lane == 3 * SLOTS) | (lane == 4 * SLOTS)
    sums = jnp.sum(jnp.where(mine, slot_lines(arrived.all(), slots), 0.0), axis=1, keepdims=True)
    degrees = jnp.transpose(jnp.broadcast_to(sums, (slots, EDGE)))[0:1]
    slab = slab.all()
    rows = own.size
    for g in range(own.pieces):
        take(sources, own.pieces, g)
        at = own.rows(g)
        left = flat(tiles.held, range(g * GROUP, (g + 1) * GROUP), range(tiles.held.shape[1]))
        total = partial.held[at, :] + dot(left, slab[...])
        hit = iota((rows, slots), 0) + g * rows == asked[0:1]
        more = jnp.sum(jnp.where(hit, degrees, 0.0), axis=1, keepdims=True)
        factor = 1.0 / (1.0 + (degree.held[at, :] + more))
        scale.held[at, :] = factor
        base.held[at, :] = own.held[at, :] + total * jnp.concatenate([factor, factor], axis=1)
        base.start(g)
    scale.start()


def far(tiles, slab, partial, degree, own, arrived, asked_column):
    masters, width = own.shape
    n = masters // EDGE // GROUP
    return run(
        far_kernel,
        (),
        (
            (slab, 1),
            (arrived, 1),
            (asked_column, 1),
            (tiles, groups(tiles)),
            (partial, groups(tiles)),
            (own, n),
            (degree, n),
        ),
        (
            (inner(struct(masters, width, dtype=F32)), n, 0),
            (struct(masters, EDGE, dtype=F32), 1, 0),
            (struct(8, asked_column.shape[0], dtype=I32), 1, 0),
        ),
        flops=5e9,
    )


def turn_kernel(scalars, ins, outs):
    asked_row, back, base, scale, cotangent, asked_column = ins
    mixed, low, spread, send = outs
    for source in (base, scale, cotangent):
        source.start(0)
    asked, back = asked_row.all()[0:1], back.all()
    step = 512
    for g in range(base.held.shape[0] // step):
        if g * step % base.size == 0:
            p = g * step // base.size
            for source in (base, scale, cotangent):
                source.wait(p)
            for source in (base, scale, cotangent, asked_column):
                if p + 1 < source.pieces:
                    source.start(p + 1)
        at = slice(g * step, (g + 1) * step)
        both = jnp.concatenate([scale.held[at, :], scale.held[at, :]], axis=1)
        added = dot(pick_rows(step, g * step, asked), back[...])
        u = base.held[at, :] + added * both
        square = u * u
        bend = jnp.tanh(u * (ROOT + (ROOT * CUBIC) * square))
        half = 0.5 + 0.5 * bend
        mixed.held[at, :] = (u * half).astype(BF16)
        slope = half * (1.0 + u * (1.0 - bend) * (ROOT + (3.0 * ROOT * CUBIC) * square))
        d_pre = cotangent.held[at, :].astype(F32) * slope
        low.held[at, :] = d_pre.astype(BF16)
        spread.held[at, :] = (d_pre * both).astype(BF16)
    asked_column.start(0)
    for out in (spread, low, mixed):
        out.start()
    gather(spread.held, asked_column.all(), send)


def turn(base, scale, cotangent, back, asked_row, asked_column):
    masters, width = base.shape
    return run(
        turn_kernel,
        (),
        (
            (asked_row, 1),
            (back, 1),
            (inner(base), 2),
            (scale, 2),
            (cotangent, 2),
            (asked_column, 2),
        ),
        ((struct(masters, width), 1, 0),) * 3 + ((struct(*back.shape), 2, 0),),
        flops=3e9,
    )


def put_blocks(total, first, value):
    for k in range(value.shape[1] // EDGE):
        total[first + k] = value[:, k * EDGE : (k + 1) * EDGE]


def back_near_kernel(scalars, ins, outs, dense):
    count, column = scalars
    tiles, values = ins
    (total,) = outs
    rows = dense.shape[0]
    begin((tiles,), rows // GROUP)
    for b in range(rows):
        dense[b] = jnp.zeros(dense.shape[1:], BF16)
    turned = jnp.transpose(values.all()[...].astype(F32)).astype(BF16)
    for g in range(rows // GROUP):
        take((tiles,), rows // GROUP, g)
        densify(count, column, tiles.held, dense, g)
    for g in range(total.pieces):
        right = flat(dense, range(rows), range(g * GROUP, (g + 1) * GROUP))
        put_blocks(total.held, g * GROUP, dot(turned, right))
        total.start(g)


def back_near(tile_count, tile_column, tiles, values):
    row_blocks, width = tiles.shape[0], values.shape[1]
    n = groups(tiles)
    (total,) = run(
        back_near_kernel,
        (tile_count, tile_column),
        ((tiles, n), (values, 1)),
        ((struct(row_blocks, width, EDGE, dtype=F32), n, 0),),
        (pltpu.VMEM((values.shape[0] // EDGE, row_blocks + 1, EDGE, EDGE), BF16),),
        flops=5e9,
    )
    return total


def mirror_back_kernel(scalars, ins, outs):
    arrived, slot_column, tiles, partial, slot_row = ins
    send, turned = outs
    last = tiles.pieces - 1
    tiles.start(last)
    partial.start(last)
    pick = pick_columns(slot_column.all()[...], 0, arrived.held.shape[0])
    turned.held[...] = jnp.transpose(dot(pick, arrived.all()[...])).astype(BF16)
    turned.start()
    tiles.wait(last)
    blocks = range(tiles.held.shape[1])
    right = flat(tiles.held, [last * GROUP + b for b in blocks], blocks)
    more = dot(turned.held[...], right)
    partial.wait(last)
    own = jnp.concatenate([partial.held[last * GROUP + c] for c in blocks], axis=1)
    rows = jnp.transpose(own + more).astype(BF16)
    to_slots(slot_row.all()[...], rows, send)


def mirror_back(arrived, slot_column, slot_row, partial, tiles):
    slots, width = arrived.shape
    mirrors = slot_row.shape[1]
    return run(
        mirror_back_kernel,
        (),
        (
            (inner(arrived), 1),
            (slot_column, 1),
            (tiles, groups(tiles)),
            (partial, groups(tiles)),
            (slot_row, 1),
        ),
        ((struct(slots, width), 2, 0), (struct(width, mirrors), 1, 0)),
        flops=2e9,
    )


def back_far_kernel(scalars, ins, outs, dense):
    count, column = scalars
    tiles, turned, partial = ins
    (total,) = outs
    last = tiles.pieces - 1
    tiles.start(last)
    for g in range(total.pieces):
        partial.start(g)
    dense[...] = jnp.zeros(dense.shape, BF16)
    turned = turned.all()
    tiles.wait(last)
    densify(count, column, tiles.held, dense, last, last * GROUP)
    for g in range(total.pieces):
        columns = range(g * GROUP, (g + 1) * GROUP)
        right = flat(dense, range(GROUP), columns)
        partial.wait(g)
        own = jnp.concatenate([partial.held[c] for c in columns], axis=1)
        put_blocks(total.held, g * GROUP, own + dot(turned[...], right))
        total.start(g)


def back_far(tile_count, tile_column, tiles, turned, partial):
    width, mirrors = turned.shape
    row_blocks = tiles.shape[0]
    masters = row_blocks - mirrors // EDGE
    (total,) = run(
        back_far_kernel,
        (tile_count, tile_column),
        ((tiles, groups(tiles)), (turned, 1), (partial, groups(partial))),
        ((inner(struct(masters, width, EDGE, dtype=F32)), masters // GROUP, 0),),
        (pltpu.VMEM((mirrors // EDGE, row_blocks + 1, EDGE, EDGE), BF16),),
        flops=3e9,
    )
    return total


def finish_kernel(scalars, ins, outs):
    (core,) = scalars
    back, asked_column, partial, features, grad_self = ins
    turned, keep, give = outs
    width, masters = turned.held.shape
    inputs = features.held.shape[1]
    step = 512
    flipped = jnp.transpose(back.all()[...].astype(F32)).astype(BF16)
    asked, partial = asked_column.all(), partial.all()
    for g in range(masters // step):
        own = []
        for b in range(g * step // EDGE, (g + 1) * step // EDGE):
            own.append(partial[b])
        added = dot(flipped, pick_columns(asked[...], g * step, step))
        turned.held[:, g * step : (g + 1) * step] = (
            jnp.concatenate(own, axis=1) + added
        ).astype(BF16)
    turned.start()
    total = dot(turned.held[...], features.all()[...])
    grad_self = grad_self.all()
    for h in range(width // EDGE):
        lines = pl.ds(h * inputs, inputs)
        first = grad_self[:, h * EDGE : (h + 1) * EDGE].astype(F32)
        second = jnp.transpose(total[h * EDGE : (h + 1) * EDGE, :])
        keep.held[lines, :] = jnp.where(core[0] == 0, first, second)
        give.held[lines, :] = jnp.where(core[0] == 0, second, first).astype(BF16)


def finish(core, partial, back, asked_column, features, grad_self):
    width = back.shape[1]
    masters, inputs = features.shape
    lines = inputs * width // EDGE
    return run(
        finish_kernel,
        (core,),
        (
            (back, 1),
            (asked_column, 1),
            (inner(partial), 1),
            (features, 1),
            (grad_self, 1),
        ),
        (
            (struct(width, masters), 1, 0),
            (struct(lines, EDGE, dtype=F32), 1, 0),
            (struct(lines, EDGE), 1, 0),
        ),
        flops=3e9,
    )


def input_grads_kernel(scalars, ins, outs):
    low, turned, w_self, w_neigh = ins
    (out,) = outs
    step = out.size
    own, other, low, turned = w_self.all(), w_neigh.all(), low.all(), turned.all()
    for g in range(out.pieces):
        at = slice(g * step, (g + 1) * step)
        d_projected = jnp.transpose(turned[:, at].astype(F32)).astype(BF16)
        value = dot(low[at, :], own[...], 1, 1) + dot(d_projected, other[...], 1, 1)
        out.held[at, :] = value.astype(BF16)
        out.start(g)


def input_grads(low, turned, w_self, w_neigh):
    masters, inputs = low.shape[0], w_self.shape[0]
    (out,) = run(
        input_grads_kernel,
        (),
        ((low, 1), (turned, 1), (w_self, 1), (w_neigh, 1)),
        ((struct(masters, inputs), 2, 0),),
        flops=3e9,
    )
    return out


def share_kernel(parts, out):
    share = jnp.sum(parts[...].astype(F32), axis=0, keepdims=True).astype(BF16)
    out[...] = jnp.broadcast_to(share, out.shape)


def share_out(parts):
    return pl.pallas_call(
        share_kernel,
        out_shape=struct(*parts.shape),
        compiler_params=params(8 * MIB),
        cost_estimate=cost(1e8),
    )(parts)


def unpack_kernel(core, mine, other, first, second):
    inputs = first.shape[0]
    for h in range(2):
        lines, lanes = pl.ds(h * inputs, inputs), pl.ds(h * EDGE, EDGE)
        a, b = mine[lines, :].astype(F32), other[lines, :].astype(F32)
        first[:, lanes] = jnp.where(core[0] == 0, a, b)
        second[:, lanes] = jnp.where(core[0] == 0, b, a)


def unpack(core, mine, other, inputs, width):
    smem, vmem = pl.BlockSpec(memory_space=pltpu.SMEM), pl.BlockSpec(memory_space=pltpu.VMEM)
    return pl.pallas_call(
        unpack_kernel,
        in_specs=[smem, vmem, vmem],
        out_specs=[vmem, vmem],
        out_shape=[struct(inputs, width, dtype=F32)] * 2,
        compiler_params=params(8 * MIB),
        cost_estimate=cost(1e8),
    )(core, mine, other)


def exchange(buffer, axes=EVERY):
    parts = lax.axis_size(axes)
    moved = lax.all_to_all(
        buffer.reshape(parts, buffer.shape[0] // parts, buffer.shape[1]),
        axes,
        split_axis=0,
        concat_axis=0,
        tiled=True,
    )
    return moved.reshape(buffer.shape)


def to_other_core(value):
    return lax.ppermute(value, "core", [(0, 1), (1, 0)])


def on_device(
    features,
    w_self,
    w_neigh,
    mirror_master_part,
    mirror_row,
    tile_count,
    tile_column,
    tile_weight,
    cotangent,
):
    inputs, width = w_neigh.shape
    parts = lax.axis_size(EVERY)
    core = lax.axis_index("core").astype(I32).reshape(1)
    slots = SLOTS * parts
    peer = mirror_master_part[:, 0]
    tile_column = tile_column.T
    ask, slot_row, slot_column = place(tile_count, peer, mirror_row, tile_weight, parts)
    asked = exchange(ask)
    projected = jnp.dot(features, w_neigh, preferred_element_type=F32).astype(BF16)
    own = jnp.dot(features, w_self, preferred_element_type=F32)
    asked, own = lax.optimization_barrier((asked, own))
    asked = pltpu.with_memory_space_constraint(asked, pltpu.HBM)
    rows, asked_column = fetch(asked, projected, slots)
    rows, projected = lax.optimization_barrier((rows, projected))
    arrived = exchange(rows)
    partial, degree, far_tiles = near(tile_count, tile_column, tile_weight, projected)
    send, slab = mirror_out(arrived, slot_column, slot_row, partial, far_tiles)
    back = pltpu.with_memory_space_constraint(exchange(send), pltpu.HBM)
    base, scale, asked_row = far(far_tiles, slab, partial, degree, own, asked, asked_column)
    mixed, low, spread, send = turn(base, scale, cotangent, back, asked_row, asked_column)
    arrived = exchange(send)
    partial = back_near(tile_count, tile_column, tile_weight, spread)
    grad_self = lax.dot_general(
        features, low, (((0,), (0,)), ((), ())), preferred_element_type=F32
    ).astype(BF16)
    send, turned = mirror_back(arrived, slot_column, slot_row, partial, far_tiles)
    back = pltpu.with_memory_space_constraint(exchange(send), pltpu.HBM)
    partial = back_far(tile_count, tile_column, tile_weight, turned, partial)
    d_projected, keep, give = finish(core, partial, back, asked_column, features, grad_self)
    pair = (keep + to_other_core(give).astype(F32)).astype(BF16)
    same = ("chip", "local")
    shares = exchange(pair, same).reshape(lax.axis_size(same), -1, EDGE)
    grad_features = input_grads(low, d_projected, w_self, w_neigh)
    shares, grad_features = lax.optimization_barrier((shares, grad_features))
    mine = exchange(share_out(shares).reshape(pair.shape), same)
    grad_self, grad_neigh = unpack(core, mine, to_other_core(mine), inputs, width)
    return (mixed, grad_features, grad_self, grad_neigh)


def solution(mesh):
    machine, local = mesh.devices.shape
    devices = mesh.devices.reshape(machine // 2, 2, local)
    split, rows = P(EVERY), P(EVERY, None)
    return jax.shard_map(
        on_device,
        mesh=jax.sharding.Mesh(devices, EVERY),
        in_specs=(rows, P(), P(), rows, split, split, rows, P(EVERY, None, None, None), rows),
        out_specs=(rows, rows, P(), P()),
        check_vma=False,
    )
```

```python
import jax
import jax.numpy as jnp
from jax import lax
from jax.experimental import pallas as pl
from jax.experimental.pallas import tpu as pltpu
from jax.sharding import PartitionSpec as P

F32 = jnp.float32
BF16 = jnp.bfloat16
I32 = jnp.int32
EDGE = 128
SLOTS = 8
MIB = 1024 * 1024
VMEM_BYTES = 60 * MIB
GROUP = 4
AHEAD = 2
ROOT = 0.7978845608028654
CUBIC = 0.044715
EVERY = ("chip", "core", "local")


def dot(a, b, ca=1, cb=0):
    return lax.dot_general(a, b, (((ca,), (cb,)), ((), ())), preferred_element_type=F32)


def iota(shape, dim):
    return lax.broadcasted_iota(I32, shape, dim)


def pick_rows(rows, base, row):
    return jnp.where(iota((rows, row.shape[1]), 0) + base == row, 1.0, 0.0).astype(BF16)


def pick_columns(column, base, columns):
    lane = iota(column.shape, 1) + base
    parts = [
        jnp.where(column == lane + EDGE * g, 1.0, 0.0).astype(BF16) for g in range(columns // EDGE)
    ]
    return jnp.concatenate(parts, axis=1)


def struct(*shape, dtype=BF16):
    return jax.ShapeDtypeStruct(shape, dtype)


class Moved:
    def __init__(self, far, held, sems, pieces, inward):
        self.far, self.held, self.sems, self.pieces, self.inward = far, held, sems, pieces, inward
        self.size = far.shape[0] // pieces
        self.started, self.waited = False, False

    def rows(self, p):
        return slice(p * self.size, (p + 1) * self.size)

    def copy(self, p):
        at = pl.ds(p * self.size, self.size)
        ends = self.far.at[at], self.held.at[at]
        return pltpu.make_async_copy(*(ends if self.inward else ends[::-1]), self.sems.at[p])

    def start(self, p=0):
        self.started = True
        self.copy(p).start()

    def wait(self, p=0):
        self.copy(p).wait()

    def all(self):
        if not self.waited:
            for p in range(self.pieces):
                self.wait(p)
        self.waited = True
        return self.held


class Here(Moved):
    def __init__(self, held, pieces):
        self.held, self.pieces = held, pieces
        self.size = held.shape[0] // pieces
        self.waited = True

    def start(self, p=0):
        pass

    def wait(self, p=0):
        pass


def inner(array):
    return ("inner", array)


def begin(sources, pieces):
    for g in range(min(AHEAD, pieces)):
        for source in sources:
            source.start(g)


def take(sources, pieces, g):
    for source in sources:
        source.wait(g)
    if g + AHEAD < pieces:
        for source in sources:
            source.start(g + AHEAD)


def run(kernel, scalars, ins, outs, scratch=(), flops=1e9):
    entries = [(x, pieces, 0) for x, pieces in ins] + list(outs)
    n = len(ins)
    kept = [isinstance(entry[0], tuple) for entry in entries]
    arrays = [entry[0][1] if k else entry[0] for entry, k in zip(entries, kept)]
    own = [k for k, entry in enumerate(entries) if entry[1] and not kept[k]]

    def body(*refs):
        scalar_refs, refs = refs[: len(scalars)], refs[len(scalars) :]
        far, refs = list(refs[: len(entries)]), refs[len(entries) :]
        held, sems, rest = refs[: len(own)], refs[len(own) : 2 * len(own)], refs[2 * len(own) :]
        for k, entry in enumerate(entries):
            if kept[k]:
                far[k] = Here(far[k], entry[1])
        for at, k in enumerate(own):
            far[k] = Moved(far[k], held[at], sems[at], entries[k][1], k < n)
            if k < n and entries[k][1] == 1:
                far[k].start()
        kernel(scalar_refs, far[:n], far[n:], *rest)
        results = [far[k] for k in own if k >= n]
        for out in results:
            if not out.started:
                for p in range(out.pieces):
                    out.start(p)
        for out in results:
            out.all()

    def place_of(k):
        shape = arrays[k].shape
        return pltpu.VMEM((shape[0] + entries[k][2], *shape[1:]), arrays[k].dtype)

    smem, vmem = pl.BlockSpec(memory_space=pltpu.SMEM), pl.BlockSpec(memory_space=pltpu.VMEM)
    specs = [vmem if k else pl.BlockSpec(memory_space=pl.ANY) for k in kept]
    given = [
        pltpu.with_memory_space_constraint(x, pltpu.VMEM) if k else x
        for x, k in zip(arrays[:n], kept)
    ]
    return pl.pallas_call(
        body,
        in_specs=[smem] * len(scalars) + specs[:n],
        out_specs=specs[n:],
        out_shape=[
            pltpu.VMEM(x.shape, x.dtype) if k else x for x, k in zip(arrays[n:], kept[n:])
        ],
        scratch_shapes=[place_of(k) for k in own]
        + [pltpu.SemaphoreType.DMA((entries[k][1],)) for k in own]
        + list(scratch),
        compiler_params=params(),
        cost_estimate=cost(flops),
    )(*scalars, *given)


def params(limit=VMEM_BYTES):
    return pltpu.CompilerParams(vmem_limit_bytes=limit)


def cost(flops):
    return pl.CostEstimate(flops=int(flops), bytes_accessed=4 * MIB, transcendentals=0)


def groups(tiles):
    return tiles.shape[0] // GROUP


def thirds(value):
    first = value.astype(BF16).astype(F32)
    second = (value - first).astype(BF16).astype(F32)
    return first, second, value - first - second


def used_ones(n, most):
    return jnp.concatenate(
        [jnp.full((EDGE, EDGE), jnp.where(t < n, 1.0, 0.0), F32).astype(BF16) for t in range(most)],
        axis=0,
    )


def place_kernel(scalars, ins, outs):
    (count,) = scalars
    peer, row, tiles = ins
    ask, slot_row, slot_column = outs
    mirrors = peer.held.shape[1]
    parts = ask.held.shape[0]
    blocks, most = mirrors // EDGE, tiles.held.shape[1]
    first = count.shape[0] - blocks
    last = tiles.pieces - 1
    tiles.start(last)
    peer = peer.all()[...]
    member = iota((parts, mirrors), 0) == peer
    chosen = jnp.where(member, 1.0, 0.0).astype(BF16)
    earlier = jnp.where(
        iota((mirrors, mirrors), 0) < iota((mirrors, mirrors), 1), 1.0, 0.0
    ).astype(BF16)
    before = dot(chosen, earlier)
    rank = jnp.sum(jnp.where(member, before, 0.0), axis=0, keepdims=True).astype(I32)
    slot = peer * SLOTS + rank
    slot_row.held[...] = slot
    slot_column.held[...] = jnp.transpose(
        jnp.broadcast_to(slot.astype(F32), (EDGE, mirrors))
    ).astype(I32)
    slot_row.start()
    slot_column.start()
    lane = iota((EDGE, mirrors), 0) - rank
    named = row.all()[...] + 1
    degrees = []
    tiles.wait(last)
    for b in range(first, first + blocks):
        flat = jnp.concatenate([tiles.held[b, t] for t in range(most)], axis=1)
        degrees.append(jnp.transpose(dot(flat, used_ones(count[b], most)))[0:1])
    fields = (named // EDGE).astype(F32), (named % EDGE).astype(F32)
    fields += thirds(jnp.concatenate(degrees, axis=1))
    lines = jnp.zeros((EDGE, mirrors), F32)
    for k, field in enumerate(fields):
        lines = jnp.where(lane == SLOTS * k, field, lines)
    ask.held[...] = dot(chosen, lines.astype(BF16), 1, 1)


def place(tile_count, peer, row, tiles, parts):
    mirrors = row.shape[0]
    return run(
        place_kernel,
        (tile_count,),
        ((peer.reshape(1, mirrors), 1), (row.reshape(1, mirrors), 1), (tiles, groups(tiles))),
        (
            (struct(parts, EDGE, dtype=F32), 1, 0),
            (struct(1, mirrors, dtype=I32), 1, 0),
            (struct(mirrors, EDGE, dtype=I32), 1, 0),
        ),
    )


def slot_lines(arrived, slots):
    parts = arrived.shape[0]
    spread = jnp.where(iota((slots, parts), 0) // SLOTS == iota((slots, parts), 1), 1.0, 0.0)
    return dot(spread.astype(BF16), arrived[...].astype(BF16))


def gather(values, asked_column, rows):
    for g in range(rows.pieces):
        at = rows.rows(g)
        pick = pick_columns(asked_column[at, :], 0, values.shape[0])
        rows.held[at, :] = dot(pick, values[...]).astype(BF16)
        rows.start(g)


def to_slots(slot_row, values, send):
    for g in range(send.pieces):
        pick = pick_rows(send.size, g * send.size, slot_row)
        send.held[send.rows(g), :] = dot(pick, values).astype(BF16)
        send.start(g)


def fetch_kernel(scalars, ins, outs):
    arrived, values = ins
    rows, asked_column = outs
    slots = rows.held.shape[0]
    every = slot_lines(arrived.all(), slots)
    lane = iota((slots, EDGE), 1) - iota((slots, EDGE), 0) % SLOTS
    asked = jnp.where(lane == 0, every * EDGE, jnp.where(lane == SLOTS, every, 0.0))
    asked = jnp.sum(asked, axis=1, keepdims=True) - 1.0
    asked_column.held[...] = jnp.broadcast_to(asked, (slots, EDGE)).astype(I32)
    asked_column.start()
    gather(values.all(), asked_column.held, rows)


def fetch(arrived, values, slots):
    return run(
        fetch_kernel,
        (),
        ((arrived, 1), (values, 1)),
        ((struct(slots, values.shape[1]), 2, 0), (struct(slots, EDGE, dtype=I32), 1, 0)),
        flops=2e9,
    )


def flat(tiles, rows, columns):
    lines = [jnp.concatenate([tiles[b, c] for c in columns], axis=1) for b in rows]
    return jnp.concatenate(lines, axis=0)


def densify(count, column, tiles, dense, g, first=0):
    members = range(g * GROUP, (g + 1) * GROUP)
    last = dense.shape[1] - 1
    longest = count[g * GROUP]
    for b in members:
        longest = jnp.maximum(longest, count[b])

    def body(t, carry):
        for b in members:
            c = jnp.where(t < count[b], column[t, b], last)
            dense[b - first, c] = dense[b - first, c] + tiles[b, t]
        return carry

    lax.fori_loop(0, longest, body, 0)


def near_kernel(scalars, ins, outs, dense, far_sems):
    count, column = scalars
    tiles, values = ins
    partial, degree, far = outs
    row_blocks = tiles.held.shape[0]
    last = dense.shape[1] - 1
    cut = last - far.shape[1]

    def far_copy(g):
        at = pl.ds(g * GROUP, GROUP)
        return pltpu.make_async_copy(dense.at[at, pl.ds(cut, last - cut)], far.at[at], far_sems.at[g])

    begin((tiles,), tiles.pieces)
    for b in range(row_blocks):
        dense[b] = jnp.zeros(dense.shape[1:], BF16)
    values = values.all()
    for g in range(tiles.pieces):
        take((tiles,), tiles.pieces, g)
        densify(count, column, tiles.held, dense, g)
        far_copy(g).start()
        for b in range(g * GROUP, (g + 1) * GROUP):
            at = slice(b * EDGE, (b + 1) * EDGE)
            partial.held[at, :] = dot(flat(dense, (b,), range(cut)), values[...])
            if g < degree.pieces:
                weights = dense[b, 0].astype(F32)
                for c in range(1, last):
                    weights += dense[b, c].astype(F32)
                total = jnp.sum(weights, axis=1, keepdims=True)
                degree.held[at, :] = jnp.broadcast_to(total, (EDGE, EDGE))
        partial.start(g)
        if g < degree.pieces:
            degree.start(g)
    for g in range(tiles.pieces):
        far_copy(g).wait()


def near(tile_count, tile_column, tiles, values):
    rows, width = values.shape
    row_blocks = tiles.shape[0]
    masters = rows // EDGE
    return run(
        near_kernel,
        (tile_count, tile_column),
        ((tiles, groups(tiles)), (values, 1)),
        (
            (struct(row_blocks * EDGE, width, dtype=F32), groups(tiles), 0),
            (struct(rows, EDGE, dtype=F32), masters // GROUP, 0),
            (struct(row_blocks, row_blocks - masters, EDGE, EDGE), 0, 0),
        ),
        (
            pltpu.VMEM((row_blocks, row_blocks + 1, EDGE, EDGE), BF16),
            pltpu.SemaphoreType.DMA((groups(tiles),)),
        ),
        flops=5e9,
    )


def mirror_out_kernel(scalars, ins, outs):
    arrived, slot_column, partial, tiles, slot_row = ins
    send, slab = outs
    last = tiles.pieces - 1
    tiles.start(last)
    partial.start(last)
    pick = pick_columns(slot_column.all()[...], 0, arrived.held.shape[0])
    slab.held[...] = dot(pick, arrived.all()[...]).astype(BF16)
    slab.start()
    tiles.wait(last)
    blocks = range(tiles.held.shape[1])
    left = flat(tiles.held, [last * GROUP + b for b in blocks], blocks)
    more = dot(left, slab.held[...])
    partial.wait(last)
    total = (partial.held[partial.rows(last), :] + more).astype(BF16)
    to_slots(slot_row.all()[...], total, send)


def mirror_out(arrived, slot_column, slot_row, partial, tiles):
    slots, width = arrived.shape
    mirrors = slot_row.shape[1]
    return run(
        mirror_out_kernel,
        (),
        (
            (inner(arrived), 1),
            (slot_column, 1),
            (partial, groups(tiles)),
            (tiles, groups(tiles)),
            (slot_row, 1),
        ),
        ((struct(slots, width), 2, 0), (struct(mirrors, width), 1, 0)),
        flops=2e9,
    )


def far_kernel(scalars, ins, outs):
    slab, arrived, asked_column, tiles, partial, own, degree = ins
    base, scale, asked_row = outs
    sources = (tiles, partial, own, degree)
    begin(sources, own.pieces)
    slots = asked_column.held.shape[0]
    asked = jnp.transpose(asked_column.all()[...].astype(F32))[0:8].astype(I32)
    asked_row.held[...] = asked
    asked_row.start()
    lane = iota((slots, EDGE), 1) - iota((slots, EDGE), 0) % SLOTS
    mine = (lane == 2 * SLOTS) | (lane == 3 * SLOTS) | (lane == 4 * SLOTS)
    sums = jnp.sum(jnp.where(mine, slot_lines(arrived.all(), slots), 0.0), axis=1, keepdims=True)
    degrees = jnp.transpose(jnp.broadcast_to(sums, (slots, EDGE)))[0:1]
    slab = slab.all()
    rows = own.size
    for g in range(own.pieces):
        take(sources, own.pieces, g)
        at = own.rows(g)
        left = flat(tiles.held, range(g * GROUP, (g + 1) * GROUP), range(tiles.held.shape[1]))
        total = partial.held[at, :] + dot(left, slab[...])
        hit = iota((rows, slots), 0) + g * rows == asked[0:1]
        more = jnp.sum(jnp.where(hit, degrees, 0.0), axis=1, keepdims=True)
        factor = 1.0 / (1.0 + (degree.held[at, :] + more))
        scale.held[at, :] = factor
        base.held[at, :] = own.held[at, :] + total * jnp.concatenate([factor, factor], axis=1)
        base.start(g)
    scale.start()


def far(tiles, slab, partial, degree, own, arrived, asked_column):
    masters, width = own.shape
    n = masters // EDGE // GROUP
    return run(
        far_kernel,
        (),
        (
            (slab, 1),
            (arrived, 1),
            (asked_column, 1),
            (tiles, groups(tiles)),
            (partial, groups(tiles)),
            (own, n),
            (degree, n),
        ),
        (
            (struct(masters, width, dtype=F32), n, 0),
            (struct(masters, EDGE, dtype=F32), 1, 0),
            (struct(8, asked_column.shape[0], dtype=I32), 1, 0),
        ),
        flops=5e9,
    )


def turn_kernel(scalars, ins, outs):
    asked_row, back, base, scale, cotangent, asked_column = ins
    mixed, low, spread, send = outs
    for source in (base, scale, cotangent):
        source.start(0)
    asked, back = asked_row.all()[0:1], back.all()
    step = 512
    for g in range(base.held.shape[0] // step):
        if g * step % base.size == 0:
            p = g * step // base.size
            for source in (base, scale, cotangent):
                source.wait(p)
            for source in (base, scale, cotangent, asked_column):
                if p + 1 < source.pieces:
                    source.start(p + 1)
        at = slice(g * step, (g + 1) * step)
        both = jnp.concatenate([scale.held[at, :], scale.held[at, :]], axis=1)
        added = dot(pick_rows(step, g * step, asked), back[...])
        u = base.held[at, :] + added * both
        square = u * u
        bend = jnp.tanh(u * (ROOT + (ROOT * CUBIC) * square))
        half = 0.5 + 0.5 * bend
        mixed.held[at, :] = (u * half).astype(BF16)
        slope = half * (1.0 + u * (1.0 - bend) * (ROOT + (3.0 * ROOT * CUBIC) * square))
        d_pre = cotangent.held[at, :].astype(F32) * slope
        low.held[at, :] = d_pre.astype(BF16)
        spread.held[at, :] = (d_pre * both).astype(BF16)
    asked_column.start(0)
    for out in (spread, low, mixed):
        out.start()
    gather(spread.held, asked_column.all(), send)


def turn(base, scale, cotangent, back, asked_row, asked_column):
    masters, width = base.shape
    return run(
        turn_kernel,
        (),
        (
            (asked_row, 1),
            (inner(back), 1),
            (base, 2),
            (scale, 2),
            (cotangent, 2),
            (asked_column, 2),
        ),
        ((struct(masters, width), 1, 0),) * 3 + ((struct(*back.shape), 2, 0),),
        flops=3e9,
    )


def put_blocks(total, first, value):
    for k in range(value.shape[1] // EDGE):
        total[first + k] = value[:, k * EDGE : (k + 1) * EDGE]


def back_near_kernel(scalars, ins, outs, dense):
    count, column = scalars
    tiles, values = ins
    (total,) = outs
    rows = dense.shape[0]
    begin((tiles,), rows // GROUP)
    for b in range(rows):
        dense[b] = jnp.zeros(dense.shape[1:], BF16)
    turned = jnp.transpose(values.all()[...].astype(F32)).astype(BF16)
    for g in range(rows // GROUP):
        take((tiles,), rows // GROUP, g)
        densify(count, column, tiles.held, dense, g)
    for g in range(total.pieces):
        right = flat(dense, range(rows), range(g * GROUP, (g + 1) * GROUP))
        put_blocks(total.held, g * GROUP, dot(turned, right))
        total.start(g)


def back_near(tile_count, tile_column, tiles, values):
    row_blocks, width = tiles.shape[0], values.shape[1]
    n = groups(tiles)
    (total,) = run(
        back_near_kernel,
        (tile_count, tile_column),
        ((tiles, n), (values, 1)),
        ((struct(row_blocks, width, EDGE, dtype=F32), n, 0),),
        (pltpu.VMEM((values.shape[0] // EDGE, row_blocks + 1, EDGE, EDGE), BF16),),
        flops=5e9,
    )
    return total


def mirror_back_kernel(scalars, ins, outs):
    arrived, slot_column, tiles, partial, slot_row = ins
    send, turned = outs
    last = tiles.pieces - 1
    tiles.start(last)
    partial.start(last)
    pick = pick_columns(slot_column.all()[...], 0, arrived.held.shape[0])
    turned.held[...] = jnp.transpose(dot(pick, arrived.all()[...])).astype(BF16)
    turned.start()
    tiles.wait(last)
    blocks = range(tiles.held.shape[1])
    right = flat(tiles.held, [last * GROUP + b for b in blocks], blocks)
    more = dot(turned.held[...], right)
    partial.wait(last)
    own = jnp.concatenate([partial.held[last * GROUP + c] for c in blocks], axis=1)
    rows = jnp.transpose(own + more).astype(BF16)
    to_slots(slot_row.all()[...], rows, send)


def mirror_back(arrived, slot_column, slot_row, partial, tiles):
    slots, width = arrived.shape
    mirrors = slot_row.shape[1]
    return run(
        mirror_back_kernel,
        (),
        (
            (inner(arrived), 1),
            (slot_column, 1),
            (tiles, groups(tiles)),
            (partial, groups(tiles)),
            (slot_row, 1),
        ),
        ((struct(slots, width), 2, 0), (struct(width, mirrors), 1, 0)),
        flops=2e9,
    )


def back_far_kernel(scalars, ins, outs, dense):
    count, column = scalars
    tiles, turned, partial = ins
    (total,) = outs
    last = tiles.pieces - 1
    tiles.start(last)
    for g in range(total.pieces):
        partial.start(g)
    dense[...] = jnp.zeros(dense.shape, BF16)
    turned = turned.all()
    tiles.wait(last)
    densify(count, column, tiles.held, dense, last, last * GROUP)
    for g in range(total.pieces):
        columns = range(g * GROUP, (g + 1) * GROUP)
        right = flat(dense, range(GROUP), columns)
        partial.wait(g)
        own = jnp.concatenate([partial.held[c] for c in columns], axis=1)
        put_blocks(total.held, g * GROUP, own + dot(turned[...], right))
        total.start(g)


def back_far(tile_count, tile_column, tiles, turned, partial):
    width, mirrors = turned.shape
    row_blocks = tiles.shape[0]
    masters = row_blocks - mirrors // EDGE
    (total,) = run(
        back_far_kernel,
        (tile_count, tile_column),
        ((tiles, groups(tiles)), (turned, 1), (partial, groups(partial))),
        ((struct(masters, width, EDGE, dtype=F32), masters // GROUP, 0),),
        (pltpu.VMEM((mirrors // EDGE, row_blocks + 1, EDGE, EDGE), BF16),),
        flops=3e9,
    )
    return total


def finish_kernel(scalars, ins, outs):
    (core,) = scalars
    back, asked_column, partial, features, grad_self = ins
    turned, keep, give = outs
    width, masters = turned.held.shape
    inputs = features.held.shape[1]
    step = 512
    flipped = jnp.transpose(back.all()[...].astype(F32)).astype(BF16)
    asked, partial = asked_column.all(), partial.all()
    for g in range(masters // step):
        own = []
        for b in range(g * step // EDGE, (g + 1) * step // EDGE):
            own.append(partial[b])
        added = dot(flipped, pick_columns(asked[...], g * step, step))
        turned.held[:, g * step : (g + 1) * step] = (
            jnp.concatenate(own, axis=1) + added
        ).astype(BF16)
    turned.start()
    total = dot(turned.held[...], features.all()[...])
    grad_self = grad_self.all()
    for h in range(width // EDGE):
        lines = pl.ds(h * inputs, inputs)
        first = grad_self[:, h * EDGE : (h + 1) * EDGE].astype(F32)
        second = jnp.transpose(total[h * EDGE : (h + 1) * EDGE, :])
        keep.held[lines, :] = jnp.where(core[0] == 0, first, second)
        give.held[lines, :] = jnp.where(core[0] == 0, second, first).astype(BF16)


def finish(core, partial, back, asked_column, features, grad_self):
    width = back.shape[1]
    masters, inputs = features.shape
    lines = inputs * width // EDGE
    return run(
        finish_kernel,
        (core,),
        (
            (inner(back), 1),
            (asked_column, 1),
            (partial, 1),
            (features, 1),
            (grad_self, 1),
        ),
        (
            (struct(width, masters), 1, 0),
            (struct(lines, EDGE, dtype=F32), 1, 0),
            (struct(lines, EDGE), 1, 0),
        ),
        flops=3e9,
    )


def input_grads_kernel(scalars, ins, outs):
    low, turned, w_self, w_neigh = ins
    (out,) = outs
    step = out.size
    own, other, low, turned = w_self.all(), w_neigh.all(), low.all(), turned.all()
    for g in range(out.pieces):
        at = slice(g * step, (g + 1) * step)
        d_projected = jnp.transpose(turned[:, at].astype(F32)).astype(BF16)
        value = dot(low[at, :], own[...], 1, 1) + dot(d_projected, other[...], 1, 1)
        out.held[at, :] = value.astype(BF16)
        out.start(g)


def input_grads(low, turned, w_self, w_neigh):
    masters, inputs = low.shape[0], w_self.shape[0]
    (out,) = run(
        input_grads_kernel,
        (),
        ((low, 1), (turned, 1), (w_self, 1), (w_neigh, 1)),
        ((struct(masters, inputs), 2, 0),),
        flops=3e9,
    )
    return out


def share_kernel(parts, out):
    share = jnp.sum(parts[...].astype(F32), axis=0, keepdims=True).astype(BF16)
    out[...] = jnp.broadcast_to(share, out.shape)


def share_out(parts):
    return pl.pallas_call(
        share_kernel,
        out_shape=struct(*parts.shape),
        compiler_params=params(8 * MIB),
        cost_estimate=cost(1e8),
    )(parts)


def unpack_kernel(core, mine, other, first, second):
    inputs = first.shape[0]
    for h in range(2):
        lines, lanes = pl.ds(h * inputs, inputs), pl.ds(h * EDGE, EDGE)
        a, b = mine[lines, :].astype(F32), other[lines, :].astype(F32)
        first[:, lanes] = jnp.where(core[0] == 0, a, b)
        second[:, lanes] = jnp.where(core[0] == 0, b, a)


def unpack(core, mine, other, inputs, width):
    smem, vmem = pl.BlockSpec(memory_space=pltpu.SMEM), pl.BlockSpec(memory_space=pltpu.VMEM)
    return pl.pallas_call(
        unpack_kernel,
        in_specs=[smem, vmem, vmem],
        out_specs=[vmem, vmem],
        out_shape=[struct(inputs, width, dtype=F32)] * 2,
        compiler_params=params(8 * MIB),
        cost_estimate=cost(1e8),
    )(core, mine, other)


def exchange(buffer, axes=EVERY):
    parts = lax.axis_size(axes)
    moved = lax.all_to_all(
        buffer.reshape(parts, buffer.shape[0] // parts, buffer.shape[1]),
        axes,
        split_axis=0,
        concat_axis=0,
        tiled=True,
    )
    return moved.reshape(buffer.shape)


def to_other_core(value):
    return lax.ppermute(value, "core", [(0, 1), (1, 0)])


def on_device(
    features,
    w_self,
    w_neigh,
    mirror_master_part,
    mirror_row,
    tile_count,
    tile_column,
    tile_weight,
    cotangent,
):
    inputs, width = w_neigh.shape
    parts = lax.axis_size(EVERY)
    core = lax.axis_index("core").astype(I32).reshape(1)
    slots = SLOTS * parts
    peer = mirror_master_part[:, 0]
    tile_column = tile_column.T
    ask, slot_row, slot_column = place(tile_count, peer, mirror_row, tile_weight, parts)
    asked = exchange(ask)
    projected = jnp.dot(features, w_neigh, preferred_element_type=F32).astype(BF16)
    own = jnp.dot(features, w_self, preferred_element_type=F32)
    asked, own = lax.optimization_barrier((asked, own))
    asked = pltpu.with_memory_space_constraint(asked, pltpu.HBM)
    rows, asked_column = fetch(asked, projected, slots)
    rows, projected = lax.optimization_barrier((rows, projected))
    arrived = exchange(rows)
    partial, degree, far_tiles = near(tile_count, tile_column, tile_weight, projected)
    send, slab = mirror_out(arrived, slot_column, slot_row, partial, far_tiles)
    back = exchange(send)
    base, scale, asked_row = far(far_tiles, slab, partial, degree, own, asked, asked_column)
    mixed, low, spread, send = turn(base, scale, cotangent, back, asked_row, asked_column)
    arrived = exchange(send)
    partial = back_near(tile_count, tile_column, tile_weight, spread)
    grad_self = lax.dot_general(
        features, low, (((0,), (0,)), ((), ())), preferred_element_type=F32
    ).astype(BF16)
    send, turned = mirror_back(arrived, slot_column, slot_row, partial, far_tiles)
    back = exchange(send)
    partial = back_far(tile_count, tile_column, tile_weight, turned, partial)
    d_projected, keep, give = finish(core, partial, back, asked_column, features, grad_self)
    pair = (keep + to_other_core(give).astype(F32)).astype(BF16)
    same = ("chip", "local")
    shares = exchange(pair, same).reshape(lax.axis_size(same), -1, EDGE)
    grad_features = input_grads(low, d_projected, w_self, w_neigh)
    shares, grad_features = lax.optimization_barrier((shares, grad_features))
    mine = exchange(share_out(shares).reshape(pair.shape), same)
    grad_self, grad_neigh = unpack(core, mine, to_other_core(mine), inputs, width)
    return (mixed, grad_features, grad_self, grad_neigh)


def solution(mesh):
    machine, local = mesh.devices.shape
    devices = mesh.devices.reshape(machine // 2, 2, local)
    split, rows = P(EVERY), P(EVERY, None)
    return jax.shard_map(
        on_device,
        mesh=jax.sharding.Mesh(devices, EVERY),
        in_specs=(rows, P(), P(), rows, split, split, rows, P(EVERY, None, None, None), rows),
        out_specs=(rows, rows, P(), P()),
        check_vma=False,
    )
```

```python
import jax
import jax.numpy as jnp
from jax import lax
from jax.experimental import pallas as pl
from jax.experimental.pallas import tpu as pltpu
from jax.sharding import PartitionSpec as P

F32 = jnp.float32
BF16 = jnp.bfloat16
I32 = jnp.int32
EDGE = 128
SLOTS = 8
MIB = 1024 * 1024
VMEM_BYTES = 60 * MIB
GROUP = 4
AHEAD = 2
ROOT = 0.7978845608028654
CUBIC = 0.044715
EVERY = ("chip", "core", "local")


def dot(a, b, ca=1, cb=0):
    return lax.dot_general(a, b, (((ca,), (cb,)), ((), ())), preferred_element_type=F32)


def iota(shape, dim):
    return lax.broadcasted_iota(I32, shape, dim)


def pick_rows(rows, base, row):
    return jnp.where(iota((rows, row.shape[1]), 0) + base == row, 1.0, 0.0).astype(BF16)


def pick_columns(column, base, columns):
    lane = iota(column.shape, 1) + base
    parts = [
        jnp.where(column == lane + EDGE * g, 1.0, 0.0).astype(BF16) for g in range(columns // EDGE)
    ]
    return jnp.concatenate(parts, axis=1)


def struct(*shape, dtype=BF16):
    return jax.ShapeDtypeStruct(shape, dtype)


class Moved:
    def __init__(self, far, held, sems, pieces, inward):
        self.far, self.held, self.sems, self.pieces, self.inward = far, held, sems, pieces, inward
        self.size = far.shape[0] // pieces
        self.started, self.waited = False, False

    def rows(self, p):
        return slice(p * self.size, (p + 1) * self.size)

    def copy(self, p):
        at = pl.ds(p * self.size, self.size)
        ends = self.far.at[at], self.held.at[at]
        return pltpu.make_async_copy(*(ends if self.inward else ends[::-1]), self.sems.at[p])

    def start(self, p=0):
        self.started = True
        self.copy(p).start()

    def wait(self, p=0):
        self.copy(p).wait()

    def all(self):
        if not self.waited:
            for p in range(self.pieces):
                self.wait(p)
        self.waited = True
        return self.held


class Here(Moved):
    def __init__(self, held, pieces):
        self.held, self.pieces = held, pieces
        self.size = held.shape[0] // pieces
        self.waited = True

    def start(self, p=0):
        pass

    def wait(self, p=0):
        pass


def inner(array):
    return ("inner", array)


def begin(sources, pieces):
    for g in range(min(AHEAD, pieces)):
        for source in sources:
            source.start(g)


def take(sources, pieces, g):
    for source in sources:
        source.wait(g)
    if g + AHEAD < pieces:
        for source in sources:
            source.start(g + AHEAD)


def run(kernel, scalars, ins, outs, scratch=(), flops=1e9):
    entries = [(x, pieces, 0) for x, pieces in ins] + list(outs)
    n = len(ins)
    kept = [isinstance(entry[0], tuple) for entry in entries]
    arrays = [entry[0][1] if k else entry[0] for entry, k in zip(entries, kept)]
    own = [k for k, entry in enumerate(entries) if entry[1] and not kept[k]]

    def body(*refs):
        scalar_refs, refs = refs[: len(scalars)], refs[len(scalars) :]
        far, refs = list(refs[: len(entries)]), refs[len(entries) :]
        held, sems, rest = refs[: len(own)], refs[len(own) : 2 * len(own)], refs[2 * len(own) :]
        for k, entry in enumerate(entries):
            if kept[k]:
                far[k] = Here(far[k], entry[1])
        for at, k in enumerate(own):
            far[k] = Moved(far[k], held[at], sems[at], entries[k][1], k < n)
            if k < n and entries[k][1] == 1:
                far[k].start()
        kernel(scalar_refs, far[:n], far[n:], *rest)
        results = [far[k] for k in own if k >= n]
        for out in results:
            if not out.started:
                for p in range(out.pieces):
                    out.start(p)
        for out in results:
            out.all()

    def place_of(k):
        shape = arrays[k].shape
        return pltpu.VMEM((shape[0] + entries[k][2], *shape[1:]), arrays[k].dtype)

    smem, vmem = pl.BlockSpec(memory_space=pltpu.SMEM), pl.BlockSpec(memory_space=pltpu.VMEM)
    specs = [vmem if k else pl.BlockSpec(memory_space=pl.ANY) for k in kept]
    given = [
        pltpu.with_memory_space_constraint(x, pltpu.VMEM) if k else x
        for x, k in zip(arrays[:n], kept)
    ]
    return pl.pallas_call(
        body,
        in_specs=[smem] * len(scalars) + specs[:n],
        out_specs=specs[n:],
        out_shape=[
            pltpu.VMEM(x.shape, x.dtype) if k else x for x, k in zip(arrays[n:], kept[n:])
        ],
        scratch_shapes=[place_of(k) for k in own]
        + [pltpu.SemaphoreType.DMA((entries[k][1],)) for k in own]
        + list(scratch),
        compiler_params=params(),
        cost_estimate=cost(flops),
    )(*scalars, *given)


def params(limit=VMEM_BYTES):
    return pltpu.CompilerParams(vmem_limit_bytes=limit)


def cost(flops):
    return pl.CostEstimate(flops=int(flops), bytes_accessed=4 * MIB, transcendentals=0)


def groups(tiles):
    return tiles.shape[0] // GROUP


def thirds(value):
    first = value.astype(BF16).astype(F32)
    second = (value - first).astype(BF16).astype(F32)
    return first, second, value - first - second


def used_ones(n, most):
    return jnp.concatenate(
        [jnp.full((EDGE, EDGE), jnp.where(t < n, 1.0, 0.0), F32).astype(BF16) for t in range(most)],
        axis=0,
    )


def place_kernel(scalars, ins, outs):
    (count,) = scalars
    peer, row, tiles = ins
    ask, slot_row, slot_column = outs
    mirrors = peer.held.shape[1]
    parts = ask.held.shape[0]
    blocks, most = mirrors // EDGE, tiles.held.shape[1]
    first = count.shape[0] - blocks
    last = tiles.pieces - 1
    tiles.start(last)
    peer = peer.all()[...]
    member = iota((parts, mirrors), 0) == peer
    chosen = jnp.where(member, 1.0, 0.0).astype(BF16)
    earlier = jnp.where(
        iota((mirrors, mirrors), 0) < iota((mirrors, mirrors), 1), 1.0, 0.0
    ).astype(BF16)
    before = dot(chosen, earlier)
    rank = jnp.sum(jnp.where(member, before, 0.0), axis=0, keepdims=True).astype(I32)
    slot = peer * SLOTS + rank
    slot_row.held[...] = slot
    slot_column.held[...] = jnp.transpose(
        jnp.broadcast_to(slot.astype(F32), (EDGE, mirrors))
    ).astype(I32)
    slot_row.start()
    slot_column.start()
    lane = iota((EDGE, mirrors), 0) - rank
    named = row.all()[...] + 1
    degrees = []
    tiles.wait(last)
    for b in range(first, first + blocks):
        flat = jnp.concatenate([tiles.held[b, t] for t in range(most)], axis=1)
        degrees.append(jnp.transpose(dot(flat, used_ones(count[b], most)))[0:1])
    fields = (named // EDGE).astype(F32), (named % EDGE).astype(F32)
    fields += thirds(jnp.concatenate(degrees, axis=1))
    lines = jnp.zeros((EDGE, mirrors), F32)
    for k, field in enumerate(fields):
        lines = jnp.where(lane == SLOTS * k, field, lines)
    ask.held[...] = dot(chosen, lines.astype(BF16), 1, 1)


def place(tile_count, peer, row, tiles, parts):
    mirrors = row.shape[0]
    return run(
        place_kernel,
        (tile_count,),
        ((peer.reshape(1, mirrors), 1), (row.reshape(1, mirrors), 1), (tiles, groups(tiles))),
        (
            (struct(parts, EDGE, dtype=F32), 1, 0),
            (struct(1, mirrors, dtype=I32), 1, 0),
            (struct(mirrors, EDGE, dtype=I32), 1, 0),
        ),
    )


def slot_lines(arrived, slots):
    parts = arrived.shape[0]
    spread = jnp.where(iota((slots, parts), 0) // SLOTS == iota((slots, parts), 1), 1.0, 0.0)
    return dot(spread.astype(BF16), arrived[...].astype(BF16))


def gather(values, asked_column, rows):
    for g in range(rows.pieces):
        at = rows.rows(g)
        pick = pick_columns(asked_column[at, :], 0, values.shape[0])
        rows.held[at, :] = dot(pick, values[...]).astype(BF16)
        rows.start(g)


def to_slots(slot_row, values, send):
    for g in range(send.pieces):
        pick = pick_rows(send.size, g * send.size, slot_row)
        send.held[send.rows(g), :] = dot(pick, values).astype(BF16)
        send.start(g)


def fetch_kernel(scalars, ins, outs):
    arrived, values = ins
    rows, asked_column = outs
    slots = rows.held.shape[0]
    every = slot_lines(arrived.all(), slots)
    lane = iota((slots, EDGE), 1) - iota((slots, EDGE), 0) % SLOTS
    asked = jnp.where(lane == 0, every * EDGE, jnp.where(lane == SLOTS, every, 0.0))
    asked = jnp.sum(asked, axis=1, keepdims=True) - 1.0
    asked_column.held[...] = jnp.broadcast_to(asked, (slots, EDGE)).astype(I32)
    asked_column.start()
    gather(values.all(), asked_column.held, rows)


def fetch(arrived, values, slots):
    return run(
        fetch_kernel,
        (),
        ((arrived, 1), (values, 1)),
        ((struct(slots, values.shape[1]), 2, 0), (struct(slots, EDGE, dtype=I32), 1, 0)),
        flops=2e9,
    )


def flat(tiles, rows, columns):
    lines = [jnp.concatenate([tiles[b, c] for c in columns], axis=1) for b in rows]
    return jnp.concatenate(lines, axis=0)


def densify(count, column, tiles, dense, g, first=0):
    members = range(g * GROUP, (g + 1) * GROUP)
    last = dense.shape[1] - 1
    longest = count[g * GROUP]
    for b in members:
        longest = jnp.maximum(longest, count[b])

    def body(t, carry):
        for b in members:
            c = jnp.where(t < count[b], column[t, b], last)
            dense[b - first, c] = dense[b - first, c] + tiles[b, t]
        return carry

    lax.fori_loop(0, longest, body, 0)


def near_kernel(scalars, ins, outs, dense, far_sems):
    count, column = scalars
    tiles, values = ins
    partial, degree, far = outs
    row_blocks = tiles.held.shape[0]
    last = dense.shape[1] - 1
    cut = last - far.shape[1]

    def far_copy(g):
        at = pl.ds(g * GROUP, GROUP)
        return pltpu.make_async_copy(dense.at[at, pl.ds(cut, last - cut)], far.at[at], far_sems.at[g])

    begin((tiles,), tiles.pieces)
    for b in range(row_blocks):
        dense[b] = jnp.zeros(dense.shape[1:], BF16)
    values = values.all()
    for g in range(tiles.pieces):
        take((tiles,), tiles.pieces, g)
        densify(count, column, tiles.held, dense, g)
        far_copy(g).start()
        for b in range(g * GROUP, (g + 1) * GROUP):
            at = slice(b * EDGE, (b + 1) * EDGE)
            partial.held[at, :] = dot(flat(dense, (b,), range(cut)), values[...])
            if g < degree.pieces:
                weights = dense[b, 0].astype(F32)
                for c in range(1, last):
                    weights += dense[b, c].astype(F32)
                total = jnp.sum(weights, axis=1, keepdims=True)
                degree.held[at, :] = jnp.broadcast_to(total, (EDGE, EDGE))
        partial.start(g)
        if g < degree.pieces:
            degree.start(g)
    for g in range(tiles.pieces):
        far_copy(g).wait()


def near(tile_count, tile_column, tiles, values):
    rows, width = values.shape
    row_blocks = tiles.shape[0]
    masters = rows // EDGE
    return run(
        near_kernel,
        (tile_count, tile_column),
        ((tiles, groups(tiles)), (values, 1)),
        (
            (struct(row_blocks * EDGE, width, dtype=F32), groups(tiles), 0),
            (struct(rows, EDGE, dtype=F32), masters // GROUP, 0),
            (struct(row_blocks, row_blocks - masters, EDGE, EDGE), 0, 0),
        ),
        (
            pltpu.VMEM((row_blocks, row_blocks + 1, EDGE, EDGE), BF16),
            pltpu.SemaphoreType.DMA((groups(tiles),)),
        ),
        flops=5e9,
    )


def mirror_out_kernel(scalars, ins, outs):
    arrived, slot_column, partial, tiles, slot_row = ins
    send, slab = outs
    last = tiles.pieces - 1
    tiles.start(last)
    partial.start(last)
    pick = pick_columns(slot_column.all()[...], 0, arrived.held.shape[0])
    slab.held[...] = dot(pick, arrived.all()[...]).astype(BF16)
    slab.start()
    tiles.wait(last)
    blocks = range(tiles.held.shape[1])
    left = flat(tiles.held, [last * GROUP + b for b in blocks], blocks)
    more = dot(left, slab.held[...])
    partial.wait(last)
    total = (partial.held[partial.rows(last), :] + more).astype(BF16)
    to_slots(slot_row.all()[...], total, send)


def mirror_out(arrived, slot_column, slot_row, partial, tiles):
    slots, width = arrived.shape
    mirrors = slot_row.shape[1]
    return run(
        mirror_out_kernel,
        (),
        (
            (inner(arrived), 1),
            (slot_column, 1),
            (partial, groups(tiles)),
            (tiles, groups(tiles)),
            (slot_row, 1),
        ),
        ((struct(slots, width), 2, 0), (struct(mirrors, width), 1, 0)),
        flops=2e9,
    )


def far_kernel(scalars, ins, outs):
    slab, arrived, asked_column, tiles, partial, own, degree = ins
    base, scale, asked_row = outs
    sources = (tiles, partial, own, degree)
    begin(sources, own.pieces)
    slots = asked_column.held.shape[0]
    asked = jnp.transpose(asked_column.all()[...].astype(F32))[0:8].astype(I32)
    asked_row.held[...] = asked
    asked_row.start()
    lane = iota((slots, EDGE), 1) - iota((slots, EDGE), 0) % SLOTS
    mine = (lane == 2 * SLOTS) | (lane == 3 * SLOTS) | (lane == 4 * SLOTS)
    sums = jnp.sum(jnp.where(mine, slot_lines(arrived.all(), slots), 0.0), axis=1, keepdims=True)
    degrees = jnp.transpose(jnp.broadcast_to(sums, (slots, EDGE)))[0:1]
    slab = slab.all()
    rows = own.size
    for g in range(own.pieces):
        take(sources, own.pieces, g)
        at = own.rows(g)
        left = flat(tiles.held, range(g * GROUP, (g + 1) * GROUP), range(tiles.held.shape[1]))
        total = partial.held[at, :] + dot(left, slab[...])
        hit = iota((rows, slots), 0) + g * rows == asked[0:1]
        more = jnp.sum(jnp.where(hit, degrees, 0.0), axis=1, keepdims=True)
        factor = 1.0 / (1.0 + (degree.held[at, :] + more))
        scale.held[at, :] = factor
        base.held[at, :] = own.held[at, :] + total * jnp.concatenate([factor, factor], axis=1)
        base.start(g)
    scale.start()


def far(tiles, slab, partial, degree, own, arrived, asked_column):
    masters, width = own.shape
    n = masters // EDGE // GROUP
    return run(
        far_kernel,
        (),
        (
            (slab, 1),
            (arrived, 1),
            (asked_column, 1),
            (tiles, groups(tiles)),
            (partial, groups(tiles)),
            (own, n),
            (degree, n),
        ),
        (
            (struct(masters, width, dtype=F32), n, 0),
            (struct(masters, EDGE, dtype=F32), 1, 0),
            (struct(8, asked_column.shape[0], dtype=I32), 1, 0),
        ),
        flops=5e9,
    )


def turn_kernel(scalars, ins, outs):
    asked_row, back, base, scale, cotangent, asked_column = ins
    mixed, low, spread, send = outs
    for source in (base, scale, cotangent):
        source.start(0)
    asked, back = asked_row.all()[0:1], back.all()
    step = 512
    for g in range(base.held.shape[0] // step):
        if g * step % base.size == 0:
            p = g * step // base.size
            for source in (base, scale, cotangent):
                source.wait(p)
            for source in (base, scale, cotangent, asked_column):
                if p + 1 < source.pieces:
                    source.start(p + 1)
        at = slice(g * step, (g + 1) * step)
        both = jnp.concatenate([scale.held[at, :], scale.held[at, :]], axis=1)
        added = dot(pick_rows(step, g * step, asked), back[...])
        u = base.held[at, :] + added * both
        square = u * u
        bend = jnp.tanh(u * (ROOT + (ROOT * CUBIC) * square))
        half = 0.5 + 0.5 * bend
        mixed.held[at, :] = (u * half).astype(BF16)
        slope = half * (1.0 + u * (1.0 - bend) * (ROOT + (3.0 * ROOT * CUBIC) * square))
        d_pre = cotangent.held[at, :].astype(F32) * slope
        low.held[at, :] = d_pre.astype(BF16)
        spread.held[at, :] = (d_pre * both).astype(BF16)
    asked_column.start(0)
    for out in (spread, low, mixed):
        out.start()
    gather(spread.held, asked_column.all(), send)


def turn(base, scale, cotangent, back, asked_row, asked_column):
    masters, width = base.shape
    return run(
        turn_kernel,
        (),
        (
            (asked_row, 1),
            (inner(back), 1),
            (base, 2),
            (scale, 2),
            (cotangent, 2),
            (asked_column, 2),
        ),
        ((struct(masters, width), 1, 0),) * 3 + ((struct(*back.shape), 2, 0),),
        flops=3e9,
    )


def put_blocks(total, first, value):
    for k in range(value.shape[1] // EDGE):
        total[first + k] = value[:, k * EDGE : (k + 1) * EDGE]


def back_near_kernel(scalars, ins, outs, dense):
    count, column = scalars
    tiles, values = ins
    (total,) = outs
    rows = dense.shape[0]
    begin((tiles,), rows // GROUP)
    for b in range(rows):
        dense[b] = jnp.zeros(dense.shape[1:], BF16)
    turned = jnp.transpose(values.all()[...].astype(F32)).astype(BF16)
    for g in range(rows // GROUP):
        take((tiles,), rows // GROUP, g)
        densify(count, column, tiles.held, dense, g)
    for g in range(total.pieces):
        right = flat(dense, range(rows), range(g * GROUP, (g + 1) * GROUP))
        put_blocks(total.held, g * GROUP, dot(turned, right))
        total.start(g)


def back_near(tile_count, tile_column, tiles, values):
    row_blocks, width = tiles.shape[0], values.shape[1]
    n = groups(tiles)
    (total,) = run(
        back_near_kernel,
        (tile_count, tile_column),
        ((tiles, n), (values, 1)),
        ((struct(row_blocks, width, EDGE, dtype=F32), n, 0),),
        (pltpu.VMEM((values.shape[0] // EDGE, row_blocks + 1, EDGE, EDGE), BF16),),
        flops=5e9,
    )
    return total


def mirror_back_kernel(scalars, ins, outs):
    arrived, slot_column, tiles, partial, slot_row = ins
    send, turned = outs
    last = tiles.pieces - 1
    tiles.start(last)
    partial.start(last)
    pick = pick_columns(slot_column.all()[...], 0, arrived.held.shape[0])
    turned.held[...] = jnp.transpose(dot(pick, arrived.all()[...])).astype(BF16)
    turned.start()
    tiles.wait(last)
    blocks = range(tiles.held.shape[1])
    right = flat(tiles.held, [last * GROUP + b for b in blocks], blocks)
    more = dot(turned.held[...], right)
    partial.wait(last)
    own = jnp.concatenate([partial.held[last * GROUP + c] for c in blocks], axis=1)
    rows = jnp.transpose(own + more).astype(BF16)
    to_slots(slot_row.all()[...], rows, send)


def mirror_back(arrived, slot_column, slot_row, partial, tiles):
    slots, width = arrived.shape
    mirrors = slot_row.shape[1]
    return run(
        mirror_back_kernel,
        (),
        (
            (inner(arrived), 1),
            (slot_column, 1),
            (tiles, groups(tiles)),
            (partial, groups(tiles)),
            (slot_row, 1),
        ),
        ((struct(slots, width), 2, 0), (struct(width, mirrors), 1, 0)),
        flops=2e9,
    )


def back_far_kernel(scalars, ins, outs, dense):
    count, column = scalars
    tiles, turned, partial = ins
    (total,) = outs
    last = tiles.pieces - 1
    tiles.start(last)
    for g in range(total.pieces):
        partial.start(g)
    dense[...] = jnp.zeros(dense.shape, BF16)
    turned = turned.all()
    tiles.wait(last)
    densify(count, column, tiles.held, dense, last, last * GROUP)
    for g in range(total.pieces):
        columns = range(g * GROUP, (g + 1) * GROUP)
        right = flat(dense, range(GROUP), columns)
        partial.wait(g)
        own = jnp.concatenate([partial.held[c] for c in columns], axis=1)
        put_blocks(total.held, g * GROUP, own + dot(turned[...], right))
        total.start(g)


def back_far(tile_count, tile_column, tiles, turned, partial):
    width, mirrors = turned.shape
    row_blocks = tiles.shape[0]
    masters = row_blocks - mirrors // EDGE
    (total,) = run(
        back_far_kernel,
        (tile_count, tile_column),
        ((tiles, groups(tiles)), (turned, 1), (partial, groups(partial))),
        ((inner(struct(masters, width, EDGE, dtype=F32)), masters // GROUP, 0),),
        (pltpu.VMEM((mirrors // EDGE, row_blocks + 1, EDGE, EDGE), BF16),),
        flops=3e9,
    )
    return total


def finish_kernel(scalars, ins, outs):
    (core,) = scalars
    back, asked_column, partial, features, grad_self = ins
    turned, keep, give = outs
    width, masters = turned.held.shape
    inputs = features.held.shape[1]
    step = 512
    flipped = jnp.transpose(back.all()[...].astype(F32)).astype(BF16)
    asked, partial = asked_column.all(), partial.all()
    for g in range(masters // step):
        own = []
        for b in range(g * step // EDGE, (g + 1) * step // EDGE):
            own.append(partial[b])
        added = dot(flipped, pick_columns(asked[...], g * step, step))
        turned.held[:, g * step : (g + 1) * step] = (
            jnp.concatenate(own, axis=1) + added
        ).astype(BF16)
    turned.start()
    total = dot(turned.held[...], features.all()[...])
    grad_self = grad_self.all()
    for h in range(width // EDGE):
        lines = pl.ds(h * inputs, inputs)
        first = grad_self[:, h * EDGE : (h + 1) * EDGE].astype(F32)
        second = jnp.transpose(total[h * EDGE : (h + 1) * EDGE, :])
        keep.held[lines, :] = jnp.where(core[0] == 0, first, second)
        give.held[lines, :] = jnp.where(core[0] == 0, second, first).astype(BF16)


def finish(core, partial, back, asked_column, features, grad_self):
    width = back.shape[1]
    masters, inputs = features.shape
    lines = inputs * width // EDGE
    return run(
        finish_kernel,
        (core,),
        (
            (back, 1),
            (asked_column, 1),
            (inner(partial), 1),
            (features, 1),
            (grad_self, 1),
        ),
        (
            (struct(width, masters), 1, 0),
            (struct(lines, EDGE, dtype=F32), 1, 0),
            (struct(lines, EDGE), 1, 0),
        ),
        flops=3e9,
    )


def input_grads_kernel(scalars, ins, outs):
    low, turned, w_self, w_neigh = ins
    (out,) = outs
    step = out.size
    own, other, low, turned = w_self.all(), w_neigh.all(), low.all(), turned.all()
    for g in range(out.pieces):
        at = slice(g * step, (g + 1) * step)
        d_projected = jnp.transpose(turned[:, at].astype(F32)).astype(BF16)
        value = dot(low[at, :], own[...], 1, 1) + dot(d_projected, other[...], 1, 1)
        out.held[at, :] = value.astype(BF16)
        out.start(g)


def input_grads(low, turned, w_self, w_neigh):
    masters, inputs = low.shape[0], w_self.shape[0]
    (out,) = run(
        input_grads_kernel,
        (),
        ((low, 1), (turned, 1), (w_self, 1), (w_neigh, 1)),
        ((struct(masters, inputs), 2, 0),),
        flops=3e9,
    )
    return out


def share_kernel(parts, out):
    share = jnp.sum(parts[...].astype(F32), axis=0, keepdims=True).astype(BF16)
    out[...] = jnp.broadcast_to(share, out.shape)


def share_out(parts):
    return pl.pallas_call(
        share_kernel,
        out_shape=struct(*parts.shape),
        compiler_params=params(8 * MIB),
        cost_estimate=cost(1e8),
    )(parts)


def unpack_kernel(core, mine, other, first, second):
    inputs = first.shape[0]
    for h in range(2):
        lines, lanes = pl.ds(h * inputs, inputs), pl.ds(h * EDGE, EDGE)
        a, b = mine[lines, :].astype(F32), other[lines, :].astype(F32)
        first[:, lanes] = jnp.where(core[0] == 0, a, b)
        second[:, lanes] = jnp.where(core[0] == 0, b, a)


def unpack(core, mine, other, inputs, width):
    smem, vmem = pl.BlockSpec(memory_space=pltpu.SMEM), pl.BlockSpec(memory_space=pltpu.VMEM)
    return pl.pallas_call(
        unpack_kernel,
        in_specs=[smem, vmem, vmem],
        out_specs=[vmem, vmem],
        out_shape=[struct(inputs, width, dtype=F32)] * 2,
        compiler_params=params(8 * MIB),
        cost_estimate=cost(1e8),
    )(core, mine, other)


def exchange(buffer, axes=EVERY):
    parts = lax.axis_size(axes)
    moved = lax.all_to_all(
        buffer.reshape(parts, buffer.shape[0] // parts, buffer.shape[1]),
        axes,
        split_axis=0,
        concat_axis=0,
        tiled=True,
    )
    return moved.reshape(buffer.shape)


def to_other_core(value):
    return lax.ppermute(value, "core", [(0, 1), (1, 0)])


def on_device(
    features,
    w_self,
    w_neigh,
    mirror_master_part,
    mirror_row,
    tile_count,
    tile_column,
    tile_weight,
    cotangent,
):
    inputs, width = w_neigh.shape
    parts = lax.axis_size(EVERY)
    core = lax.axis_index("core").astype(I32).reshape(1)
    slots = SLOTS * parts
    peer = mirror_master_part[:, 0]
    tile_column = tile_column.T
    ask, slot_row, slot_column = place(tile_count, peer, mirror_row, tile_weight, parts)
    asked = exchange(ask)
    projected = jnp.dot(features, w_neigh, preferred_element_type=F32).astype(BF16)
    own = jnp.dot(features, w_self, preferred_element_type=F32)
    asked, own = lax.optimization_barrier((asked, own))
    asked = pltpu.with_memory_space_constraint(asked, pltpu.HBM)
    rows, asked_column = fetch(asked, projected, slots)
    rows, projected = lax.optimization_barrier((rows, projected))
    arrived = exchange(rows)
    partial, degree, far_tiles = near(tile_count, tile_column, tile_weight, projected)
    send, slab = mirror_out(arrived, slot_column, slot_row, partial, far_tiles)
    back = exchange(send)
    base, scale, asked_row = far(far_tiles, slab, partial, degree, own, asked, asked_column)
    mixed, low, spread, send = turn(base, scale, cotangent, back, asked_row, asked_column)
    arrived = exchange(send)
    partial = back_near(tile_count, tile_column, tile_weight, spread)
    grad_self = lax.dot_general(
        features, low, (((0,), (0,)), ((), ())), preferred_element_type=F32
    ).astype(BF16)
    send, turned = mirror_back(arrived, slot_column, slot_row, partial, far_tiles)
    back = pltpu.with_memory_space_constraint(exchange(send), pltpu.HBM)
    partial = back_far(tile_count, tile_column, tile_weight, turned, partial)
    d_projected, keep, give = finish(core, partial, back, asked_column, features, grad_self)
    pair = (keep + to_other_core(give).astype(F32)).astype(BF16)
    same = ("chip", "local")
    shares = exchange(pair, same).reshape(lax.axis_size(same), -1, EDGE)
    grad_features = input_grads(low, d_projected, w_self, w_neigh)
    shares, grad_features = lax.optimization_barrier((shares, grad_features))
    mine = exchange(share_out(shares).reshape(pair.shape), same)
    grad_self, grad_neigh = unpack(core, mine, to_other_core(mine), inputs, width)
    return (mixed, grad_features, grad_self, grad_neigh)


def solution(mesh):
    machine, local = mesh.devices.shape
    devices = mesh.devices.reshape(machine // 2, 2, local)
    split, rows = P(EVERY), P(EVERY, None)
    return jax.shard_map(
        on_device,
        mesh=jax.sharding.Mesh(devices, EVERY),
        in_specs=(rows, P(), P(), rows, split, split, rows, P(EVERY, None, None, None), rows),
        out_specs=(rows, rows, P(), P()),
        check_vma=False,
    )
```
